32 devices in a mesh: dp: 16 (over z, y, x), mp: 2 (over core).
Axes of the slice: x: 2, y: 2, z: 4, core: 2. Of those that a mesh axis runs over, the one named last changes fastest.
Arguments:
- inputs: bfloat16 [16, 2048, 512], P('dp', 'mp'), may hold values from -6 to 6
- cotangent: bfloat16 [16, 2048, 512], P('dp', 'mp'), may hold values from -6 to 6
- lengths: int32 [16], P('dp'), may hold values from 1024 to 2048, as said below
- hidden_weights: float32 [2, 4, 512, 1024], P(None, None, None, 'mp'), may hold values from -0.25 to 0.25
- mlp_weights: float32 [2, 2, 512, 2048], P(None, None, None, 'mp'), may hold values from -0.25 to 0.25
- norm_gains: float32 [2, 2, 512], replicated, may hold values from 0.5 to 1.5
- gate_bias: float32 [2, 2, 1024], P(None, None, 'mp'), may hold values from -8.5 to 4
- left_bases: float32 [2, 6, 512, 512], replicated, may hold values from -1 to 1, as said below
- hidden_blocks: float32 [2, 4, 8, 128, 128], P(None, None, 'mp'), may hold values from -1 to 1, as said below
- mlp_blocks: float32 [2, 2, 16, 128, 128], P(None, None, 'mp'), may hold values from -1 to 1, as said below
- hidden_first: float32 [512, 2, 4, 1024], P('dp', None, None, 'mp'), as said below
- hidden_second: float32 [512, 2, 4, 1024], P('dp', None, None, 'mp'), as said below
- mlp_first: float32 [512, 2, 2, 2048], P('dp', None, None, 'mp'), as said below
- mlp_second: float32 [512, 2, 2, 2048], P('dp', None, None, 'mp'), as said below
- gain_first: float32 [2, 2, 512], replicated, as said below
- gain_second: float32 [2, 2, 512], replicated, as said below
- bias_first: float32 [2, 2, 1024], P(None, None, 'mp'), as said below
- bias_second: float32 [2, 2, 1024], P(None, None, 'mp'), as said below
- step_count: int32 [1], replicated, may hold values from 2 to 20
- row_owner: int32 [16], replicated, may hold values from 0 to 15, each once
Outputs:
- output: float32 [16, 2048, 512], P('dp', 'mp')
- input_grad: float32 [16, 2048, 512], P('dp', 'mp')
- hidden_grad: float32 [512, 2, 4, 1024], P('dp', None, None, 'mp')
- hidden_first_new: float32 [512, 2, 4, 1024], P('dp', None, None, 'mp')
- hidden_second_new: float32 [512, 2, 2, 1024], P('dp', None, None, 'mp')
- gate_second_new: float32 [512, 2, 2, 1024], P('dp', None, None, 'mp')
- hidden_new: float32 [2, 4, 512, 1024], P(None, None, None, 'mp')
- mlp_grad: float32 [512, 2, 2, 2048], P('dp', None, None, 'mp')
- mlp_first_new: float32 [512, 2, 2, 2048], P('dp', None, None, 'mp')
- mlp_second_new: float32 [512, 2, 2, 2048], P('dp', None, None, 'mp')
- mlp_new: float32 [2, 2, 512, 2048], P(None, None, None, 'mp')
- gain_grad: float32 [2, 2, 512], replicated
- gain_first_new: float32 [2, 2, 512], replicated
- gain_second_new: float32 [2, 2, 512], replicated
- gain_new: float32 [2, 2, 512], replicated
- bias_grad: float32 [2, 2, 1024], P(None, None, 'mp')
- bias_first_new: float32 [2, 2, 1024], P(None, None, 'mp')
- bias_second_new: float32 [2, 2, 1024], P(None, None, 'mp')
- bias_new: float32 [2, 2, 1024], P(None, None, 'mp')
The draws below stay inside these ranges and needn't reach their ends.
Inputs may be any that keep to these rules, and one draw needn't show every extreme that they name: `lengths`: positions at or past a sequence's length are padding; at least one sequence has length 2048. `left_bases`: each [512, 512] matrix is orthogonal. `hidden_blocks`: each [128, 128] block is orthogonal. `mlp_blocks`: each [128, 128] block is orthogonal. `hidden_first`: real values of either sign. `hidden_second`: Positive. `mlp_first`: real values of either sign. `mlp_second`: Positive. `gain_first`: real values of either sign. `gain_second`: Positive. `bias_first`: real values of either sign. `bias_second`: Positive. `row_owner`: each dp index appears once.
All inputs are finite; a program needn't handle non-finite values.
Results may differ from the reference program's by a relative error of at most 0.025.
The reference program's roundings to bfloat16 on the way count: a program that leaves them out, or rounds other values in their place, can miss the bound.
Values may be sent and summed in bfloat16 or wider, within the bound.
No kernel may reach another device: no remote copies, remote signals or barrier semaphores. Data moves between devices by JAX's collectives and lax.ppermute only.
A program may use at most 384 MiB of HBM per device.

```python
import math
import jax
import jax.numpy as jnp
from jax import lax

D = 512
H = 1024
FF = 2048
RB = 128
LAYERS = 2
LEN = 2048
SEQS = 16
TOKENS = 32768
N_DP = 16


def orthogonal_set(key, count, order):
    key_rows, key_cols, key_perm = jax.random.split(key, 3)
    index = jnp.arange(order, dtype=jnp.int32)
    picks = jax.vmap(lambda one_key: jax.random.permutation(one_key, order))(jax.random.split(key_perm, count)).astype(jnp.int32)
    phase = (2 * index[None, :, None] + 1) * picks[:, None, :] % (4 * order)
    table = jnp.cos(jnp.pi * phase.astype(jnp.float32) / (2.0 * order))
    scaled = jnp.where(picks == 0, jnp.sqrt(jnp.float32(1.0 / order)), jnp.sqrt(jnp.float32(2.0 / order)))[:, None, :]
    signs_rows = (2 * jax.random.randint(key_rows, (count, order, 1), 0, 2) - 1).astype(jnp.float32)
    signs_cols = (2 * jax.random.randint(key_cols, (count, 1, order), 0, 2) - 1).astype(jnp.float32)
    return signs_rows * table * scaled * signs_cols


def grad_size(factors):
    return jnp.array(factors, jnp.float32) * jnp.sqrt(jnp.float32(0.75 * TOKENS))


def first_moment(key, shape, size):
    return jax.random.normal(key, shape, jnp.float32) * size * (0.1 / 0.9)


def second_moment(key, shape, size):
    spread = jnp.exp(jax.random.uniform(key, shape, jnp.float32, 0.0, jnp.log(4.0)))
    return spread * size * size * (0.05 / 0.95)


def draw_lengths(key, part):
    key_len, key_where = jax.random.split(key)
    drawn = jax.random.randint(key_len, (SEQS,), LEN // 2, LEN + 1)
    longest = jax.random.randint(key_where, (), 0, SEQS)
    return jnp.where(jnp.arange(SEQS, dtype=jnp.int32) == longest, LEN, drawn).astype(jnp.int32)


def draw_gate_bias(key, part):
    key = jax.random.fold_in(key, 11)
    key_pick, key_fast, key_keep, key_take = jax.random.split(key, 4)
    chosen = jax.random.randint(key_pick, (LAYERS, 1, H), 0, 2) == 1
    fast = jax.random.uniform(key_fast, (LAYERS, 2, H), jnp.float32, -4.0, 4.0)
    keep = jax.random.uniform(key_keep, (LAYERS, 1, H), jnp.float32, 2.0, 4.0)
    take = jax.random.uniform(key_take, (LAYERS, 1, H), jnp.float32, -8.5, -6.5)
    other = jnp.concatenate([keep, take], axis=1)
    return jnp.where(chosen, other, fast)


def draw_left_bases(key, part):
    return orthogonal_set(key, LAYERS * 6, D).reshape(LAYERS, 6, D, D)


def draw_hidden_blocks(key, part):
    return orthogonal_set(key, LAYERS * 4 * (H // RB), RB).reshape(LAYERS, 4, H // RB, RB, RB)


def draw_mlp_blocks(key, part):
    return orthogonal_set(key, LAYERS * 2 * (FF // RB), RB).reshape(LAYERS, 2, FF // RB, RB, RB)


def draw_hidden_first(key, part):
    size = grad_size([0.08, 0.08, 0.5, 1.0])[None, None, :, None]
    return first_moment(key, (D, LAYERS, 4, H), size)


def draw_hidden_second(key, part):
    size = grad_size([0.08, 0.08, 0.5, 1.0])[None, None, :, None]
    return second_moment(key, (D, LAYERS, 4, H), size)


def draw_mlp_first(key, part):
    size = grad_size([0.3, 0.6])[None, None, :, None]
    return first_moment(key, (D, LAYERS, 2, FF), size)


def draw_mlp_second(key, part):
    size = grad_size([0.3, 0.6])[None, None, :, None]
    return second_moment(key, (D, LAYERS, 2, FF), size)


def draw_gain_first(key, part):
    return first_moment(key, (LAYERS, 2, D), grad_size([0.4])[0])


def draw_gain_second(key, part):
    return second_moment(key, (LAYERS, 2, D), grad_size([0.4])[0])


def draw_bias_first(key, part):
    return first_moment(key, (LAYERS, 2, H), grad_size([0.08])[0])


def draw_bias_second(key, part):
    return second_moment(key, (LAYERS, 2, H), grad_size([0.08])[0])


def shard_levels(key, shape, shards, smallest, top_value):
    factor_of, own = 1.0, jax.random.fold_in(key, 6)
    for axis_at, shards_of in shards:
        heights = jnp.exp(jax.random.uniform(jax.random.fold_in(own, axis_at), (shards_of,), jnp.float32, smallest / len(shards), top_value / len(shards)))
        factor_of = factor_of * jnp.repeat(heights, shape[axis_at] // shards_of).reshape([-1 if axis == axis_at else 1 for axis in range(len(shape))])
    return factor_of


def centred(rng, extent, deviation, bound, cuts=(), kind=jnp.bfloat16):
    factor_of = shard_levels(rng, extent, cuts, -0.22, 0.18) if cuts else 1.0
    values = jax.random.normal(rng, extent, jnp.float32) * deviation * factor_of
    return jnp.minimum(jnp.maximum(values, -bound), bound).astype(kind)


def setup_inputs(seed: int = 0) -> dict:
    key_list = jax.random.split(jax.random.key(seed), 21)
    inputs = centred(key_list[0], (SEQS, LEN, D), 1.0, 6.0, ((0, 16), (1, 2)))
    cotangent = centred(key_list[1], (SEQS, LEN, D), 1.0, 6.0, ((0, 16), (1, 2)))
    lengths = draw_lengths(jax.random.fold_in(key_list[20], 71), 0)
    hidden_weights = centred(key_list[3], (LAYERS, 4, D, H), D ** -0.5, 0.25, ((3, 2),), jnp.float32)
    mlp_weights = centred(key_list[4], (LAYERS, 2, D, FF), D ** -0.5, 0.25, ((3, 2),), jnp.float32)
    norm_gains = jnp.clip(1.0 + 0.1 * jax.random.normal(key_list[5], (LAYERS, 2, D), jnp.float32), 0.5, 1.5)
    gate_bias = draw_gate_bias(jax.random.fold_in(key_list[20], 71), 0)
    left_bases = draw_left_bases(jax.random.fold_in(key_list[20], 71), 0)
    hidden_blocks = draw_hidden_blocks(jax.random.fold_in(key_list[20], 71), 0)
    mlp_blocks = draw_mlp_blocks(jax.random.fold_in(key_list[20], 71), 0)
    hidden_first = draw_hidden_first(jax.random.fold_in(key_list[20], 71), 0)
    hidden_second = draw_hidden_second(jax.random.fold_in(key_list[20], 71), 0)
    mlp_first = draw_mlp_first(jax.random.fold_in(key_list[20], 71), 0)
    mlp_second = draw_mlp_second(jax.random.fold_in(key_list[20], 71), 0)
    gain_first = draw_gain_first(jax.random.fold_in(key_list[20], 71), 0)
    gain_second = draw_gain_second(jax.random.fold_in(key_list[20], 71), 0)
    bias_first = draw_bias_first(jax.random.fold_in(key_list[20], 71), 0)
    bias_second = draw_bias_second(jax.random.fold_in(key_list[20], 71), 0)
    step_count = jax.random.randint(key_list[18], (1,), 2, 21).astype(jnp.int32)
    row_owner = jax.random.permutation(key_list[19], N_DP).astype(jnp.int32)
    return {"inputs": inputs, "cotangent": cotangent, "lengths": lengths, "hidden_weights": hidden_weights, "mlp_weights": mlp_weights, "norm_gains": norm_gains, "gate_bias": gate_bias, "left_bases": left_bases, "hidden_blocks": hidden_blocks, "mlp_blocks": mlp_blocks, "hidden_first": hidden_first, "hidden_second": hidden_second, "mlp_first": mlp_first, "mlp_second": mlp_second, "gain_first": gain_first, "gain_second": gain_second, "bias_first": bias_first, "bias_second": bias_second, "step_count": step_count, "row_owner": row_owner}


@jax.custom_vjp
def low(v):
    return lax.optimization_barrier(v.astype(jnp.bfloat16)).astype(jnp.float32)

@jax.custom_vjp
def low_back(v):
    return v

def low_keep(v):
    return (low(v), None)

def low_pass(kept, grad):
    return (grad,)

def back_keep(v):
    return (v, None)

def back_low(kept, grad):
    return (low(grad),)
low.defvjp(low_keep, low_pass)
low_back.defvjp(back_keep, back_low)
NORM_EPS = 1e-05
BETA_ONE = 0.9
BETA_TWO = 0.95
ADAM_EPS = 1e-08
MATRIX_RATE = 0.08
GAIN_RATE = 0.5
BIAS_RATE = 4.0
DECAY_RATE = 0.01
HIGHEST = lax.Precision.HIGHEST

def candidate(values):
    return jnp.where(values >= 0, values + 0.5, jax.nn.sigmoid(values))

def norm_rows(values, gain):
    return values * lax.rsqrt(lax.optimization_barrier(jnp.mean(values * values, axis=-1, keepdims=True)) + NORM_EPS) * gain

def project(acts, weight):
    return jnp.einsum('std,dx->stx', acts, weight, precision=HIGHEST)

def project_back(acts, weight):
    return jnp.einsum('stx,dx->std', acts, weight, precision=HIGHEST)

def recur(carry_state, inputs_now):
    keep_now, take_now, cand_now = inputs_now
    carry_state = keep_now * carry_state + take_now * cand_now
    return (carry_state, carry_state)

def layer_block(values, hidden_w, mlp_w, gains, biases):
    w_forget = low(hidden_w[0])
    w_input = low(hidden_w[1])
    w_cand = low(hidden_w[2])
    w_output = low(hidden_w[3])
    w_up = low(mlp_w[0])
    w_down = low(mlp_w[1])
    normed_in = low(norm_rows(values, gains[0]))
    key_forget = low_back(project(normed_in, w_forget) + biases[0])
    key_input = low_back(project(normed_in, w_input) + biases[1])
    key_cand = low_back(project(normed_in, w_cand))
    gate_gap = jax.nn.softplus(-key_forget) - jax.nn.softplus(-key_input)
    keep_rate = jax.nn.sigmoid(-gate_gap)
    take_rate = jax.nn.sigmoid(gate_gap)
    cand_value = candidate(key_cand)
    moved = (jnp.moveaxis(keep_rate, 1, 0), jnp.moveaxis(take_rate, 1, 0), jnp.moveaxis(cand_value, 1, 0))
    start_state = jnp.zeros((values.shape[0], hidden_w.shape[2]), jnp.float32)
    final_state, states = lax.scan(recur, start_state, moved)
    states = low(jnp.moveaxis(states, 0, 1))
    middle = values + low_back(project_back(states, w_output))
    normed_mid = low(norm_rows(middle, gains[1]))
    pre_act = low_back(project(normed_mid, w_up))
    act_low = low(jax.nn.gelu(pre_act, approximate=False))
    return middle + low_back(project_back(act_low, w_down))

def network(values, weights, block_len):
    hidden_w, mlp_w, gains, biases = weights
    for layer_at in range(LAYERS):
        values = layer_block(values, hidden_w[layer_at], mlp_w[layer_at], gains[layer_at], biases[layer_at])
    places = jnp.arange(LEN, dtype=jnp.int32)
    pad_mask = (places[None, :] < block_len[:, None]).astype(jnp.float32)
    return values * pad_mask[:, :, None]

def rotate(grads, left, blocks):
    layer_n, kind_n, row_n, width = grads.shape
    size = blocks.shape[-1]
    tiles = grads.reshape(layer_n, kind_n, row_n, width // size, size)
    right = jnp.einsum('lkdbi,lkbij->lkdbj', tiles, blocks, precision=HIGHEST).reshape(grads.shape)
    return jnp.einsum('lkde,lkdx->elkx', left, right, precision=HIGHEST)

def rotate_back(moves, left, blocks):
    row_n, layer_n, kind_n, width = moves.shape
    size = blocks.shape[-1]
    tiles = moves.reshape(row_n, layer_n, kind_n, width // size, size)
    right = jnp.einsum('elkbj,lkbij->elkbi', tiles, blocks, precision=HIGHEST).reshape(moves.shape)
    return jnp.einsum('lkde,elkx->lkdx', left, right, precision=HIGHEST)

def to_owner(rotated, row_owner):
    blocks = rotated.reshape((N_DP, rotated.shape[0] // N_DP) + rotated.shape[1:])
    placed = jnp.zeros_like(blocks).at[row_owner.astype(jnp.int32)].set(blocks)
    return placed.reshape(rotated.shape)

def from_owner(stored, row_owner):
    blocks = stored.reshape((N_DP, stored.shape[0] // N_DP) + stored.shape[1:])
    return jnp.take(blocks, row_owner.astype(jnp.int32), axis=0).reshape(stored.shape)

def adam_moments(grads, first, second, fix_one, fix_two):
    first = BETA_ONE * first + (1.0 - BETA_ONE) * grads
    second = BETA_TWO * second + (1.0 - BETA_TWO) * grads * grads
    moves = first / fix_one / (jnp.sqrt(second / fix_two) + ADAM_EPS)
    return (first, second, moves)

def reference(inputs, cotangent, lengths, hidden_weights, mlp_weights, norm_gains, gate_bias, left_bases, hidden_blocks, mlp_blocks, hidden_first, hidden_second, mlp_first, mlp_second, gain_first, gain_second, bias_first, bias_second, step_count, row_owner):
    seq_total = inputs.shape[0]
    group_size = math.gcd(seq_total, max(1, 4096 // LEN))
    round_count = seq_total // group_size
    stacked_in = inputs.astype(jnp.float32).reshape(round_count, group_size, LEN, D)
    stacked_cot = cotangent.astype(jnp.float32).reshape(round_count, group_size, LEN, D)
    stacked_len = lengths.reshape(round_count, group_size)
    params = (hidden_weights, mlp_weights, norm_gains, gate_bias)

    def one_round(totals, batch):
        block_in, block_cot, block_len = batch

        def run(values, weights):
            return network(values, weights, block_len)
        result, pull = jax.vjp(run, block_in, params)
        grad_in, grad_params = pull(block_cot)
        return (jax.tree.map(lambda left_v, right_v: left_v + right_v, totals, grad_params), (result, grad_in))
    zero_grads = jax.tree.map(jnp.zeros_like, params)
    grads, (results, grad_inputs) = lax.scan(one_round, zero_grads, (stacked_in, stacked_cot, stacked_len))
    output = results.reshape(seq_total, LEN, D)
    input_grad = grad_inputs.reshape(seq_total, LEN, D)
    grad_hidden, grad_mlp, grad_gain, grad_bias = grads
    count_value = step_count[0].astype(jnp.float32)
    fix_one = 1.0 - jnp.power(jnp.float32(BETA_ONE), count_value)
    fix_two = 1.0 - jnp.power(jnp.float32(BETA_TWO), count_value)
    left_hidden = left_bases[:, :4]
    left_mlp = left_bases[:, 4:]
    hidden_grad = to_owner(rotate(grad_hidden, left_hidden, hidden_blocks), row_owner)
    mlp_grad = to_owner(rotate(grad_mlp, left_mlp, mlp_blocks), row_owner)
    hidden_first_new, hidden_second_new, hidden_moves = adam_moments(hidden_grad, hidden_first, hidden_second, fix_one, fix_two)
    mlp_first_new, mlp_second_new, mlp_moves = adam_moments(mlp_grad, mlp_first, mlp_second, fix_one, fix_two)
    hidden_new = hidden_weights - MATRIX_RATE * (rotate_back(from_owner(hidden_moves, row_owner), left_hidden, hidden_blocks) + DECAY_RATE * hidden_weights)
    mlp_new = mlp_weights - MATRIX_RATE * (rotate_back(from_owner(mlp_moves, row_owner), left_mlp, mlp_blocks) + DECAY_RATE * mlp_weights)
    gain_first_new, gain_second_new, gain_moves = adam_moments(grad_gain, gain_first, gain_second, fix_one, fix_two)
    bias_first_new, bias_second_new, bias_moves = adam_moments(grad_bias, bias_first, bias_second, fix_one, fix_two)
    gain_new = norm_gains - GAIN_RATE * gain_moves
    bias_new = gate_bias - BIAS_RATE * bias_moves
    return (output, input_grad, hidden_grad, hidden_first_new, hidden_second_new[:, :, 2:], hidden_second_new[:, :, :2], hidden_new, mlp_grad, mlp_first_new, mlp_second_new, mlp_new, grad_gain, gain_first_new, gain_second_new, gain_new, grad_bias, bias_first_new, bias_second_new, bias_new)
```

```python
import functools
import jax
import jax.numpy as jnp
from jax import lax
from jax.experimental import pallas as pl
from jax.experimental.pallas import tpu as pltpu
from jax.sharding import PartitionSpec as P

NORM_EPS = 1e-05
BETA_ONE = 0.9
BETA_TWO = 0.95
ADAM_EPS = 1e-08
MATRIX_RATE = 0.08
GAIN_RATE = 0.5
BIAS_RATE = 4.0
DECAY_RATE = 0.01
BF = jnp.bfloat16
F32 = jnp.float32
SEG = 8
TILE_STEPS = 32
HC = 512
VMEM_LIMIT = 58 * 1024 * 1024
LOG2E = 1.4426950408889634


def dot_nn(a, b):
    return lax.dot_general(a, b, (((1,), (0,)), ((), ())), preferred_element_type=F32)


def dot_nt(a, b):
    return lax.dot_general(a, b, (((1,), (1,)), ((), ())), preferred_element_type=F32)


def dot_tn(a, b):
    return lax.dot_general(a, b, (((0,), (0,)), ((), ())), preferred_element_type=F32)


def recip(x):
    r = pl.reciprocal(x, approx=True)
    return r * (2.0 - x * r)


def rows_loop(count, size, body, init=None, unroll=1):
    def step(i, carry):
        return body(pl.ds(pl.multiple_of(i * size, size), size), carry)

    return lax.fori_loop(0, count // size, step, init, unroll=unroll)


def row_scale(values):
    return lax.rsqrt(jnp.mean(values * values, axis=-1, keepdims=True) + NORM_EPS)


def norm_stage(x_ref, gain, out_ref):
    def body(r, c):
        x = x_ref[r, :]
        out_ref[r, :] = (x * row_scale(x) * gain).astype(BF)
        return c

    rows_loop(x_ref.shape[0], 32, body, 0)


def gate_stage(nin_ref, bias_ref, w_refs, kbuf, state, outs):
    a_ref, loc_ref, prod_ref, cand_ref, wf_ref, wi_ref, q_ref = outs
    rows = nin_ref.shape[0]
    part = w_refs[0].shape[2]
    hc = min(HC, part)
    for j, w in enumerate(w_refs):
        for c0 in range(0, part, hc):
            cols = slice(j * part + c0, j * part + c0 + hc)
            n = nin_ref[...]
            for k in range(3):
                kbuf[k, :, :hc] = dot_nn(n, w[k, :, c0 : c0 + hc])
            bias_f = bias_ref[0:1, cols]
            bias_i = bias_ref[1:2, cols]

            def body(r, carry):
                loc, prod = carry
                kf = kbuf[0, r, :hc] + bias_f
                ki = kbuf[1, r, :hc] + bias_i
                kc = kbuf[2, r, :hc]
                tf = jnp.exp(-jnp.abs(kf))
                ti = jnp.exp(-jnp.abs(ki))
                tc = jnp.exp(-jnp.abs(kc))
                of, oi = 1.0 + tf, 1.0 + ti
                gap = jnp.minimum(ki, 0.0) - jnp.minimum(kf, 0.0)
                e = jnp.exp(-jnp.abs(gap))
                nf = jnp.where(gap < 0, of * e, of)
                ni = jnp.where(gap > 0, oi * e, oi)
                inv = recip(nf + ni)
                keep = ni * inv
                take = nf * inv
                sf = jnp.where(kf >= 0, tf, 1.0) * recip(of)
                si = jnp.where(ki >= 0, ti, 1.0) * recip(oi)
                sc = tc * recip(1.0 + tc)
                up = kc >= 0
                cand = jnp.where(up, kc + 0.5, sc)
                slope = jnp.where(up, 1.0, sc * (1.0 - sc))
                both = keep * take
                a_ref[r, cols] = keep
                cand_ref[r, cols] = cand.astype(BF)
                wf_ref[r, cols] = (both * sf).astype(BF)
                wi_ref[r, cols] = (both * si).astype(BF)
                q_ref[r, cols] = (take * slope).astype(BF)
                drive = take * cand
                loc0 = keep[:8] * loc + drive[:8]
                prod0 = keep[:8] * prod
                loc1 = keep[8:] * loc0 + drive[8:]
                prod1 = keep[8:] * prod0
                loc_ref[r, cols] = jnp.concatenate([loc0, loc1])
                prod_ref[r, cols] = jnp.concatenate([prod0, prod1])
                return loc1, prod1

            loc, prod = rows_loop(rows, 16, body, (state[0, :, cols], state[1, :, cols]))
            state[0, :, cols] = loc
            state[1, :, cols] = prod


def fold_forward(state, ends_ref, fin_ref, part):
    hidden = state.shape[2]
    ends_ref[...] = state[...]
    loc = state[0, 0:1, :]
    prod = state[1, 0:1, :]
    for s in range(1, SEG):
        loc = state[0, s : s + 1, :] + state[1, s : s + 1, :] * loc
        prod = state[1, s : s + 1, :] * prod
    n = hidden // part
    for j in range(n):
        src = slice(((j + 1) % n) * part, ((j + 1) % n) * part + part)
        fin_ref[0:1, j * part : (j + 1) * part] = loc[:, src]
        fin_ref[1:2, j * part : (j + 1) * part] = prod[:, src]


def fold_backward(state, ends_ref, fin_ref, part):
    hidden = state.shape[2]
    ends_ref[...] = state[...]
    mu = state[0, SEG - 1 : SEG, :]
    prod = state[1, SEG - 1 : SEG, :]
    for s in reversed(range(SEG - 1)):
        mu = state[0, s : s + 1, :] + state[1, s : s + 1, :] * mu
        prod = state[1, s : s + 1, :] * prod
    n = hidden // part
    for j in range(n):
        src = slice(((j - 1) % n) * part, ((j - 1) % n) * part + part)
        fin_ref[0:1, j * part : (j + 1) * part] = mu[:, src]
        fin_ref[1:2, j * part : (j + 1) * part] = prod[:, src]


def carry_forward(inc_ref, ends_ref, start, live):
    start[0:1, :] = inc_ref[0:1, :] * live
    for s in range(SEG - 1):
        start[s + 1 : s + 2, :] = (
            ends_ref[0, s : s + 1, :] + ends_ref[1, s : s + 1, :] * start[s : s + 1, :]
        )


def carry_backward(inc_ref, ends_ref, start, live):
    start[SEG - 1 : SEG, :] = inc_ref[0:1, :] * live
    for s in reversed(range(1, SEG)):
        start[s - 1 : s, :] = (
            ends_ref[0, s : s + 1, :] + ends_ref[1, s : s + 1, :] * start[s : s + 1, :]
        )


def state_stage(first, start, ins, hlow_ref, cf_ref, ci_ref):
    loc_ref, prod_ref, loc_before, prod_before, cand_ref, wf_ref, wi_ref = ins
    rows, hidden = loc_ref.shape
    hc = min(HC, hidden)
    for c0 in range(0, hidden, hc):
        cols = slice(c0, c0 + hc)
        c = start[:, cols]
        before = jnp.where(first, c, loc_before[:, cols] + prod_before[:, cols] * c)

        def body(r, before):
            loc = loc_ref[r, cols]
            prod = prod_ref[r, cols]
            h0 = loc[:8] + prod[:8] * c
            h1 = loc[8:] + prod[8:] * c
            hlow_ref[r, cols] = jnp.concatenate([h0, h1]).astype(BF)
            diff = cand_ref[r, cols].astype(F32) - jnp.concatenate([before, h0])
            cf_ref[r, cols] = (-wf_ref[r, cols].astype(F32) * diff).astype(BF)
            ci_ref[r, cols] = (wi_ref[r, cols].astype(F32) * diff).astype(BF)
            return h1

        rows_loop(rows, 16, body, before)


def mlp_stage(x_ref, hlow_ref, w_refs, m_refs, gain, kbuf, mid_ref, nmid_ref, act_ref, slope_ref, xn_ref):
    rows = x_ref.shape[0]
    part = w_refs[0].shape[2]
    total = x_ref[...]
    for j, w in enumerate(w_refs):
        total = total + dot_nt(hlow_ref[:, j * part : (j + 1) * part], w[0])
    mid_ref[...] = total
    norm_stage(mid_ref, gain, nmid_ref)
    wide = m_refs[0].shape[2]
    fc = min(HC, wide)
    xn_ref[...] = mid_ref[...]
    for j, m in enumerate(m_refs):
        for c0 in range(0, wide, fc):
            cols = slice(j * wide + c0, j * wide + c0 + fc)
            kbuf[0, :, :fc] = dot_nn(nmid_ref[...], m[0, :, c0 : c0 + fc])

            def body(r, c):
                pre = kbuf[0, r, :fc]
                size = jnp.abs(pre)
                t = recip(1.0 + size * (0.3275911 * 0.7071067811865476))
                bell = jnp.exp(pre * pre * -0.5)
                poly = (
                    (((1.061405429 * t - 1.453152027) * t + 1.421413741) * t - 0.284496736) * t
                    + 0.254829592
                ) * t
                tail = (0.5 * poly) * bell
                cdf = jnp.where(pre >= 0, 1.0 - tail, tail)
                act_ref[r, cols] = (pre * cdf).astype(BF)
                slope_ref[r, cols] = (cdf + pre * (bell * 0.3989422804014327)).astype(BF)
                return c

            rows_loop(rows, 16, body, 0)
        xn_ref[...] = xn_ref[...] + dot_nt(act_ref[:, j * wide : (j + 1) * wide], m[1])


def norm_back_stage(src_ref, gain, dn_ref, dx_ref, sums_ref, low_ref):
    def body(r, total):
        x = src_ref[r, :]
        scale = row_scale(x)
        unit = x * scale
        d = dn_ref[r, :]
        e = d * gain
        dx = dx_ref[r, :] + scale * (e - unit * jnp.mean(e * unit, axis=-1, keepdims=True))
        dx_ref[r, :] = dx
        if low_ref is not None:
            low_ref[r, :] = dx.astype(BF)
        g = d * unit
        return total + g[:8] + g[8:16] + g[16:24] + g[24:]

    sums_ref[...] = rows_loop(src_ref.shape[0], 32, body, sums_ref[...])


def mlp_back_stage(dx_ref, slope_ref, mid_ref, m_refs, gain, kbuf, dn_ref, dz_ref, dpre_ref, dout_ref, sums_ref):
    rows = dx_ref.shape[0]
    dz_ref[...] = dx_ref[...].astype(BF)
    wide = m_refs[0].shape[2]
    fc = min(HC, wide)
    total = None
    for j, m in enumerate(m_refs):
        for c0 in range(0, wide, fc):
            cols = slice(j * wide + c0, j * wide + c0 + fc)
            kbuf[0, :, :fc] = dot_nn(dz_ref[...], m[1, :, c0 : c0 + fc])

            def body(r, c):
                dpre_ref[r, cols] = (kbuf[0, r, :fc] * slope_ref[r, cols].astype(F32)).astype(BF)
                return c

            rows_loop(rows, 32, body, 0)
        term = dot_nt(dpre_ref[:, j * wide : (j + 1) * wide], m[0])
        if j == 0:
            dn_ref[...] = term
        else:
            dn_ref[...] = dn_ref[...] + term
    norm_back_stage(mid_ref, gain, dn_ref, dx_ref, sums_ref, dout_ref)


def adjoint_stage(dout_ref, w_refs, a_ref, kbuf, state, lam_ref, prod_ref):
    rows = dout_ref.shape[0]
    part = w_refs[0].shape[2]
    hc = min(HC, part)
    steps = rows // 16
    for j, w in enumerate(w_refs):
        for c0 in range(0, part, hc):
            cols = slice(j * part + c0, j * part + c0 + hc)
            kbuf[0, :, :hc] = dot_nn(dout_ref[...], w[0, :, c0 : c0 + hc])

            def body(i, carry):
                mu, prod = carry
                r = pl.ds(pl.multiple_of((steps - 1 - i) * 16, 16), 16)
                u = kbuf[0, r, :hc]
                a = a_ref[r, cols]
                lam1 = u[8:] + mu
                mu = a[8:] * lam1
                lam0 = u[:8] + mu
                mu = a[:8] * lam0
                prod0 = prod * a[8:]
                lam_ref[r, cols] = jnp.concatenate([lam0, lam1])
                prod_ref[r, cols] = jnp.concatenate([prod0, prod])
                return mu, prod0 * a[:8]

            mu, prod = lax.fori_loop(0, steps, body, (state[0, :, cols], state[1, :, cols]))
            state[0, :, cols] = mu
            state[1, :, cols] = prod


def keys_stage(start, lam_ref, prod_ref, cf_ref, ci_ref, q_ref, dkf_ref, dki_ref, dkc_ref, bias_ref):
    rows, hidden = lam_ref.shape
    hc = min(HC, hidden)
    for c0 in range(0, hidden, hc):
        cols = slice(c0, c0 + hc)
        c = jnp.concatenate([start[:, cols], start[:, cols]])

        def body(r, sums):
            lam = lam_ref[r, cols] + prod_ref[r, cols] * c
            df = (lam * cf_ref[r, cols].astype(F32)).astype(BF)
            di = (lam * ci_ref[r, cols].astype(F32)).astype(BF)
            dkf_ref[r, cols] = df
            dki_ref[r, cols] = di
            dkc_ref[r, cols] = (lam * q_ref[r, cols].astype(F32)).astype(BF)
            df, di = df.astype(F32), di.astype(F32)
            return sums[0] + df[:8] + df[8:], sums[1] + di[:8] + di[8:]

        sf, si = rows_loop(rows, 16, body, (bias_ref[0, :, cols], bias_ref[1, :, cols]))
        bias_ref[0, :, cols] = sf
        bias_ref[1, :, cols] = si


def keys_back_stage(dk_refs, w_refs, dn_ref):
    part = w_refs[0].shape[2]
    total = None
    for j, w in enumerate(w_refs):
        for k in range(3):
            term = dot_nt(dk_refs[k][:, j * part : (j + 1) * part], w[k])
            total = term if total is None else total + term
    dn_ref[...] = total


def spread(src_ref, dst, lanes):
    steps = src_ref.shape[1]
    for c in range(lanes.shape[0]):
        cols = slice(c * 128, c * 128 + 128)
        for s in range(SEG):
            lanes[c, pl.ds(s, steps, stride=SEG), :] = src_ref[s, :, cols].astype(F32)
        dst[:, cols] = lanes[c]


def gather_out(src, dst_ref, lanes):
    steps = dst_ref.shape[1]
    for c in range(lanes.shape[0]):
        cols = slice(c * 128, c * 128 + 128)
        lanes[c] = src[:, cols]
        for s in range(SEG):
            dst_ref[s, :, cols] = lanes[c, pl.ds(s, steps, stride=SEG), :]


def k_first(n_parts, in_ref, gain_ref, bias_ref, *refs):
    w = refs[:n_parts]
    xp, nin, a, loc, prod, cand, wf, wi, q, ends, fin, kbuf, state, lanes = refs[n_parts:]
    g = pl.program_id(0)

    @pl.when(g == 0)
    def _():
        state[0] = jnp.zeros_like(state[0])
        state[1] = jnp.ones_like(state[1])

    spread(in_ref, xp, lanes)
    norm_stage(xp, gain_ref[0:1, :], nin)
    gate_stage(nin, bias_ref, w, kbuf, state, (a, loc, prod, cand, wf, wi, q))

    @pl.when(g == pl.num_programs(0) - 1)
    def _():
        fold_forward(state, ends, fin, w[0].shape[2])


def k_middle(n_parts, info, inc, ends_in, x, loc, prod, loc_b, prod_b, cand, wf, wi, gain, gain_next, bias, *refs):
    wo = refs[:n_parts]
    m = refs[n_parts : 2 * n_parts]
    w = refs[2 * n_parts : 3 * n_parts]
    (hlow, cf, ci, mid, nmid, act, slope, xn, nin, a, loc_o, prod_o, cand_o, wf_o, wi_o, q_o, ends, fin) = refs[
        3 * n_parts : 3 * n_parts + 18
    ]
    kbuf, state, start = refs[3 * n_parts + 18 :]
    g = pl.program_id(0)

    @pl.when(g == 0)
    def _():
        state[0] = jnp.zeros_like(state[0])
        state[1] = jnp.ones_like(state[1])
        carry_forward(inc, ends_in, start, (info[1] > 0).astype(F32))

    state_stage(g == 0, start, (loc, prod, loc_b, prod_b, cand, wf, wi), hlow, cf, ci)
    mlp_stage(x, hlow, wo, m, gain[1:2, :], kbuf, mid, nmid, act, slope, xn)
    norm_stage(xn, gain_next[0:1, :], nin)
    gate_stage(nin, bias, w, kbuf, state, (a, loc_o, prod_o, cand_o, wf_o, wi_o, q_o))

    @pl.when(g == pl.num_programs(0) - 1)
    def _():
        fold_forward(state, ends, fin, w[0].shape[2])


def k_turn(n_parts, info, inc, ends_in, x, loc, prod, loc_b, prod_b, cand, wf, wi, a, gain, cot, *refs):
    wo = refs[:n_parts]
    m = refs[n_parts : 2 * n_parts]
    (hlow, cf, ci, nmid, act, out, dz, dpre, dout, dx, lam, prod_o, ends, fin, sums) = refs[
        2 * n_parts : 2 * n_parts + 15
    ]
    kbuf, state, start, mid, slope, xn, dn, lanes = refs[2 * n_parts + 15 :]
    g = pl.program_id(0)
    tile = pl.num_programs(0) - 1 - g
    rows = x.shape[0]
    steps_all = pl.num_programs(0) * (rows // SEG)

    @pl.when(g == 0)
    def _():
        state[0] = jnp.zeros_like(state[0])
        state[1] = jnp.ones_like(state[1])
        sums[...] = jnp.zeros_like(sums)
        carry_forward(inc, ends_in, start, (info[1] > 0).astype(F32))

    state_stage(tile == 0, start, (loc, prod, loc_b, prod_b, cand, wf, wi), hlow, cf, ci)
    mlp_stage(x, hlow, wo, m, gain[1:2, :], kbuf, mid, nmid, act, slope, xn)
    at = lax.broadcasted_iota(jnp.int32, (rows, 1), 0)
    place = info[1] * (SEG * steps_all) + (at % SEG) * steps_all + tile * (rows // SEG) + at // SEG
    mask = (place < info[0]).astype(F32)
    xn[...] = xn[...] * mask
    gather_out(xn, out, lanes)
    spread(cot, dx, lanes)
    dx[...] = dx[...] * mask
    mlp_back_stage(dx, slope, mid, m, gain[1:2, :], kbuf, dn, dz, dpre, dout, sums)
    adjoint_stage(dout, wo, a, kbuf, state, lam, prod_o)

    @pl.when(g == pl.num_programs(0) - 1)
    def _():
        fold_backward(state, ends, fin, wo[0].shape[2])


def k_return(n_parts, info, inc, ends_in, lam, prod, cf, ci, q, x, dx_in, mid, slope, a, gain, gain_prev, *refs):
    w = refs[:n_parts]
    m = refs[n_parts : 2 * n_parts]
    wo = refs[2 * n_parts : 3 * n_parts]
    (dkf, dki, dkc, dz, dpre, dout, dx, lam_o, prod_o, ends, fin, sums_in, sums_mid, bias) = refs[
        3 * n_parts : 3 * n_parts + 14
    ]
    kbuf, state, start, dn = refs[3 * n_parts + 14 :]
    g = pl.program_id(0)

    @pl.when(g == 0)
    def _():
        state[0] = jnp.zeros_like(state[0])
        state[1] = jnp.ones_like(state[1])
        sums_in[...] = jnp.zeros_like(sums_in)
        sums_mid[...] = jnp.zeros_like(sums_mid)
        bias[...] = jnp.zeros_like(bias)
        carry_backward(inc, ends_in, start, (info[1] < info[2] - 1).astype(F32))

    keys_stage(start, lam, prod, cf, ci, q, dkf, dki, dkc, bias)
    keys_back_stage((dkf, dki, dkc), w, dn)
    dx[...] = dx_in[...]
    norm_back_stage(x, gain[0:1, :], dn, dx, sums_in, None)
    mlp_back_stage(dx, slope, mid, m, gain_prev[1:2, :], kbuf, dn, dz, dpre, dout, sums_mid)
    adjoint_stage(dout, wo, a, kbuf, state, lam_o, prod_o)

    @pl.when(g == pl.num_programs(0) - 1)
    def _():
        fold_backward(state, ends, fin, wo[0].shape[2])


def k_last(n_parts, info, inc, ends_in, lam, prod, cf, ci, q, x, dx_in, gain, *refs):
    w = refs[:n_parts]
    dkf, dki, dkc, out, sums_in, bias = refs[n_parts : n_parts + 6]
    start, dn, dx, lanes = refs[n_parts + 6 :]
    g = pl.program_id(0)

    @pl.when(g == 0)
    def _():
        sums_in[...] = jnp.zeros_like(sums_in)
        bias[...] = jnp.zeros_like(bias)
        carry_backward(inc, ends_in, start, (info[1] < info[2] - 1).astype(F32))

    keys_stage(start, lam, prod, cf, ci, q, dkf, dki, dkc, bias)
    keys_back_stage((dkf, dki, dkc), w, dn)
    dx[...] = dx_in[...]
    norm_back_stage(x, gain[0:1, :], dn, dx, sums_in, None)
    gather_out(dx, out, lanes)


def k_grads(pairs, *refs):
    out = refs[-1]
    for k, (left, right) in enumerate(pairs):
        out[k] = dot_tn(refs[left][...], refs[right][...]).astype(BF)


def k_rotate(n_recv, share, owner, basis, blocks, own, *refs):
    recv = refs[:n_recv]
    out = refs[n_recv]
    order = blocks.shape[-1]
    total = own[0].astype(F32)
    for ref in recv:
        total = total + ref[0].astype(F32)
    low = total.astype(BF)
    turned = jnp.concatenate(
        [
            dot_nn(low[:, b * order : (b + 1) * order], blocks[0, b].astype(BF))
            for b in range(blocks.shape[1])
        ],
        axis=1,
    ).astype(BF)
    done = dot_tn(basis[0].astype(BF), turned).astype(BF)
    for b in range(done.shape[0] // share):
        at = pl.multiple_of(owner[b] * share, share)
        out[pl.ds(at, share), :] = done[b * share : (b + 1) * share, :]


def k_apply(share, owner, basis, blocks, moves, weight, out, sorted_moves):
    order = blocks.shape[-1]
    for b in range(moves.shape[0] // share):
        at = pl.multiple_of(owner[b] * share, share)
        sorted_moves[b * share : (b + 1) * share, :] = moves[pl.ds(at, share), :]
    back = dot_nn(basis[0].astype(BF), sorted_moves[...]).astype(BF)
    for b in range(blocks.shape[1]):
        cols = slice(b * order, (b + 1) * order)
        step = dot_nt(back[:, cols], blocks[0, b].astype(BF))
        old = weight[0, :, cols]
        out[0, :, cols] = old - MATRIX_RATE * (step + DECAY_RATE * old)


def adam_moments(grads, first, second, fix_one, fix_two):
    first = BETA_ONE * first + (1.0 - BETA_ONE) * grads
    second = BETA_TWO * second + (1.0 - BETA_TWO) * grads * grads
    moves = first / fix_one / (jnp.sqrt(second / fix_two) + ADAM_EPS)
    return (first, second, moves)


def params(parallel=False):
    return pltpu.CompilerParams(
        dimension_semantics=("arbitrary",), vmem_limit_bytes=VMEM_LIMIT
    )


def sds(*shape, dtype=F32):
    return jax.ShapeDtypeStruct(shape, dtype)


def per_device(
    inputs,
    cotangent,
    lengths,
    hidden_weights,
    mlp_weights,
    norm_gains,
    gate_bias,
    left_bases,
    hidden_blocks,
    mlp_blocks,
    hidden_first,
    hidden_second,
    mlp_first,
    mlp_second,
    gain_first,
    gain_second,
    bias_first,
    bias_second,
    step_count,
    row_owner,
):
    dp_count = lax.axis_size("dp")
    mp = lax.axis_size("mp")
    me = lax.axis_index("mp")
    tokens = inputs.shape[1]
    width = inputs.shape[2]
    part_h = hidden_weights.shape[3]
    part_f = mlp_weights.shape[3]
    hid = part_h * mp
    ff = part_f * mp
    layers = hidden_weights.shape[0]
    steps = tokens // SEG
    ts = min(TILE_STEPS, steps)
    tr = ts * SEG
    grid = steps // ts
    hc = min(HC, part_h)
    share = width // dp_count

    def from_peer(value, j):
        return lax.ppermute(value, "mp", [((m + j) % mp, m) for m in range(mp)])

    def to_next(value):
        return lax.ppermute(value, "mp", [(m, (m + 1) % mp) for m in range(mp)])

    def to_prev(value):
        return lax.ppermute(value, "mp", [((m + 1) % mp, m) for m in range(mp)])

    hid_parts, mlp_parts = [], []
    for l in range(layers):
        own = hidden_weights[l].astype(BF)
        hid_parts.append([own] + [from_peer(own, j) for j in range(1, mp)])
    for l in range(layers):
        own = mlp_weights[l].astype(BF)
        mlp_parts.append([own] + [from_peer(own, j) for j in range(1, mp)])
    bias_all = jnp.concatenate([gate_bias] + [from_peer(gate_bias, j) for j in range(1, mp)], axis=2)
    info = jnp.stack([lengths[0], me, jnp.int32(mp)]).astype(jnp.int32)

    def make_specs(order):
        def tile(cols):
            return pl.BlockSpec((tr, cols), lambda g: (order(g), 0))

        return tile

    def whole(*shape):
        return pl.BlockSpec(shape, lambda g: (0,) * len(shape), pipeline_mode=pl.Buffered(1))

    smem = pl.BlockSpec(memory_space=pltpu.SMEM)
    fwd = make_specs(lambda g: g)
    rev = make_specs(lambda g: grid - 1 - g)
    seg_fwd = pl.BlockSpec((SEG, ts, width), lambda g: (0, g, 0))
    seg_rev = pl.BlockSpec((SEG, ts, width), lambda g: (0, grid - 1 - g, 0))
    before_fwd = pl.BlockSpec((SEG, hid), lambda g: (jnp.maximum(g * ts - 1, 0), 0))
    before_rev = pl.BlockSpec((SEG, hid), lambda g: (jnp.maximum((grid - 1 - g) * ts - 1, 0), 0))
    gates_spec = pl.BlockSpec((3, width, part_h), lambda g: (0, 0, 0), pipeline_mode=pl.Buffered(1))
    wout_spec = pl.BlockSpec((1, width, part_h), lambda g: (3, 0, 0), pipeline_mode=pl.Buffered(1))
    mlp_spec = whole(2, width, part_f)
    gain_spec = whole(2, width)
    bias_spec = whole(2, hid)
    ends_spec = pl.BlockSpec((2, SEG, hid), lambda g: (0, 0, 0))
    fin_spec = pl.BlockSpec((2, hid), lambda g: (0, 0))
    sums_spec = pl.BlockSpec((SEG, width), lambda g: (0, 0))
    bsum_spec = pl.BlockSpec((2, SEG, hid), lambda g: (0, 0, 0))
    kbuf = pltpu.VMEM((3, tr, HC), F32)
    state = pltpu.VMEM((2, SEG, hid), F32)
    start = pltpu.VMEM((SEG, hid), F32)
    row_f32 = pltpu.VMEM((tr, width), F32)
    lanes = pltpu.VMEM((width // 128, tr, 128), F32)

    t_w = sds(tokens, width)
    t_wb = sds(tokens, width, dtype=BF)
    t_h = sds(tokens, hid)
    t_hb = sds(tokens, hid, dtype=BF)
    t_fb = sds(tokens, ff, dtype=BF)
    ends_s = sds(2, SEG, hid)
    fin_s = sds(2, hid)
    sums_s = sds(SEG, width)
    bsum_s = sds(2, SEG, hid)

    def cost(matmul_cols, elems):
        return pl.CostEstimate(
            flops=2 * tokens * width * matmul_cols,
            bytes_accessed=elems,
            transcendentals=0,
        )

    def chain(fin, send, shift, live):
        carry = send(fin)
        for _ in range(mp - 2):
            known = jnp.roll(carry[0:1] * live, shift, axis=1)
            carry = send(jnp.concatenate([fin[0:1] + fin[1:2] * known, fin[1:2]]))
        return carry

    def chain_forward(fin):
        return chain(fin, to_next, -part_h, (me > 0).astype(F32))

    def chain_backward(fin):
        return chain(fin, to_prev, part_h, (me < mp - 1).astype(F32))

    seg_in = inputs.reshape(SEG, steps, width)
    seg_cot = cotangent.reshape(SEG, steps, width)
    saved = []
    f1_out_specs = lambda t: [t(width), t(hid), t(hid), t(hid), t(hid), t(hid), t(hid), t(hid), ends_spec, fin_spec]
    f1_out_shapes = [t_wb, t_h, t_h, t_h, t_hb, t_hb, t_hb, t_hb, ends_s, fin_s]
    outs = pl.pallas_call(
        functools.partial(k_first, mp),
        grid=(grid,),
        in_specs=[seg_fwd, gain_spec, bias_spec] + [gates_spec] * mp,
        out_specs=[fwd(width)] + f1_out_specs(fwd),
        out_shape=[t_w] + f1_out_shapes,
        scratch_shapes=[kbuf, state, lanes],
        compiler_params=params(),
        cost_estimate=cost(3 * hid, 24 * 2**20),
        name="gates_first",
    )(seg_in, norm_gains[0], bias_all[0], *hid_parts[0])
    x, gate = outs[0], outs[1:]
    xs = [x]
    for l in range(layers - 1):
        nin, a, loc, prod, cand, wf, wi, q, ends, fin = gate
        inc = chain_forward(fin)
        outs = pl.pallas_call(
            functools.partial(k_middle, mp),
            grid=(grid,),
            in_specs=[smem, fin_spec, ends_spec, fwd(width), fwd(hid), fwd(hid), before_fwd, before_fwd]
            + [fwd(hid)] * 3
            + [gain_spec, gain_spec, bias_spec]
            + [wout_spec] * mp
            + [mlp_spec] * mp
            + [gates_spec] * mp,
            out_specs=[fwd(hid)] * 3 + [fwd(width)] * 2 + [fwd(ff)] * 2 + [fwd(width)] + f1_out_specs(fwd),
            out_shape=[t_hb] * 3 + [t_w, t_wb, t_fb, t_fb, t_w] + f1_out_shapes,
            scratch_shapes=[kbuf, state, start],
            compiler_params=params(),
            cost_estimate=cost(4 * hid + 2 * ff, 60 * 2**20),
            name="block_forward",
        )(
            info, inc, ends, xs[l], loc, prod, loc, prod, cand, wf, wi,
            norm_gains[l], norm_gains[l + 1], bias_all[l + 1],
            *hid_parts[l], *mlp_parts[l], *hid_parts[l + 1],
        )
        hlow, cf, ci, mid, nmid, act, slope, xn = outs[:8]
        saved.append((nin, a, q, hlow, cf, ci, mid, nmid, act, slope))
        xs.append(xn)
        gate = outs[8:]
    top = layers - 1
    nin, a, loc, prod, cand, wf, wi, q, ends, fin = gate
    inc = chain_forward(fin)
    outs = pl.pallas_call(
        functools.partial(k_turn, mp),
        grid=(grid,),
        in_specs=[smem, fin_spec, ends_spec, rev(width), rev(hid), rev(hid), before_rev, before_rev]
        + [rev(hid)] * 4
        + [gain_spec, seg_rev]
        + [wout_spec] * mp
        + [mlp_spec] * mp,
        out_specs=[rev(hid)] * 3
        + [rev(width), rev(ff), seg_rev, rev(width), rev(ff), rev(width), rev(width), rev(hid), rev(hid)]
        + [ends_spec, fin_spec, sums_spec],
        out_shape=[t_hb] * 3
        + [t_wb, t_fb, sds(SEG, steps, width), t_wb, t_fb, t_wb, t_w, t_h, t_h, ends_s, fin_s, sums_s],
        scratch_shapes=[kbuf, state, start, row_f32, pltpu.VMEM((tr, ff), BF), row_f32, row_f32, lanes],
        compiler_params=params(),
        cost_estimate=cost(2 * hid + 4 * ff, 60 * 2**20),
        name="block_turn",
    )(
        info, inc, ends, xs[top], loc, prod, loc, prod, cand, wf, wi, a, norm_gains[top], seg_cot,
        *hid_parts[top], *mlp_parts[top],
    )
    hlow, cf, ci, nmid, act, output, dz, dpre, dout, dx, lam, rprod, ends, fin, sums_mid = outs
    output = output.reshape(1, tokens, width)
    saved.append((nin, a, q, hlow, cf, ci, None, nmid, act, None))

    def weight_grads(pairs, lefts, rights, part, wide, block):
        count = len(pairs)
        per = wide // block
        in_specs = [pl.BlockSpec((tokens, width), lambda g: (0, 0), pipeline_mode=pl.Buffered(1)) for _ in lefts]
        in_specs += [pl.BlockSpec((tokens, block), lambda g: (0, part * per + g)) for _ in rights]
        return pl.pallas_call(
            functools.partial(k_grads, pairs),
            grid=(per,),
            in_specs=in_specs,
            out_specs=pl.BlockSpec((count, width, block), lambda g: (0, 0, g)),
            out_shape=sds(count, width, wide, dtype=BF),
            compiler_params=params(),
            cost_estimate=cost(count * wide, tokens * wide * count * 2),
            name="weight_grads",
        )(*lefts, *rights)

    def reduce_parts(pairs, lefts, rights, wide):
        block = min(256, wide)
        others = []
        for j in range(1, mp):
            sent = weight_grads(pairs, lefts, rights, j, wide, block)
            others.append(lax.ppermute(sent, "mp", [(m, (m + j) % mp) for m in range(mp)]))
        return weight_grads(pairs, lefts, rights, 0, wide, block), others

    def rotate(own, others, basis, blocks):
        count, _, wide = own.shape
        block = min(512, wide)
        per = wide // block
        nb = block // blocks.shape[-1]
        order = blocks.shape[-1]
        piece = pl.BlockSpec((1, width, block), lambda g: (g // per, 0, g % per))
        return pl.pallas_call(
            functools.partial(k_rotate, mp - 1, share),
            grid=(count * per,),
            in_specs=[
                smem,
                pl.BlockSpec((1, width, width), lambda g: (g // per, 0, 0)),
                pl.BlockSpec((1, nb, order, order), lambda g: (g // per, g % per, 0, 0)),
            ]
            + [piece] * mp,
            out_specs=pl.BlockSpec((width, block), lambda g: (0, g)),
            out_shape=sds(width, count * wide, dtype=BF),
            compiler_params=params(),
            cost_estimate=cost(count * wide // 2, width * wide * count * 8),
            name="rotate",
        )(row_owner, basis, blocks, own, *others)

    def apply_moves(moves, basis, blocks, weight):
        count, _, wide = weight.shape
        block = min(512, wide)
        per = wide // block
        order = blocks.shape[-1]
        nb = block // order
        piece = pl.BlockSpec((1, width, block), lambda g: (g // per, 0, g % per))
        return pl.pallas_call(
            functools.partial(k_apply, share),
            grid=(count * per,),
            in_specs=[
                smem,
                pl.BlockSpec((1, width, width), lambda g: (g // per, 0, 0)),
                pl.BlockSpec((1, nb, order, order), lambda g: (g // per, g % per, 0, 0)),
                pl.BlockSpec((width, block), lambda g: (0, g)),
                piece,
            ],
            out_specs=piece,
            out_shape=sds(count, width, wide),
            scratch_shapes=[pltpu.VMEM((width, block), BF)],
            compiler_params=params(),
            cost_estimate=cost(count * wide // 2, width * wide * count * 10),
            name="apply_moves",
        )(row_owner, basis, blocks, moves, weight)

    count_value = step_count[0].astype(F32)
    fix_one = 1.0 - jnp.power(jnp.float32(BETA_ONE), count_value)
    fix_two = 1.0 - jnp.power(jnp.float32(BETA_TWO), count_value)

    def finish(own, others, basis, blocks, first, second, weight):
        count, _, wide = own.shape
        rotated = rotate(own, others, basis, blocks)
        mine = lax.psum_scatter(rotated, "dp", scatter_dimension=0, tiled=True)
        grad = mine.astype(F32).reshape(share, count, wide)
        first, second, moves = adam_moments(grad, first, second, fix_one, fix_two)
        moves = moves.astype(BF).reshape(share, count * wide)
        moves = lax.all_gather(moves, "dp", axis=0, tiled=True)
        return grad, first, second, apply_moves(moves, basis, blocks, weight)

    def all_sum(value):
        step = 1
        while step < dp_count:
            value = value + lax.ppermute(value, "dp", [(i, i ^ step) for i in range(dp_count)])
            step *= 2
        return value

    hid_done = [None] * layers
    mlp_done = [None] * layers
    small = [None] * layers
    for l in reversed(range(layers)):
        nin, a, q, hlow, cf, ci, mid, nmid, act, slope = saved[l]
        inc = chain_backward(fin)
        mlp_own, mlp_others = reduce_parts(((0, 2), (1, 3)), (nmid, dz), (dpre, act), part_f)
        mlp_done[l] = finish(
            mlp_own, mlp_others, left_bases[l, 4:], mlp_blocks[l], mlp_first[:, l], mlp_second[:, l], mlp_weights[l]
        )
        if l > 0:
            below = saved[l - 1]
            outs = pl.pallas_call(
                functools.partial(k_return, mp),
                grid=(grid,),
                in_specs=[smem, fin_spec, ends_spec]
                + [rev(hid)] * 5
                + [rev(width)] * 3
                + [rev(ff), rev(hid), gain_spec, gain_spec]
                + [gates_spec] * mp
                + [mlp_spec] * mp
                + [wout_spec] * mp,
                out_specs=[rev(hid)] * 3
                + [rev(width), rev(ff), rev(width), rev(width), rev(hid), rev(hid)]
                + [ends_spec, fin_spec, sums_spec, sums_spec, bsum_spec],
                out_shape=[t_hb] * 3
                + [t_wb, t_fb, t_wb, t_w, t_h, t_h, ends_s, fin_s, sums_s, sums_s, bsum_s],
                scratch_shapes=[kbuf, state, start, row_f32],
                compiler_params=params(),
                cost_estimate=cost(4 * hid + 2 * ff, 60 * 2**20),
                name="block_return",
            )(
                info, inc, ends, lam, rprod, cf, ci, q, xs[l], dx, below[6], below[9], below[1],
                norm_gains[l], norm_gains[l - 1],
                *hid_parts[l], *mlp_parts[l - 1], *hid_parts[l - 1],
            )
            dkf, dki, dkc, dz, dpre, dout_next, dx, lam, rprod, ends, fin, sums_in, sums_next, bsum = outs
        else:
            outs = pl.pallas_call(
                functools.partial(k_last, mp),
                grid=(grid,),
                in_specs=[smem, fin_spec, ends_spec]
                + [rev(hid)] * 5
                + [rev(width)] * 2
                + [gain_spec]
                + [gates_spec] * mp,
                out_specs=[rev(hid)] * 3 + [seg_rev, sums_spec, bsum_spec],
                out_shape=[t_hb] * 3 + [sds(SEG, steps, width), sums_s, bsum_s],
                scratch_shapes=[start, row_f32, row_f32, lanes],
                compiler_params=params(),
                cost_estimate=cost(3 * hid, 30 * 2**20),
                name="block_last",
            )(info, inc, ends, lam, rprod, cf, ci, q, xs[l], dx, norm_gains[l], *hid_parts[l])
            dkf, dki, dkc, input_grad, sums_in, bsum = outs
            dout_next, sums_next = None, None
        hid_own, hid_others = reduce_parts(
            ((0, 2), (0, 3), (0, 4), (1, 5)), (nin, dout), (dkf, dki, dkc, hlow), part_h
        )
        hid_done[l] = finish(
            hid_own, hid_others, left_bases[l, :4], hidden_blocks[l], hidden_first[:, l], hidden_second[:, l],
            hidden_weights[l],
        )
        gains = jnp.stack([sums_in.sum(0), sums_mid.sum(0)])
        biases = bsum.sum(1)
        vector = jnp.concatenate([gains.reshape(-1), biases[:, :part_h].reshape(-1)])
        total = vector
        for j in range(1, mp):
            sent = jnp.concatenate([gains.reshape(-1), biases[:, j * part_h : (j + 1) * part_h].reshape(-1)])
            total = total + lax.ppermute(sent, "mp", [(m, (m + j) % mp) for m in range(mp)])
        total = all_sum(total.reshape(-1, 128)).reshape(-1)
        small[l] = (total[: 2 * width].reshape(2, width), total[2 * width :].reshape(2, part_h))
        dout, sums_mid = dout_next, sums_next
    input_grad = input_grad.reshape(1, tokens, width)
    hidden_grad, hidden_first_new, hidden_second_new = (
        jnp.stack([hid_done[l][i] for l in range(layers)], axis=1) for i in range(3)
    )
    mlp_grad, mlp_first_new, mlp_second_new = (
        jnp.stack([mlp_done[l][i] for l in range(layers)], axis=1) for i in range(3)
    )
    hidden_new = jnp.stack([hid_done[l][3] for l in range(layers)])
    mlp_new = jnp.stack([mlp_done[l][3] for l in range(layers)])
    gain_grad = jnp.stack([small[l][0] for l in range(layers)])
    bias_grad = jnp.stack([small[l][1] for l in range(layers)])
    gain_first_new, gain_second_new, gain_moves = adam_moments(
        gain_grad, gain_first, gain_second, fix_one, fix_two
    )
    bias_first_new, bias_second_new, bias_moves = adam_moments(
        bias_grad, bias_first, bias_second, fix_one, fix_two
    )
    gain_new = norm_gains - GAIN_RATE * gain_moves
    bias_new = gate_bias - BIAS_RATE * bias_moves
    return (
        output,
        input_grad,
        hidden_grad,
        hidden_first_new,
        hidden_second_new[:, :, 2:],
        hidden_second_new[:, :, :2],
        hidden_new,
        mlp_grad,
        mlp_first_new,
        mlp_second_new,
        mlp_new,
        gain_grad,
        gain_first_new,
        gain_second_new,
        gain_new,
        bias_grad,
        bias_first_new,
        bias_second_new,
        bias_new,
    )


def solution(mesh):
    in_specs = (
        P("dp", "mp", None),
        P("dp", "mp", None),
        P("dp"),
        P(None, None, None, "mp"),
        P(None, None, None, "mp"),
        P(),
        P(None, None, "mp"),
        P(),
        P(None, None, "mp", None, None),
        P(None, None, "mp", None, None),
        P("dp", None, None, "mp"),
        P("dp", None, None, "mp"),
        P("dp", None, None, "mp"),
        P("dp", None, None, "mp"),
        P(),
        P(),
        P(None, None, "mp"),
        P(None, None, "mp"),
        P(),
        P(),
    )
    out_specs = (
        P("dp", "mp", None),
        P("dp", "mp", None),
        P("dp", None, None, "mp"),
        P("dp", None, None, "mp"),
        P("dp", None, None, "mp"),
        P("dp", None, None, "mp"),
        P(None, None, None, "mp"),
        P("dp", None, None, "mp"),
        P("dp", None, None, "mp"),
        P("dp", None, None, "mp"),
        P(None, None, None, "mp"),
        P(),
        P(),
        P(),
        P(),
        P(None, None, "mp"),
        P(None, None, "mp"),
        P(None, None, "mp"),
        P(None, None, "mp"),
    )
    return jax.shard_map(
        per_device, mesh=mesh, in_specs=in_specs, out_specs=out_specs, check_vma=False
    )
```

```python
import functools
import jax
import jax.numpy as jnp
from jax import lax
from jax.experimental import pallas as pl
from jax.experimental.pallas import tpu as pltpu
from jax.sharding import PartitionSpec as P

NORM_EPS = 1e-05
BETA_ONE = 0.9
BETA_TWO = 0.95
ADAM_EPS = 1e-08
MATRIX_RATE = 0.08
GAIN_RATE = 0.5
BIAS_RATE = 4.0
DECAY_RATE = 0.01
BF = jnp.bfloat16
F32 = jnp.float32
SEG = 8
TILE_STEPS = 32
HC = 512
VMEM_LIMIT = 58 * 1024 * 1024
LOG2E = 1.4426950408889634


def dot_nn(a, b):
    return lax.dot_general(a, b, (((1,), (0,)), ((), ())), preferred_element_type=F32)


def dot_nt(a, b):
    return lax.dot_general(a, b, (((1,), (1,)), ((), ())), preferred_element_type=F32)


def dot_tn(a, b):
    return lax.dot_general(a, b, (((0,), (0,)), ((), ())), preferred_element_type=F32)


def recip(x):
    r = pl.reciprocal(x, approx=True)
    return r * (2.0 - x * r)


def rows_loop(count, size, body, init=None, unroll=1):
    def step(i, carry):
        return body(pl.ds(pl.multiple_of(i * size, size), size), carry)

    return lax.fori_loop(0, count // size, step, init, unroll=unroll)


def row_scale(values):
    return lax.rsqrt(jnp.mean(values * values, axis=-1, keepdims=True) + NORM_EPS)


def norm_stage(x_ref, gain, out_ref):
    def body(r, c):
        x = x_ref[r, :]
        out_ref[r, :] = (x * row_scale(x) * gain).astype(BF)
        return c

    rows_loop(x_ref.shape[0], 32, body, 0)


def gate_stage(nin_ref, bias_ref, w_refs, kbuf, state, outs):
    a_ref, loc_ref, prod_ref, cand_ref, wf_ref, wi_ref, q_ref = outs
    rows = nin_ref.shape[0]
    part = w_refs[0].shape[2]
    hc = min(HC, part)
    for j, w in enumerate(w_refs):
        for c0 in range(0, part, hc):
            cols = slice(j * part + c0, j * part + c0 + hc)
            n = nin_ref[...]
            for k in range(3):
                kbuf[k, :, :hc] = dot_nn(n, w[k, :, c0 : c0 + hc])
            bias_f = bias_ref[0:1, cols]
            bias_i = bias_ref[1:2, cols]

            def body(r, carry):
                loc, prod = carry
                kf = kbuf[0, r, :hc] + bias_f
                ki = kbuf[1, r, :hc] + bias_i
                kc = kbuf[2, r, :hc]
                tf = jnp.exp(-jnp.abs(kf))
                ti = jnp.exp(-jnp.abs(ki))
                tc = jnp.exp(-jnp.abs(kc))
                of, oi = 1.0 + tf, 1.0 + ti
                gap = jnp.minimum(ki, 0.0) - jnp.minimum(kf, 0.0)
                e = jnp.exp(-jnp.abs(gap))
                nf = jnp.where(gap < 0, of * e, of)
                ni = jnp.where(gap > 0, oi * e, oi)
                inv = recip(nf + ni)
                keep = ni * inv
                take = nf * inv
                sf = jnp.where(kf >= 0, tf, 1.0) * recip(of)
                si = jnp.where(ki >= 0, ti, 1.0) * recip(oi)
                sc = tc * recip(1.0 + tc)
                up = kc >= 0
                cand = jnp.where(up, kc + 0.5, sc)
                slope = jnp.where(up, 1.0, sc * (1.0 - sc))
                both = keep * take
                a_ref[r, cols] = keep
                cand_ref[r, cols] = cand.astype(BF)
                wf_ref[r, cols] = (both * sf).astype(BF)
                wi_ref[r, cols] = (both * si).astype(BF)
                q_ref[r, cols] = (take * slope).astype(BF)
                drive = take * cand
                loc0 = keep[:8] * loc + drive[:8]
                prod0 = keep[:8] * prod
                loc1 = keep[8:] * loc0 + drive[8:]
                prod1 = keep[8:] * prod0
                loc_ref[r, cols] = jnp.concatenate([loc0, loc1])
                prod_ref[r, cols] = jnp.concatenate([prod0, prod1])
                return loc1, prod1

            loc, prod = rows_loop(rows, 16, body, (state[0, :, cols], state[1, :, cols]))
            state[0, :, cols] = loc
            state[1, :, cols] = prod


def fold_forward(state, ends_ref, fin_ref, part):
    hidden = state.shape[2]
    ends_ref[...] = state[...]
    loc = state[0, 0:1, :]
    prod = state[1, 0:1, :]
    for s in range(1, SEG):
        loc = state[0, s : s + 1, :] + state[1, s : s + 1, :] * loc
        prod = state[1, s : s + 1, :] * prod
    n = hidden // part
    for j in range(n):
        src = slice(((j + 1) % n) * part, ((j + 1) % n) * part + part)
        fin_ref[0:1, j * part : (j + 1) * part] = loc[:, src]
        fin_ref[1:2, j * part : (j + 1) * part] = prod[:, src]


def fold_backward(state, ends_ref, fin_ref, part):
    hidden = state.shape[2]
    ends_ref[...] = state[...]
    mu = state[0, SEG - 1 : SEG, :]
    prod = state[1, SEG - 1 : SEG, :]
    for s in reversed(range(SEG - 1)):
        mu = state[0, s : s + 1, :] + state[1, s : s + 1, :] * mu
        prod = state[1, s : s + 1, :] * prod
    n = hidden // part
    for j in range(n):
        src = slice(((j - 1) % n) * part, ((j - 1) % n) * part + part)
        fin_ref[0:1, j * part : (j + 1) * part] = mu[:, src]
        fin_ref[1:2, j * part : (j + 1) * part] = prod[:, src]


def carry_forward(inc_ref, ends_ref, start, live):
    start[0:1, :] = inc_ref[0:1, :] * live
    for s in range(SEG - 1):
        start[s + 1 : s + 2, :] = (
            ends_ref[0, s : s + 1, :] + ends_ref[1, s : s + 1, :] * start[s : s + 1, :]
        )


def carry_backward(inc_ref, ends_ref, start, live):
    start[SEG - 1 : SEG, :] = inc_ref[0:1, :] * live
    for s in reversed(range(1, SEG)):
        start[s - 1 : s, :] = (
            ends_ref[0, s : s + 1, :] + ends_ref[1, s : s + 1, :] * start[s : s + 1, :]
        )


def state_stage(first, start, ins, hlow_ref, cf_ref, ci_ref):
    loc_ref, prod_ref, loc_before, prod_before, cand_ref, wf_ref, wi_ref = ins
    rows, hidden = loc_ref.shape
    hc = min(HC, hidden)
    for c0 in range(0, hidden, hc):
        cols = slice(c0, c0 + hc)
        c = start[:, cols]
        before = jnp.where(first, c, loc_before[:, cols] + prod_before[:, cols] * c)

        def body(r, before):
            loc = loc_ref[r, cols]
            prod = prod_ref[r, cols]
            h0 = loc[:8] + prod[:8] * c
            h1 = loc[8:] + prod[8:] * c
            hlow_ref[r, cols] = jnp.concatenate([h0, h1]).astype(BF)
            diff = cand_ref[r, cols].astype(F32) - jnp.concatenate([before, h0])
            cf_ref[r, cols] = (-wf_ref[r, cols].astype(F32) * diff).astype(BF)
            ci_ref[r, cols] = (wi_ref[r, cols].astype(F32) * diff).astype(BF)
            return h1

        rows_loop(rows, 16, body, before)


def mlp_stage(x_ref, hlow_ref, w_refs, m_refs, gain, kbuf, mid_ref, nmid_ref, act_ref, slope_ref, xn_ref):
    rows = x_ref.shape[0]
    part = w_refs[0].shape[2]
    total = x_ref[...]
    for j, w in enumerate(w_refs):
        total = total + dot_nt(hlow_ref[:, j * part : (j + 1) * part], w[0])
    mid_ref[...] = total
    norm_stage(mid_ref, gain, nmid_ref)
    wide = m_refs[0].shape[2]
    fc = min(HC, wide)
    xn_ref[...] = mid_ref[...]
    for j, m in enumerate(m_refs):
        for c0 in range(0, wide, fc):
            cols = slice(j * wide + c0, j * wide + c0 + fc)
            kbuf[0, :, :fc] = dot_nn(nmid_ref[...], m[0, :, c0 : c0 + fc])

            def body(r, c):
                pre = kbuf[0, r, :fc]
                size = jnp.abs(pre)
                t = recip(1.0 + size * (0.3275911 * 0.7071067811865476))
                bell = jnp.exp(pre * pre * -0.5)
                poly = (
                    (((1.061405429 * t - 1.453152027) * t + 1.421413741) * t - 0.284496736) * t
                    + 0.254829592
                ) * t
                tail = (0.5 * poly) * bell
                cdf = jnp.where(pre >= 0, 1.0 - tail, tail)
                act_ref[r, cols] = (pre * cdf).astype(BF)
                slope_ref[r, cols] = (cdf + pre * (bell * 0.3989422804014327)).astype(BF)
                return c

            rows_loop(rows, 16, body, 0)
        xn_ref[...] = xn_ref[...] + dot_nt(act_ref[:, j * wide : (j + 1) * wide], m[1])


def norm_back_stage(src_ref, gain, dn_ref, dx_ref, sums_ref, low_ref):
    def body(r, total):
        x = src_ref[r, :]
        scale = row_scale(x)
        unit = x * scale
        d = dn_ref[r, :]
        e = d * gain
        dx = dx_ref[r, :] + scale * (e - unit * jnp.mean(e * unit, axis=-1, keepdims=True))
        dx_ref[r, :] = dx
        if low_ref is not None:
            low_ref[r, :] = dx.astype(BF)
        g = d * unit
        return total + g[:8] + g[8:16] + g[16:24] + g[24:]

    sums_ref[...] = rows_loop(src_ref.shape[0], 32, body, sums_ref[...])


def mlp_back_stage(dx_ref, slope_ref, mid_ref, m_refs, gain, kbuf, dn_ref, dz_ref, dpre_ref, dout_ref, sums_ref):
    rows = dx_ref.shape[0]
    dz_ref[...] = dx_ref[...].astype(BF)
    wide = m_refs[0].shape[2]
    fc = min(HC, wide)
    total = None
    for j, m in enumerate(m_refs):
        for c0 in range(0, wide, fc):
            cols = slice(j * wide + c0, j * wide + c0 + fc)
            kbuf[0, :, :fc] = dot_nn(dz_ref[...], m[1, :, c0 : c0 + fc])

            def body(r, c):
                dpre_ref[r, cols] = (kbuf[0, r, :fc] * slope_ref[r, cols].astype(F32)).astype(BF)
                return c

            rows_loop(rows, 32, body, 0)
        term = dot_nt(dpre_ref[:, j * wide : (j + 1) * wide], m[0])
        if j == 0:
            dn_ref[...] = term
        else:
            dn_ref[...] = dn_ref[...] + term
    norm_back_stage(mid_ref, gain, dn_ref, dx_ref, sums_ref, dout_ref)


def adjoint_stage(dout_ref, w_refs, a_ref, kbuf, state, lam_ref, prod_ref):
    rows = dout_ref.shape[0]
    part = w_refs[0].shape[2]
    hc = min(HC, part)
    steps = rows // 16
    for j, w in enumerate(w_refs):
        for c0 in range(0, part, hc):
            cols = slice(j * part + c0, j * part + c0 + hc)
            kbuf[0, :, :hc] = dot_nn(dout_ref[...], w[0, :, c0 : c0 + hc])

            def body(i, carry):
                mu, prod = carry
                r = pl.ds(pl.multiple_of((steps - 1 - i) * 16, 16), 16)
                u = kbuf[0, r, :hc]
                a = a_ref[r, cols]
                lam1 = u[8:] + mu
                mu = a[8:] * lam1
                lam0 = u[:8] + mu
                mu = a[:8] * lam0
                prod0 = prod * a[8:]
                lam_ref[r, cols] = jnp.concatenate([lam0, lam1])
                prod_ref[r, cols] = jnp.concatenate([prod0, prod])
                return mu, prod0 * a[:8]

            mu, prod = lax.fori_loop(0, steps, body, (state[0, :, cols], state[1, :, cols]))
            state[0, :, cols] = mu
            state[1, :, cols] = prod


def keys_stage(start, lam_ref, prod_ref, cf_ref, ci_ref, q_ref, dkf_ref, dki_ref, dkc_ref, bias_ref):
    rows, hidden = lam_ref.shape
    hc = min(HC, hidden)
    for c0 in range(0, hidden, hc):
        cols = slice(c0, c0 + hc)
        c = jnp.concatenate([start[:, cols], start[:, cols]])

        def body(r, sums):
            lam = lam_ref[r, cols] + prod_ref[r, cols] * c
            df = (lam * cf_ref[r, cols].astype(F32)).astype(BF)
            di = (lam * ci_ref[r, cols].astype(F32)).astype(BF)
            dkf_ref[r, cols] = df
            dki_ref[r, cols] = di
            dkc_ref[r, cols] = (lam * q_ref[r, cols].astype(F32)).astype(BF)
            df, di = df.astype(F32), di.astype(F32)
            return sums[0] + df[:8] + df[8:], sums[1] + di[:8] + di[8:]

        sf, si = rows_loop(rows, 16, body, (bias_ref[0, :, cols], bias_ref[1, :, cols]))
        bias_ref[0, :, cols] = sf
        bias_ref[1, :, cols] = si


def keys_back_stage(dk_refs, w_refs, dn_ref):
    part = w_refs[0].shape[2]
    total = None
    for j, w in enumerate(w_refs):
        for k in range(3):
            term = dot_nt(dk_refs[k][:, j * part : (j + 1) * part], w[k])
            total = term if total is None else total + term
    dn_ref[...] = total


def spread(src_ref, dst, lanes):
    steps = src_ref.shape[1]
    for c in range(lanes.shape[0]):
        cols = slice(c * 128, c * 128 + 128)
        for s in range(SEG):
            lanes[c, pl.ds(s, steps, stride=SEG), :] = src_ref[s, :, cols].astype(F32)
        dst[:, cols] = lanes[c]


def gather_out(src, dst_ref, lanes):
    steps = dst_ref.shape[1]
    for c in range(lanes.shape[0]):
        cols = slice(c * 128, c * 128 + 128)
        lanes[c] = src[:, cols]
        for s in range(SEG):
            dst_ref[s, :, cols] = lanes[c, pl.ds(s, steps, stride=SEG), :]


def k_first(n_parts, in_ref, gain_ref, bias_ref, *refs):
    w = refs[:n_parts]
    xp, nin, a, loc, prod, cand, wf, wi, q, ends, fin, kbuf, state, lanes = refs[n_parts:]
    g = pl.program_id(0)

    @pl.when(g == 0)
    def _():
        state[0] = jnp.zeros_like(state[0])
        state[1] = jnp.ones_like(state[1])

    spread(in_ref, xp, lanes)
    norm_stage(xp, gain_ref[0:1, :], nin)
    gate_stage(nin, bias_ref, w, kbuf, state, (a, loc, prod, cand, wf, wi, q))

    @pl.when(g == pl.num_programs(0) - 1)
    def _():
        fold_forward(state, ends, fin, w[0].shape[2])


def k_middle(n_parts, info, inc, ends_in, x, loc, prod, loc_b, prod_b, cand, wf, wi, gain, gain_next, bias, *refs):
    wo = refs[:n_parts]
    m = refs[n_parts : 2 * n_parts]
    w = refs[2 * n_parts : 3 * n_parts]
    (hlow, cf, ci, mid, nmid, act, slope, xn, nin, a, loc_o, prod_o, cand_o, wf_o, wi_o, q_o, ends, fin) = refs[
        3 * n_parts : 3 * n_parts + 18
    ]
    kbuf, state, start = refs[3 * n_parts + 18 :]
    g = pl.program_id(0)

    @pl.when(g == 0)
    def _():
        state[0] = jnp.zeros_like(state[0])
        state[1] = jnp.ones_like(state[1])
        carry_forward(inc, ends_in, start, (info[1] > 0).astype(F32))

    state_stage(g == 0, start, (loc, prod, loc_b, prod_b, cand, wf, wi), hlow, cf, ci)
    mlp_stage(x, hlow, wo, m, gain[1:2, :], kbuf, mid, nmid, act, slope, xn)
    norm_stage(xn, gain_next[0:1, :], nin)
    gate_stage(nin, bias, w, kbuf, state, (a, loc_o, prod_o, cand_o, wf_o, wi_o, q_o))

    @pl.when(g == pl.num_programs(0) - 1)
    def _():
        fold_forward(state, ends, fin, w[0].shape[2])


def k_turn(n_parts, info, inc, ends_in, x, loc, prod, loc_b, prod_b, cand, wf, wi, a, gain, cot, *refs):
    wo = refs[:n_parts]
    m = refs[n_parts : 2 * n_parts]
    (hlow, cf, ci, nmid, act, out, dz, dpre, dout, dx, lam, prod_o, ends, fin, sums) = refs[
        2 * n_parts : 2 * n_parts + 15
    ]
    kbuf, state, start, mid, slope, xn, dn, lanes = refs[2 * n_parts + 15 :]
    g = pl.program_id(0)
    tile = pl.num_programs(0) - 1 - g
    rows = x.shape[0]
    steps_all = pl.num_programs(0) * (rows // SEG)

    @pl.when(g == 0)
    def _():
        state[0] = jnp.zeros_like(state[0])
        state[1] = jnp.ones_like(state[1])
        sums[...] = jnp.zeros_like(sums)
        carry_forward(inc, ends_in, start, (info[1] > 0).astype(F32))

    state_stage(tile == 0, start, (loc, prod, loc_b, prod_b, cand, wf, wi), hlow, cf, ci)
    mlp_stage(x, hlow, wo, m, gain[1:2, :], kbuf, mid, nmid, act, slope, xn)
    at = lax.broadcasted_iota(jnp.int32, (rows, 1), 0)
    place = info[1] * (SEG * steps_all) + (at % SEG) * steps_all + tile * (rows // SEG) + at // SEG
    mask = (place < info[0]).astype(F32)
    xn[...] = xn[...] * mask
    gather_out(xn, out, lanes)
    spread(cot, dx, lanes)
    dx[...] = dx[...] * mask
    mlp_back_stage(dx, slope, mid, m, gain[1:2, :], kbuf, dn, dz, dpre, dout, sums)
    adjoint_stage(dout, wo, a, kbuf, state, lam, prod_o)

    @pl.when(g == pl.num_programs(0) - 1)
    def _():
        fold_backward(state, ends, fin, wo[0].shape[2])


def k_return(n_parts, info, inc, ends_in, lam, prod, cf, ci, q, x, dx_in, mid, slope, a, gain, gain_prev, *refs):
    w = refs[:n_parts]
    m = refs[n_parts : 2 * n_parts]
    wo = refs[2 * n_parts : 3 * n_parts]
    (dkf, dki, dkc, dz, dpre, dout, dx, lam_o, prod_o, ends, fin, sums_in, sums_mid, bias) = refs[
        3 * n_parts : 3 * n_parts + 14
    ]
    kbuf, state, start, dn = refs[3 * n_parts + 14 :]
    g = pl.program_id(0)

    @pl.when(g == 0)
    def _():
        state[0] = jnp.zeros_like(state[0])
        state[1] = jnp.ones_like(state[1])
        sums_in[...] = jnp.zeros_like(sums_in)
        sums_mid[...] = jnp.zeros_like(sums_mid)
        bias[...] = jnp.zeros_like(bias)
        carry_backward(inc, ends_in, start, (info[1] < info[2] - 1).astype(F32))

    keys_stage(start, lam, prod, cf, ci, q, dkf, dki, dkc, bias)
    keys_back_stage((dkf, dki, dkc), w, dn)
    dx[...] = dx_in[...]
    norm_back_stage(x, gain[0:1, :], dn, dx, sums_in, None)
    mlp_back_stage(dx, slope, mid, m, gain_prev[1:2, :], kbuf, dn, dz, dpre, dout, sums_mid)
    adjoint_stage(dout, wo, a, kbuf, state, lam_o, prod_o)

    @pl.when(g == pl.num_programs(0) - 1)
    def _():
        fold_backward(state, ends, fin, wo[0].shape[2])


def k_last(n_parts, info, inc, ends_in, lam, prod, cf, ci, q, x, dx_in, gain, *refs):
    w = refs[:n_parts]
    dkf, dki, dkc, out, sums_in, bias = refs[n_parts : n_parts + 6]
    start, dn, dx, lanes = refs[n_parts + 6 :]
    g = pl.program_id(0)

    @pl.when(g == 0)
    def _():
        sums_in[...] = jnp.zeros_like(sums_in)
        bias[...] = jnp.zeros_like(bias)
        carry_backward(inc, ends_in, start, (info[1] < info[2] - 1).astype(F32))

    keys_stage(start, lam, prod, cf, ci, q, dkf, dki, dkc, bias)
    keys_back_stage((dkf, dki, dkc), w, dn)
    dx[...] = dx_in[...]
    norm_back_stage(x, gain[0:1, :], dn, dx, sums_in, None)
    gather_out(dx, out, lanes)


def k_grads(pairs, *refs):
    out = refs[-1]
    for k, (left, right) in enumerate(pairs):
        out[k] = dot_tn(refs[left][...], refs[right][...]).astype(BF)


def digits_place(relative, stages):
    place = None
    for low, count in stages:
        digit = (relative >> low) & ((1 << count) - 1)
        place = digit if place is None else (place << count) + digit
    return place


def turn_blocks(value, blocks, inverse):
    order = blocks.shape[-1]
    dot = dot_nt if inverse else dot_nn
    return jnp.concatenate(
        [
            dot(value[:, b * order : (b + 1) * order], blocks[0, 0, b].astype(BF))
            for b in range(blocks.shape[2])
        ],
        axis=1,
    )


def k_rotate(plan, per_source, who, basis, *refs):
    n_src = len(plan.sources)
    blocks = refs[:n_src]
    grads = refs[n_src : n_src * (1 + per_source)]
    n_out = sum(plan.firsts)
    outs = refs[n_src * (1 + per_source) :][:n_out]
    bufs = refs[n_src * (1 + per_source) + n_out : -1]
    done = refs[-1]
    g = pl.program_id(0)
    share = plan.share
    for at in range(n_src):

        @pl.when((g >= plan.begins[at]) & (g < plan.begins[at + 1]))
        def _(at=at):
            mine = grads[at * per_source : (at + 1) * per_source]
            total = mine[0][0].astype(F32)
            for ref in mine[1:]:
                total = total + ref[0].astype(F32)
            turned = turn_blocks(total.astype(BF), blocks[at], False).astype(BF)
            done[:, : plan.blocks[at]] = dot_tn(basis[0, 0].astype(BF), turned).astype(BF)

    count = done.shape[0] // share
    relative = [who[b] ^ who[count] for b in range(count)]
    for chunk, runs in enumerate(plan.runs):

        @pl.when(g == chunk)
        def _(runs=runs):
            for stream, src, dst, wide in runs:
                for b in range(count):
                    at = digits_place(relative[b], plan.stages[stream]) * share
                    bufs[stream][pl.ds(pl.multiple_of(at, share), share), dst : dst + wide] = done[
                        b * share : (b + 1) * share, src : src + wide
                    ]

    @pl.when(g == pl.num_programs(0) - 1)
    def _():
        at = 0
        for stream, pieces in enumerate(plan.firsts):
            rows = done.shape[0] // pieces
            for r in range(pieces):
                outs[at][...] = bufs[stream][r * rows : (r + 1) * rows, :]
                at += 1


def sum_pieces(refs):
    total = refs[0][...].astype(F32)
    for ref in refs[1:]:
        total = total + ref[...].astype(F32)
    return total


def k_combine(n_in, n_out, *refs):
    i, o = 0, sum(n_in)
    for take, give in zip(n_in, n_out):
        total = sum_pieces(refs[i : i + take]).astype(BF)
        rows = total.shape[0] // give
        for r in range(give):
            refs[o + r][...] = total[r * rows : (r + 1) * rows, :]
        i += take
        o += give


def k_adam(plan, splits, n_alias, fix, *refs):
    n_in = sum(plan.lasts)
    n_src = len(plan.sources)
    pieces = refs[:n_in]
    olds = refs[n_in : n_in + 2 * n_src]
    outs = refs[n_in + 2 * n_src + n_alias :]
    bufs = refs[len(refs) - n_src :]
    moves_o = outs[sum(2 + len(split) for split in splits) :][: len(plan.stages)]
    sums, i = [], 0
    for take in plan.lasts:
        sums.append(sum_pieces(pieces[i : i + take]))
        i += take
    o = 0
    for at, split in enumerate(splits):
        grad_o, first_o = outs[o : o + 2]
        second_o = outs[o + 2 : o + 2 + len(split)]
        o += 2 + len(split)
        first, second = olds[2 * at : 2 * at + 2]
        for chunk in range(plan.begins[at], plan.begins[at + 1]):
            kind, base = plan.where(at, chunk)
            for stream, src, dst, wide in plan.runs[chunk]:
                grad_o[:, 0, kind, base + src : base + src + wide] = sums[stream][:, dst : dst + wide]
        grad = grad_o[...]
        one = BETA_ONE * first[...] + (1.0 - BETA_ONE) * grad
        two = BETA_TWO * second[...] + (1.0 - BETA_TWO) * grad * grad
        first_o[...] = one
        for ref, (lo, hi) in zip(second_o, split):
            ref[...] = two[:, :, lo:hi, :]
        bufs[at][...] = one * fix[0] / (jnp.sqrt(two * fix[1]) + ADAM_EPS)
        for chunk in range(plan.begins[at], plan.begins[at + 1]):
            kind, base = plan.where(at, chunk)
            for stream, src, dst, wide in plan.runs[chunk]:
                moves_o[stream][:, dst : dst + wide] = bufs[at][
                    :, 0, kind, base + src : base + src + wide
                ].astype(BF)


def k_apply(plan, n_alias, who, basis, *refs):
    n_src = len(plan.sources)
    n_in = sum(plan.firsts)
    blocks = refs[:n_src]
    weights = refs[n_src : 2 * n_src]
    pieces = refs[2 * n_src : 2 * n_src + n_in]
    outs = refs[2 * n_src + n_in + n_alias :][:n_src]
    bufs = refs[2 * n_src + n_in + n_alias + n_src : -1]
    moves = refs[-1]
    g = pl.program_id(0)
    share = plan.share
    width = basis.shape[2]
    count = width // share

    @pl.when(g == 0)
    def _():
        at = 0
        for stream, n in enumerate(plan.firsts):
            rows = width // n
            for r in range(n):
                bufs[stream][r * rows : (r + 1) * rows, :] = pieces[at][...]
                at += 1

    relative = [who[b] ^ who[count] for b in range(count)]
    for chunk, runs in enumerate(plan.runs):

        @pl.when(g == chunk)
        def _(runs=runs):
            for stream, src, dst, wide in runs:
                for b in range(count):
                    at = digits_place(relative[b], plan.stages[stream]) * share
                    moves[b * share : (b + 1) * share, src : src + wide] = bufs[stream][
                        pl.ds(pl.multiple_of(at, share), share), dst : dst + wide
                    ]

    for at in range(n_src):

        @pl.when((g >= plan.begins[at]) & (g < plan.begins[at + 1]))
        def _(at=at):
            wide = plan.blocks[at]
            back = dot_nn(basis[0, 0].astype(BF), moves[:, :wide]).astype(BF)
            step = turn_blocks(back, blocks[at], True)
            old = weights[at][0, 0]
            outs[at][0, 0] = old - MATRIX_RATE * (step + DECAY_RATE * old)


class Plan:
    def __init__(self, dp_count, width, sources):
        bits = dp_count.bit_length() - 1
        plane, rest = (0, 2), (2, bits - 2)
        orders = [[plane, rest], [rest, plane]]
        self.share = width // dp_count
        self.sources = sources
        self.blocks = [min(512, wide) for _, _, wide in sources]
        self.pers = [wide // block for (_, _, wide), block in zip(sources, self.blocks)]
        self.begins = [0]
        for (_, count, _), per in zip(sources, self.pers):
            self.begins.append(self.begins[-1] + count * per)
        chunks = self.begins[-1]
        named = []
        for at, block in enumerate(self.blocks):
            for chunk in range(self.begins[at], self.begins[at + 1]):
                lanes = block // 128
                cut = lanes - (1 if chunk % 3 else 2)
                named.append([0 if lane < max(cut, 1) else 1 for lane in range(lanes)])
        used = sorted({stream for row in named for stream in row})
        self.stages = [orders[stream] for stream in used]
        self.cols = [0] * len(used)
        self.runs = []
        for row in named:
            runs = []
            for lane, stream in enumerate(row):
                at = used.index(stream)
                if runs and runs[-1][0] == at:
                    runs[-1][3] += 128
                else:
                    runs.append([at, lane * 128, self.cols[at], 128])
                self.cols[at] += 128
            self.runs.append(runs)
        self.firsts = [1 << stages[0][1] for stages in self.stages]
        self.lasts = [1 << stages[-1][1] for stages in self.stages]

    def where(self, at, chunk):
        local = chunk - self.begins[at]
        return local // self.pers[at], local % self.pers[at] * self.blocks[at]

    def local(self, at, g):
        return jnp.clip(g - self.begins[at], 0, self.begins[at + 1] - self.begins[at] - 1)

    def basis_at(self, g):
        index = None
        for at, (base, _, _) in enumerate(self.sources):
            here = base + self.local(at, g) // self.pers[at]
            index = here if index is None else jnp.where(g < self.begins[at], index, here)
        return index


def adam_moments(grads, first, second, fix_one, fix_two):
    first = BETA_ONE * first + (1.0 - BETA_ONE) * grads
    second = BETA_TWO * second + (1.0 - BETA_TWO) * grads * grads
    moves = first / fix_one / (jnp.sqrt(second / fix_two) + ADAM_EPS)
    return (first, second, moves)


def params(parallel=False):
    return pltpu.CompilerParams(
        dimension_semantics=("arbitrary",), vmem_limit_bytes=VMEM_LIMIT
    )


def sds(*shape, dtype=F32):
    return jax.ShapeDtypeStruct(shape, dtype)


def per_device(
    inputs,
    cotangent,
    lengths,
    hidden_weights,
    mlp_weights,
    norm_gains,
    gate_bias,
    left_bases,
    hidden_blocks,
    mlp_blocks,
    hidden_first,
    hidden_second,
    mlp_first,
    mlp_second,
    gain_first,
    gain_second,
    bias_first,
    bias_second,
    step_count,
    row_owner,
):
    dp_count = lax.axis_size("dp")
    mp = lax.axis_size("mp")
    me = lax.axis_index("mp")
    tokens = inputs.shape[1]
    width = inputs.shape[2]
    part_h = hidden_weights.shape[3]
    part_f = mlp_weights.shape[3]
    hid = part_h * mp
    ff = part_f * mp
    layers = hidden_weights.shape[0]
    steps = tokens // SEG
    ts = min(TILE_STEPS, steps)
    tr = ts * SEG
    grid = steps // ts
    hc = min(HC, part_h)
    share = width // dp_count

    def from_peer(value, j):
        return lax.ppermute(value, "mp", [((m + j) % mp, m) for m in range(mp)])

    def to_next(value):
        return lax.ppermute(value, "mp", [(m, (m + 1) % mp) for m in range(mp)])

    def to_prev(value):
        return lax.ppermute(value, "mp", [((m + 1) % mp, m) for m in range(mp)])

    hid_parts, mlp_parts = [], []
    for l in range(layers):
        own = hidden_weights[l].astype(BF)
        hid_parts.append([own] + [from_peer(own, j) for j in range(1, mp)])
    for l in range(layers):
        own = mlp_weights[l].astype(BF)
        mlp_parts.append([own] + [from_peer(own, j) for j in range(1, mp)])
    bias_all = jnp.concatenate([gate_bias] + [from_peer(gate_bias, j) for j in range(1, mp)], axis=2)
    info = jnp.stack([lengths[0], me, jnp.int32(mp)]).astype(jnp.int32)

    def make_specs(order):
        def tile(cols):
            return pl.BlockSpec((tr, cols), lambda g: (order(g), 0))

        return tile

    def whole(*shape):
        return pl.BlockSpec(shape, lambda g: (0,) * len(shape), pipeline_mode=pl.Buffered(1))

    smem = pl.BlockSpec(memory_space=pltpu.SMEM)
    fwd = make_specs(lambda g: g)
    rev = make_specs(lambda g: grid - 1 - g)
    seg_fwd = pl.BlockSpec((SEG, ts, width), lambda g: (0, g, 0))
    seg_rev = pl.BlockSpec((SEG, ts, width), lambda g: (0, grid - 1 - g, 0))
    before_fwd = pl.BlockSpec((SEG, hid), lambda g: (jnp.maximum(g * ts - 1, 0), 0))
    before_rev = pl.BlockSpec((SEG, hid), lambda g: (jnp.maximum((grid - 1 - g) * ts - 1, 0), 0))
    gates_spec = pl.BlockSpec((3, width, part_h), lambda g: (0, 0, 0), pipeline_mode=pl.Buffered(1))
    wout_spec = pl.BlockSpec((1, width, part_h), lambda g: (3, 0, 0), pipeline_mode=pl.Buffered(1))
    mlp_spec = whole(2, width, part_f)
    gain_spec = whole(2, width)
    bias_spec = whole(2, hid)
    ends_spec = pl.BlockSpec((2, SEG, hid), lambda g: (0, 0, 0))
    fin_spec = pl.BlockSpec((2, hid), lambda g: (0, 0))
    sums_spec = pl.BlockSpec((SEG, width), lambda g: (0, 0))
    bsum_spec = pl.BlockSpec((2, SEG, hid), lambda g: (0, 0, 0))
    kbuf = pltpu.VMEM((3, tr, HC), F32)
    state = pltpu.VMEM((2, SEG, hid), F32)
    start = pltpu.VMEM((SEG, hid), F32)
    row_f32 = pltpu.VMEM((tr, width), F32)
    lanes = pltpu.VMEM((width // 128, tr, 128), F32)

    t_w = sds(tokens, width)
    t_wb = sds(tokens, width, dtype=BF)
    t_h = sds(tokens, hid)
    t_hb = sds(tokens, hid, dtype=BF)
    t_fb = sds(tokens, ff, dtype=BF)
    ends_s = sds(2, SEG, hid)
    fin_s = sds(2, hid)
    sums_s = sds(SEG, width)
    bsum_s = sds(2, SEG, hid)

    def cost(matmul_cols, elems):
        return pl.CostEstimate(
            flops=2 * tokens * width * matmul_cols,
            bytes_accessed=elems,
            transcendentals=0,
        )

    def chain(fin, send, shift, live):
        carry = send(fin)
        for _ in range(mp - 2):
            known = jnp.roll(carry[0:1] * live, shift, axis=1)
            carry = send(jnp.concatenate([fin[0:1] + fin[1:2] * known, fin[1:2]]))
        return carry

    def chain_forward(fin):
        return chain(fin, to_next, -part_h, (me > 0).astype(F32))

    def chain_backward(fin):
        return chain(fin, to_prev, part_h, (me < mp - 1).astype(F32))

    seg_in = inputs.reshape(SEG, steps, width)
    seg_cot = cotangent.reshape(SEG, steps, width)
    saved = []
    f1_out_specs = lambda t: [t(width), t(hid), t(hid), t(hid), t(hid), t(hid), t(hid), t(hid), ends_spec, fin_spec]
    f1_out_shapes = [t_wb, t_h, t_h, t_h, t_hb, t_hb, t_hb, t_hb, ends_s, fin_s]
    outs = pl.pallas_call(
        functools.partial(k_first, mp),
        grid=(grid,),
        in_specs=[seg_fwd, gain_spec, bias_spec] + [gates_spec] * mp,
        out_specs=[fwd(width)] + f1_out_specs(fwd),
        out_shape=[t_w] + f1_out_shapes,
        scratch_shapes=[kbuf, state, lanes],
        compiler_params=params(),
        cost_estimate=cost(3 * hid, 24 * 2**20),
        name="gates_first",
    )(seg_in, norm_gains[0], bias_all[0], *hid_parts[0])
    x, gate = outs[0], outs[1:]
    xs = [x]
    for l in range(layers - 1):
        nin, a, loc, prod, cand, wf, wi, q, ends, fin = gate
        inc = chain_forward(fin)
        outs = pl.pallas_call(
            functools.partial(k_middle, mp),
            grid=(grid,),
            in_specs=[smem, fin_spec, ends_spec, fwd(width), fwd(hid), fwd(hid), before_fwd, before_fwd]
            + [fwd(hid)] * 3
            + [gain_spec, gain_spec, bias_spec]
            + [wout_spec] * mp
            + [mlp_spec] * mp
            + [gates_spec] * mp,
            out_specs=[fwd(hid)] * 3 + [fwd(width)] * 2 + [fwd(ff)] * 2 + [fwd(width)] + f1_out_specs(fwd),
            out_shape=[t_hb] * 3 + [t_w, t_wb, t_fb, t_fb, t_w] + f1_out_shapes,
            scratch_shapes=[kbuf, state, start],
            compiler_params=params(),
            cost_estimate=cost(4 * hid + 2 * ff, 60 * 2**20),
            name="block_forward",
        )(
            info, inc, ends, xs[l], loc, prod, loc, prod, cand, wf, wi,
            norm_gains[l], norm_gains[l + 1], bias_all[l + 1],
            *hid_parts[l], *mlp_parts[l], *hid_parts[l + 1],
        )
        hlow, cf, ci, mid, nmid, act, slope, xn = outs[:8]
        saved.append((nin, a, q, hlow, cf, ci, mid, nmid, act, slope))
        xs.append(xn)
        gate = outs[8:]
    top = layers - 1
    nin, a, loc, prod, cand, wf, wi, q, ends, fin = gate
    inc = chain_forward(fin)
    outs = pl.pallas_call(
        functools.partial(k_turn, mp),
        grid=(grid,),
        in_specs=[smem, fin_spec, ends_spec, rev(width), rev(hid), rev(hid), before_rev, before_rev]
        + [rev(hid)] * 4
        + [gain_spec, seg_rev]
        + [wout_spec] * mp
        + [mlp_spec] * mp,
        out_specs=[rev(hid)] * 3
        + [rev(width), rev(ff), seg_rev, rev(width), rev(ff), rev(width), rev(width), rev(hid), rev(hid)]
        + [ends_spec, fin_spec, sums_spec],
        out_shape=[t_hb] * 3
        + [t_wb, t_fb, sds(SEG, steps, width), t_wb, t_fb, t_wb, t_w, t_h, t_h, ends_s, fin_s, sums_s],
        scratch_shapes=[kbuf, state, start, row_f32, pltpu.VMEM((tr, ff), BF), row_f32, row_f32, lanes],
        compiler_params=params(),
        cost_estimate=cost(2 * hid + 4 * ff, 60 * 2**20),
        name="block_turn",
    )(
        info, inc, ends, xs[top], loc, prod, loc, prod, cand, wf, wi, a, norm_gains[top], seg_cot,
        *hid_parts[top], *mlp_parts[top],
    )
    hlow, cf, ci, nmid, act, output, dz, dpre, dout, dx, lam, rprod, ends, fin, sums_mid = outs
    output = output.reshape(1, tokens, width)
    saved.append((nin, a, q, hlow, cf, ci, None, nmid, act, None))

    def weight_grads(pairs, lefts, rights, part, wide, block):
        count = len(pairs)
        per = wide // block
        in_specs = [pl.BlockSpec((tokens, width), lambda g: (0, 0), pipeline_mode=pl.Buffered(1)) for _ in lefts]
        in_specs += [pl.BlockSpec((tokens, block), lambda g: (0, part * per + g)) for _ in rights]
        return pl.pallas_call(
            functools.partial(k_grads, pairs),
            grid=(per,),
            in_specs=in_specs,
            out_specs=pl.BlockSpec((count, width, block), lambda g: (0, 0, g)),
            out_shape=sds(count, width, wide, dtype=BF),
            compiler_params=params(),
            cost_estimate=cost(count * wide, tokens * wide * count * 2),
            name="weight_grads",
        )(*lefts, *rights)

    def reduce_parts(pairs, lefts, rights, wide):
        block = min(256, wide)
        others = []
        for j in range(1, mp):
            sent = weight_grads(pairs, lefts, rights, j, wide, block)
            others.append(lax.ppermute(sent, "mp", [(m, (m + j) % mp) for m in range(mp)]))
        return weight_grads(pairs, lefts, rights, 0, wide, block), others

    dp_me = lax.axis_index("dp")
    who = jnp.concatenate([row_owner, dp_me[None].astype(jnp.int32)])
    count_value = step_count[0].astype(F32)
    fix_one = 1.0 - jnp.power(jnp.float32(BETA_ONE), count_value)
    fix_two = 1.0 - jnp.power(jnp.float32(BETA_TWO), count_value)
    fix = jnp.stack([1.0 / fix_one, 1.0 / fix_two])
    vmem = pl.BlockSpec(memory_space=pltpu.VMEM)
    hbm = pl.BlockSpec(memory_space=pl.ANY)

    def exchange(value, stage):
        low, count = stage
        return [
            lax.ppermute(value, "dp", [(i, i ^ (r << low)) for i in range(dp_count)])
            for r in range(1, 1 << count)
        ]

    def source_spec(plan, at, shape, tail):
        return pl.BlockSpec(shape, lambda g: tail(plan.local(at, g) // plan.pers[at], plan.local(at, g) % plan.pers[at]))

    def rotate(plan, l, grads, blocks):
        basis_spec = pl.BlockSpec((1, 1, width, width), lambda g: (l, plan.basis_at(g), 0, 0))
        specs, flat = [], []
        for at, one in enumerate(blocks):
            order = one.shape[-1]
            nb = plan.blocks[at] // order
            specs.append(source_spec(plan, at, (1, 1, nb, order, order), lambda k, c: (l, k, c, 0, 0)))
        for at, ones in enumerate(grads):
            for one in ones:
                specs.append(source_spec(plan, at, (1, width, plan.blocks[at]), lambda k, c: (k, 0, c)))
                flat.append(one)
        out_shapes = [
            sds(width // n, cols, dtype=BF) for n, cols in zip(plan.firsts, plan.cols) for _ in range(n)
        ]
        outs = pl.pallas_call(
            functools.partial(k_rotate, plan, mp),
            grid=(plan.begins[-1],),
            in_specs=[smem, basis_spec] + specs,
            out_specs=[pl.BlockSpec(o.shape, lambda g: (0, 0)) for o in out_shapes],
            out_shape=out_shapes,
            scratch_shapes=[pltpu.VMEM((width, cols), BF) for cols in plan.cols]
            + [pltpu.VMEM((width, max(plan.blocks)), BF)],
            compiler_params=params(),
            cost_estimate=cost(2 * sum(plan.cols), 16 * 2**20),
            name="rotate",
        )(who, left_bases, *blocks, *flat)
        pieces, at = [], 0
        for n in plan.firsts:
            pieces.append(outs[at : at + n])
            at += n
        return pieces

    def scatter_stage(plan, pieces, at):
        held = []
        for stages, mine in zip(plan.stages, pieces):
            low, count = stages[at]
            got = [
                lax.ppermute(mine[r], "dp", [(i, i ^ (r << low)) for i in range(dp_count)])
                for r in range(1, 1 << count)
            ]
            held.append([mine[0]] + got)
        return held

    def combine(plan, held, at):
        flat = [v for one in held for v in one]
        n_in = [len(one) for one in held]
        n_out = [1 << stages[at + 1][1] for stages in plan.stages]
        shapes = [
            sds(one[0].shape[0] // n, one[0].shape[1], dtype=BF) for one, n in zip(held, n_out) for _ in range(n)
        ]
        outs = pl.pallas_call(
            functools.partial(k_combine, n_in, n_out),
            in_specs=[vmem] * len(flat),
            out_specs=[vmem] * len(shapes),
            out_shape=shapes,
            compiler_params=pltpu.CompilerParams(vmem_limit_bytes=VMEM_LIMIT),
            cost_estimate=pl.CostEstimate(flops=0, bytes_accessed=6 * 2**20, transcendentals=0),
            name="combine",
        )(*flat)
        pieces, i = [], 0
        for n in n_out:
            pieces.append(outs[i : i + n])
            i += n
        return pieces

    def adam(plan, l, held, olds, splits, before):
        flat = [v for one in held for v in one]
        out_specs, shapes, in_specs, bufs = [], [], [], []
        for (_, count, wide), split in zip(plan.sources, splits):
            for lo, hi in ((0, count),) * 2 + split:
                out_specs.append(pl.BlockSpec((share, 1, hi - lo, wide), lambda g: (0, l, 0, 0)))
                shapes.append(sds(share, layers, hi - lo, wide))
            in_specs += [pl.BlockSpec((share, 1, count, wide), lambda g: (0, l, 0, 0))] * 2
            bufs.append(pltpu.VMEM((share, 1, count, wide), F32))
        n_state = len(shapes)
        before = before or ()
        outs = pl.pallas_call(
            functools.partial(k_adam, plan, splits, len(before)),
            grid=(1,),
            in_specs=[smem] + [vmem] * len(flat) + in_specs + [hbm] * len(before),
            out_specs=out_specs + [vmem] * len(plan.cols),
            out_shape=shapes + [sds(share, cols, dtype=BF) for cols in plan.cols],
            scratch_shapes=bufs,
            input_output_aliases={1 + len(flat) + len(olds) + i: i for i in range(len(before))},
            compiler_params=pltpu.CompilerParams(vmem_limit_bytes=VMEM_LIMIT),
            cost_estimate=pl.CostEstimate(flops=0, bytes_accessed=8 * 2**20, transcendentals=0),
            name="adam",
        )(fix, *flat, *olds, *before)
        return tuple(outs[:n_state]), outs[n_state:]

    def gather_moves(plan, moves):
        flat = []
        for stages, value in zip(plan.stages, moves):
            for stage in reversed(stages[1:]):
                value = jnp.concatenate([value] + exchange(value, stage), axis=0)
            flat += [value] + exchange(value, stages[0])
        return flat

    def apply_moves(plan, l, flat, blocks, weights, before):
        basis_spec = pl.BlockSpec((1, 1, width, width), lambda g: (l, plan.basis_at(g), 0, 0))
        block_specs, specs = [], []
        for at, one in enumerate(blocks):
            order = one.shape[-1]
            nb = plan.blocks[at] // order
            block_specs.append(source_spec(plan, at, (1, 1, nb, order, order), lambda k, c: (l, k, c, 0, 0)))
            specs.append(source_spec(plan, at, (1, 1, width, plan.blocks[at]), lambda k, c: (l, k, 0, c)))
        before = before or ()
        ins = 2 + 2 * len(blocks) + len(flat)
        return tuple(
            pl.pallas_call(
                functools.partial(k_apply, plan, len(before)),
                grid=(plan.begins[-1],),
                in_specs=[smem, basis_spec]
                + block_specs
                + specs
                + [whole(*v.shape) for v in flat]
                + [hbm] * len(before),
                out_specs=specs,
                out_shape=[sds(*w.shape) for w in weights],
                scratch_shapes=[pltpu.VMEM((width, cols), BF) for cols in plan.cols]
                + [pltpu.VMEM((width, max(plan.blocks)), BF)],
                input_output_aliases={ins + i: i for i in range(len(before))},
                compiler_params=params(),
                cost_estimate=cost(2 * sum(plan.cols), 24 * 2**20),
                name="apply_moves",
            )(who, left_bases, *blocks, *weights, *flat, *before)
        )

    plan = Plan(dp_count, width, ((4, 2, part_f), (0, 4, part_h)))
    olds = (mlp_first, mlp_second, hidden_first, hidden_second)
    splits = (((0, 2),), ((0, 2), (2, 4)))

    def finish(l, grads, before):
        state, new = before or (None, None)
        blocks = (mlp_blocks, hidden_blocks)
        pieces = rotate(plan, l, grads, blocks)
        stages = len(plan.stages[0])
        for at in range(stages - 1):
            pieces = combine(plan, scatter_stage(plan, pieces, at), at)
        held = scatter_stage(plan, pieces, stages - 1)
        state, moves = adam(plan, l, held, olds, splits, state)
        flat = gather_moves(plan, moves)
        return state, apply_moves(plan, l, flat, blocks, (mlp_weights, hidden_weights), new)

    def all_sum(value):
        step = 1
        while step < dp_count:
            value = value + lax.ppermute(value, "dp", [(i, i ^ step) for i in range(dp_count)])
            step *= 2
        return value

    done = None
    small = [None] * layers
    for l in reversed(range(layers)):
        nin, a, q, hlow, cf, ci, mid, nmid, act, slope = saved[l]
        inc = chain_backward(fin)
        mlp_own, mlp_others = reduce_parts(((0, 2), (1, 3)), (nmid, dz), (dpre, act), part_f)
        if l > 0:
            below = saved[l - 1]
            outs = pl.pallas_call(
                functools.partial(k_return, mp),
                grid=(grid,),
                in_specs=[smem, fin_spec, ends_spec]
                + [rev(hid)] * 5
                + [rev(width)] * 3
                + [rev(ff), rev(hid), gain_spec, gain_spec]
                + [gates_spec] * mp
                + [mlp_spec] * mp
                + [wout_spec] * mp,
                out_specs=[rev(hid)] * 3
                + [rev(width), rev(ff), rev(width), rev(width), rev(hid), rev(hid)]
                + [ends_spec, fin_spec, sums_spec, sums_spec, bsum_spec],
                out_shape=[t_hb] * 3
                + [t_wb, t_fb, t_wb, t_w, t_h, t_h, ends_s, fin_s, sums_s, sums_s, bsum_s],
                scratch_shapes=[kbuf, state, start, row_f32],
                compiler_params=params(),
                cost_estimate=cost(4 * hid + 2 * ff, 60 * 2**20),
                name="block_return",
            )(
                info, inc, ends, lam, rprod, cf, ci, q, xs[l], dx, below[6], below[9], below[1],
                norm_gains[l], norm_gains[l - 1],
                *hid_parts[l], *mlp_parts[l - 1], *hid_parts[l - 1],
            )
            dkf, dki, dkc, dz, dpre, dout_next, dx, lam, rprod, ends, fin, sums_in, sums_next, bsum = outs
        else:
            outs = pl.pallas_call(
                functools.partial(k_last, mp),
                grid=(grid,),
                in_specs=[smem, fin_spec, ends_spec]
                + [rev(hid)] * 5
                + [rev(width)] * 2
                + [gain_spec]
                + [gates_spec] * mp,
                out_specs=[rev(hid)] * 3 + [seg_rev, sums_spec, bsum_spec],
                out_shape=[t_hb] * 3 + [sds(SEG, steps, width), sums_s, bsum_s],
                scratch_shapes=[start, row_f32, row_f32, lanes],
                compiler_params=params(),
                cost_estimate=cost(3 * hid, 30 * 2**20),
                name="block_last",
            )(info, inc, ends, lam, rprod, cf, ci, q, xs[l], dx, norm_gains[l], *hid_parts[l])
            dkf, dki, dkc, input_grad, sums_in, bsum = outs
            dout_next, sums_next = None, None
        hid_own, hid_others = reduce_parts(
            ((0, 2), (0, 3), (0, 4), (1, 5)), (nin, dout), (dkf, dki, dkc, hlow), part_h
        )
        done = finish(l, ([mlp_own] + mlp_others, [hid_own] + hid_others), done)
        gains = jnp.stack([sums_in.sum(0), sums_mid.sum(0)])
        biases = bsum.sum(1)
        vector = jnp.concatenate([gains.reshape(-1), biases[:, :part_h].reshape(-1)])
        total = vector
        for j in range(1, mp):
            sent = jnp.concatenate([gains.reshape(-1), biases[:, j * part_h : (j + 1) * part_h].reshape(-1)])
            total = total + lax.ppermute(sent, "mp", [(m, (m + j) % mp) for m in range(mp)])
        total = all_sum(total.reshape(-1, 128)).reshape(-1)
        small[l] = (total[: 2 * width].reshape(2, width), total[2 * width :].reshape(2, part_h))
        dout, sums_mid = dout_next, sums_next
    input_grad = input_grad.reshape(1, tokens, width)
    state, (mlp_new, hidden_new) = done
    mlp_grad, mlp_first_new, mlp_second_new = state[:3]
    hidden_grad, hidden_first_new, gate_second_new, hidden_second_new = state[3:]
    gain_grad = jnp.stack([small[l][0] for l in range(layers)])
    bias_grad = jnp.stack([small[l][1] for l in range(layers)])
    gain_first_new, gain_second_new, gain_moves = adam_moments(
        gain_grad, gain_first, gain_second, fix_one, fix_two
    )
    bias_first_new, bias_second_new, bias_moves = adam_moments(
        bias_grad, bias_first, bias_second, fix_one, fix_two
    )
    gain_new = norm_gains - GAIN_RATE * gain_moves
    bias_new = gate_bias - BIAS_RATE * bias_moves
    return (
        output,
        input_grad,
        hidden_grad,
        hidden_first_new,
        hidden_second_new,
        gate_second_new,
        hidden_new,
        mlp_grad,
        mlp_first_new,
        mlp_second_new,
        mlp_new,
        gain_grad,
        gain_first_new,
        gain_second_new,
        gain_new,
        bias_grad,
        bias_first_new,
        bias_second_new,
        bias_new,
    )


def solution(mesh):
    in_specs = (
        P("dp", "mp", None),
        P("dp", "mp", None),
        P("dp"),
        P(None, None, None, "mp"),
        P(None, None, None, "mp"),
        P(),
        P(None, None, "mp"),
        P(),
        P(None, None, "mp", None, None),
        P(None, None, "mp", None, None),
        P("dp", None, None, "mp"),
        P("dp", None, None, "mp"),
        P("dp", None, None, "mp"),
        P("dp", None, None, "mp"),
        P(),
        P(),
        P(None, None, "mp"),
        P(None, None, "mp"),
        P(),
        P(),
    )
    out_specs = (
        P("dp", "mp", None),
        P("dp", "mp", None),
        P("dp", None, None, "mp"),
        P("dp", None, None, "mp"),
        P("dp", None, None, "mp"),
        P("dp", None, None, "mp"),
        P(None, None, None, "mp"),
        P("dp", None, None, "mp"),
        P("dp", None, None, "mp"),
        P("dp", None, None, "mp"),
        P(None, None, None, "mp"),
        P(),
        P(),
        P(),
        P(),
        P(None, None, "mp"),
        P(None, None, "mp"),
        P(None, None, "mp"),
        P(None, None, "mp"),
    )
    return jax.shard_map(
        per_device, mesh=mesh, in_specs=in_specs, out_specs=out_specs, check_vma=False
    )
```

```python
import functools
import jax
import jax.numpy as jnp
from jax import lax
from jax.experimental import pallas as pl
from jax.experimental.pallas import tpu as pltpu
from jax.sharding import PartitionSpec as P

NORM_EPS = 1e-05
BETA_ONE = 0.9
BETA_TWO = 0.95
ADAM_EPS = 1e-08
MATRIX_RATE = 0.08
GAIN_RATE = 0.5
BIAS_RATE = 4.0
DECAY_RATE = 0.01
BF = jnp.bfloat16
F32 = jnp.float32
SEG = 8
TILE_STEPS = 32
HC = 512
VMEM_LIMIT = 58 * 1024 * 1024
LOG2E = 1.4426950408889634


def dot_nn(a, b):
    return lax.dot_general(a, b, (((1,), (0,)), ((), ())), preferred_element_type=F32)


def dot_nt(a, b):
    return lax.dot_general(a, b, (((1,), (1,)), ((), ())), preferred_element_type=F32)


def dot_tn(a, b):
    return lax.dot_general(a, b, (((0,), (0,)), ((), ())), preferred_element_type=F32)


def recip(x):
    r = pl.reciprocal(x, approx=True)
    return r * (2.0 - x * r)


def row_blocks(count, size):
    return [slice(at, at + size) for at in range(0, count, size)]


def row_scale(values):
    return lax.rsqrt(jnp.mean(values * values, axis=-1, keepdims=True) + NORM_EPS)


def norm_stage(x_ref, gain, out_ref):
    for r in row_blocks(x_ref.shape[0], 32):
        x = x_ref[r, :]
        out_ref[r, :] = (x * row_scale(x) * gain).astype(BF)


def column_chunks(parts, wide):
    step = min(HC, wide)
    return [(j, c0, j * wide + c0, step) for j in range(parts) for c0 in range(0, wide, step)]


def gate_stage(nin_ref, bias_ref, w_refs, kbuf, state, outs):
    take_ref, loc_ref, prod_ref, cand_ref, wf_ref, wi_ref, q_ref = outs
    for turn, (j, c0, at, wide) in enumerate(column_chunks(len(w_refs), w_refs[0].shape[2])):
        slot = turn % 2
        for k in range(3):
            kbuf[slot, k, :, :wide] = dot_nn(nin_ref[...], w_refs[j][k, :, c0 : c0 + wide])
        cols = slice(at, at + wide)
        bias_f, bias_i = bias_ref[0:1, cols], bias_ref[1:2, cols]
        loc, prod = state[0, :, cols], state[1, :, cols]
        for r in row_blocks(nin_ref.shape[0], 16):
            kf = kbuf[slot, 0, r, :wide] + bias_f
            ki = kbuf[slot, 1, r, :wide] + bias_i
            kc = kbuf[slot, 2, r, :wide]
            tf = jnp.exp(-jnp.abs(kf))
            ti = jnp.exp(-jnp.abs(ki))
            tc = jnp.exp(-jnp.abs(kc))
            gap = jnp.minimum(ki, 0.0) - jnp.minimum(kf, 0.0)
            e = jnp.exp(-jnp.abs(gap))
            ef = jnp.where(gap < 0, e, 1.0)
            ei = jnp.where(gap > 0, e, 1.0)
            nf, ni = ef + ef * tf, ei + ei * ti
            inv = recip(nf + ni)
            keep = ni * inv
            take = nf * inv
            sf = ef * jnp.where(kf >= 0, tf, 1.0)
            si = ei * jnp.where(ki >= 0, ti, 1.0)
            sc = tc * recip(1.0 + tc)
            up = kc >= 0
            cand = jnp.where(up, kc + 0.5, sc)
            slope = jnp.where(up, 1.0, sc - sc * sc)
            take_ref[r, cols] = take.astype(BF)
            cand_ref[r, cols] = cand.astype(BF)
            wf_ref[r, cols] = (keep * inv * sf).astype(BF)
            wi_ref[r, cols] = (take * inv * si).astype(BF)
            q_ref[r, cols] = (take * slope).astype(BF)
            drive = take * cand
            loc0 = keep[:8] * loc + drive[:8]
            prod0 = keep[:8] * prod
            loc = keep[8:] * loc0 + drive[8:]
            prod = keep[8:] * prod0
            loc_ref[r, cols] = jnp.concatenate([loc0, loc]).astype(BF)
            prod_ref[r, cols] = jnp.concatenate([prod0, prod]).astype(BF)
        state[0, :, cols] = loc
        state[1, :, cols] = prod


def fold(state, ends_ref, fin_ref, part, backward):
    hidden = state.shape[2]
    ends_ref[...] = state[...]
    order = list(reversed(range(SEG))) if backward else list(range(SEG))
    value = state[0, order[0] : order[0] + 1, :]
    prod = state[1, order[0] : order[0] + 1, :]
    for s in order[1:]:
        value = state[0, s : s + 1, :] + state[1, s : s + 1, :] * value
        prod = state[1, s : s + 1, :] * prod
    n = hidden // part
    for j in range(n):
        at = ((j - 1) % n if backward else (j + 1) % n) * part
        fin_ref[0:1, j * part : (j + 1) * part] = value[:, at : at + part]
        fin_ref[1:2, j * part : (j + 1) * part] = prod[:, at : at + part]


def carry_forward(inc_ref, ends_ref, start, live):
    start[0:1, :] = inc_ref[0:1, :] * live
    for s in range(SEG - 1):
        start[s + 1 : s + 2, :] = (
            ends_ref[0, s : s + 1, :] + ends_ref[1, s : s + 1, :] * start[s : s + 1, :]
        )


def carry_backward(inc_ref, ends_ref, start, live):
    start[SEG - 1 : SEG, :] = inc_ref[0:1, :] * live
    for s in reversed(range(1, SEG)):
        start[s - 1 : s, :] = (
            ends_ref[0, s : s + 1, :] + ends_ref[1, s : s + 1, :] * start[s : s + 1, :]
        )


def state_stage(start, loc_ref, prod_ref, hlow_ref):
    rows, hidden = loc_ref.shape
    for _, _, at, wide in column_chunks(1, hidden):
        cols = slice(at, at + wide)
        c = jnp.concatenate([start[:, cols], start[:, cols]])
        for r in row_blocks(rows, 16):
            hlow_ref[r, cols] = (loc_ref[r, cols].astype(F32) + prod_ref[r, cols].astype(F32) * c).astype(BF)


def mlp_stage(x_ref, hlow_ref, w_refs, m_refs, gain, kbuf, mid_ref, nmid_ref, act_ref, slope_ref):
    part = w_refs[0].shape[2]
    total = x_ref[...]
    for j, w in enumerate(w_refs):
        total = total + dot_nt(hlow_ref[:, j * part : (j + 1) * part], w[0])
    mid_ref[...] = total
    norm_stage(mid_ref, gain, nmid_ref)
    wide = m_refs[0].shape[2]
    total = mid_ref[...]
    for turn, (j, c0, at, step) in enumerate(column_chunks(len(m_refs), wide)):
        slot = turn % 2
        kbuf[slot, 0, :, :step] = dot_nn(nmid_ref[...], m_refs[j][0, :, c0 : c0 + step])
        cols = slice(at, at + step)
        acts = []
        for r in row_blocks(x_ref.shape[0], 16):
            pre = kbuf[slot, 0, r, :step]
            t = recip(1.0 + jnp.abs(pre) * (0.3275911 * 0.7071067811865476))
            bell = jnp.exp(pre * pre * -0.5)
            poly = (
                (((0.5307027145 * t - 0.7265760135) * t + 0.7107068705) * t - 0.142248368) * t
                + 0.127414796
            ) * t
            tail = poly * bell
            cdf = jnp.where(pre >= 0, 1.0 - tail, tail)
            acts.append((pre * cdf).astype(BF))
            slope_ref[r, cols] = (cdf + pre * (bell * 0.3989422804014327)).astype(BF)
        acts = jnp.concatenate(acts)
        act_ref[:, cols] = acts
        total = total + dot_nt(acts, m_refs[j][1, :, c0 : c0 + step])
    return total


def norm_back_stage(src_ref, gain, dn_ref, dx_ref, sums_ref, low_ref):
    sums = sums_ref[...]
    for r in row_blocks(src_ref.shape[0], 32):
        x = src_ref[r, :]
        scale = row_scale(x)
        unit = x * scale
        d = dn_ref[r, :]
        e = d * gain
        dx = dx_ref[r, :] + scale * (e - unit * jnp.mean(e * unit, axis=-1, keepdims=True))
        dx_ref[r, :] = dx
        if low_ref is not None:
            low_ref[r, :] = dx.astype(BF)
        g = d * unit
        sums = sums + ((g[:8] + g[8:16]) + (g[16:24] + g[24:]))
    sums_ref[...] = sums


def mlp_back_stage(dx_ref, slope_ref, mid_ref, m_refs, gain, dn_ref, dz_ref, dpre_ref, dout_ref, sums_ref):
    dz_ref[...] = dx_ref[...].astype(BF)
    wide = m_refs[0].shape[2]
    for j, c0, at, step in column_chunks(len(m_refs), wide):
        cols = slice(at, at + step)
        dact = dot_nn(dz_ref[...], m_refs[j][1, :, c0 : c0 + step])
        dpre_ref[:, cols] = (dact * slope_ref[:, cols].astype(F32)).astype(BF)
    total = None
    for j, m in enumerate(m_refs):
        term = dot_nt(dpre_ref[:, j * wide : (j + 1) * wide], m[0])
        total = term if total is None else total + term
    dn_ref[...] = total
    norm_back_stage(mid_ref, gain, dn_ref, dx_ref, sums_ref, dout_ref)


def adjoint_stage(dout_ref, w_refs, take_ref, kbuf, state, lam_ref, prod_ref):
    for turn, (j, c0, at, wide) in enumerate(column_chunks(len(w_refs), w_refs[0].shape[2])):
        slot = turn % 2
        kbuf[slot, 0, :, :wide] = dot_nn(dout_ref[...], w_refs[j][0, :, c0 : c0 + wide])
        cols = slice(at, at + wide)
        mu, prod = state[0, :, cols], state[1, :, cols]
        for r in reversed(row_blocks(dout_ref.shape[0], 16)):
            u = kbuf[slot, 0, r, :wide]
            keep = 1.0 - take_ref[r, cols].astype(F32)
            lam1 = u[8:] + mu
            lam0 = u[:8] + keep[8:] * lam1
            mu = keep[:8] * lam0
            prod0 = prod * keep[8:]
            lam_ref[r, cols] = jnp.concatenate([lam0, lam1]).astype(BF)
            prod_ref[r, cols] = jnp.concatenate([prod0, prod]).astype(BF)
            prod = prod0 * keep[:8]
        state[0, :, cols] = mu
        state[1, :, cols] = prod


def keys_stage(first, mu_in, h_in, ins, dk_refs, bias_ref):
    lam_ref, prod_ref, hlow_ref, hbefore_ref, cand_ref, wf_ref, wi_ref, q_ref = ins
    dkf_ref, dki_ref, dkc_ref = dk_refs
    rows, hidden = lam_ref.shape
    for _, _, at, wide in column_chunks(1, hidden):
        cols = slice(at, at + wide)
        c = jnp.concatenate([mu_in[:, cols], mu_in[:, cols]])
        before = jnp.where(first, h_in[:, cols], hbefore_ref[:, cols].astype(F32)[8:])
        sum_f, sum_i = bias_ref[0, :, cols], bias_ref[1, :, cols]
        for r in row_blocks(rows, 16):
            lam = lam_ref[r, cols].astype(F32) + prod_ref[r, cols].astype(F32) * c
            h = hlow_ref[r, cols].astype(F32)
            diff = lam * (cand_ref[r, cols].astype(F32) - jnp.concatenate([before, h[:8]]))
            before = h[8:]
            df = (-(diff * wf_ref[r, cols].astype(F32))).astype(BF)
            di = (diff * wi_ref[r, cols].astype(F32)).astype(BF)
            dkf_ref[r, cols] = df
            dki_ref[r, cols] = di
            dkc_ref[r, cols] = (lam * q_ref[r, cols].astype(F32)).astype(BF)
            df, di = df.astype(F32), di.astype(F32)
            sum_f = sum_f + (df[:8] + df[8:])
            sum_i = sum_i + (di[:8] + di[8:])
        bias_ref[0, :, cols] = sum_f
        bias_ref[1, :, cols] = sum_i


def keys_back_stage(dk_refs, w_refs, dn_ref):
    part = w_refs[0].shape[2]
    total = None
    for j, w in enumerate(w_refs):
        for k in range(3):
            term = dot_nt(dk_refs[k][:, j * part : (j + 1) * part], w[k])
            total = term if total is None else total + term
    dn_ref[...] = total


def spread(src_ref, dst, lanes):
    steps = src_ref.shape[1]
    for c in range(lanes.shape[0]):
        cols = slice(c * 128, c * 128 + 128)
        for s in range(SEG):
            lanes[c, pl.ds(s, steps, stride=SEG), :] = src_ref[s, :, cols].astype(F32)
        dst[:, cols] = lanes[c]


def gather_out(src, dst_ref, lanes):
    steps = dst_ref.shape[1]
    for c in range(lanes.shape[0]):
        cols = slice(c * 128, c * 128 + 128)
        lanes[c] = src[:, cols]
        for s in range(SEG):
            dst_ref[s, :, cols] = lanes[c, pl.ds(s, steps, stride=SEG), :]


def reset(state):
    state[0] = jnp.zeros_like(state[0])
    state[1] = jnp.ones_like(state[1])


def k_cast(*refs):
    half = len(refs) // 2
    for src, dst in zip(refs[:half], refs[half:]):
        dst[...] = src[0].astype(BF)


def k_first(n_parts, in_ref, gain_ref, bias_ref, *refs):
    w = refs[:n_parts]
    xp, nin = refs[n_parts : n_parts + 2]
    gates = refs[n_parts + 2 : n_parts + 9]
    ends, fin, kbuf, state, lanes = refs[n_parts + 9 :]
    g = pl.program_id(0)

    @pl.when(g == 0)
    def _():
        reset(state)

    spread(in_ref, xp, lanes)
    norm_stage(xp, gain_ref[0:1, :], nin)
    gate_stage(nin, bias_ref, w, kbuf, state, gates)

    @pl.when(g == pl.num_programs(0) - 1)
    def _():
        fold(state, ends, fin, w[0].shape[2], False)


def k_middle(n_parts, info, inc, ends_in, x, loc, prod, gain, gain_next, bias, *refs):
    wo = refs[:n_parts]
    m = refs[n_parts : 2 * n_parts]
    w = refs[2 * n_parts : 3 * n_parts]
    hlow, start, mid, nmid, act, slope, xn, nin = refs[3 * n_parts : 3 * n_parts + 8]
    gates = refs[3 * n_parts + 8 : 3 * n_parts + 15]
    ends, fin, kbuf, state = refs[3 * n_parts + 15 :]
    g = pl.program_id(0)

    @pl.when(g == 0)
    def _():
        reset(state)
        carry_forward(inc, ends_in, start, (info[1] > 0).astype(F32))

    state_stage(start, loc, prod, hlow)
    xn[...] = mlp_stage(x, hlow, wo, m, gain[1:2, :], kbuf, mid, nmid, act, slope)
    norm_stage(xn, gain_next[0:1, :], nin)
    gate_stage(nin, bias, w, kbuf, state, gates)

    @pl.when(g == pl.num_programs(0) - 1)
    def _():
        fold(state, ends, fin, w[0].shape[2], False)


def k_turn(n_parts, info, inc, ends_in, x, loc, prod, take, gain, cot, *refs):
    wo = refs[:n_parts]
    m = refs[n_parts : 2 * n_parts]
    (hlow, start, nmid, act, out, dz, dpre, dout, dx, lam, prod_o, ends, fin, sums) = refs[
        2 * n_parts : 2 * n_parts + 14
    ]
    kbuf, state, mid, slope, dn, lanes, out_lanes = refs[2 * n_parts + 14 :]
    g = pl.program_id(0)
    tile = pl.num_programs(0) - 1 - g
    rows = x.shape[0]
    steps_all = pl.num_programs(0) * (rows // SEG)

    @pl.when(g == 0)
    def _():
        reset(state)
        sums[...] = jnp.zeros_like(sums)
        carry_forward(inc, ends_in, start, (info[1] > 0).astype(F32))

    state_stage(start, loc, prod, hlow)
    top = mlp_stage(x, hlow, wo, m, gain[1:2, :], kbuf, mid, nmid, act, slope)
    at = lax.broadcasted_iota(jnp.int32, (rows, 1), 0)
    place = info[1] * (SEG * steps_all) + (at % SEG) * steps_all + tile * (rows // SEG) + at // SEG
    mask = (place < info[0]).astype(F32)
    gather_out(top * mask, out, out_lanes)

    @pl.when(g >= 0)
    def _():
        spread(cot, dx, lanes)
        dx[...] = dx[...] * mask
        mlp_back_stage(dx, slope, mid, m, gain[1:2, :], dn, dz, dpre, dout, sums)
        adjoint_stage(dout, wo, take, kbuf, state, lam, prod_o)

    @pl.when(g == pl.num_programs(0) - 1)
    def _():
        fold(state, ends, fin, wo[0].shape[2], True)


def k_return(n_parts, info, inc, ends_in, h_in, *refs):
    keys = refs[:8]
    x, dx_in, mid, slope, take, gain, gain_prev = refs[8:15]
    refs = refs[15:]
    w = refs[:n_parts]
    m = refs[n_parts : 2 * n_parts]
    wo = refs[2 * n_parts : 3 * n_parts]
    (dkf, dki, dkc, dz, dpre, dout, dx, lam_o, prod_o, ends, fin, sums_in, sums_mid, bias) = refs[
        3 * n_parts : 3 * n_parts + 14
    ]
    kbuf, state, start, dn = refs[3 * n_parts + 14 :]
    g = pl.program_id(0)
    last = pl.num_programs(0) - 1

    @pl.when(g == 0)
    def _():
        reset(state)
        sums_in[...] = jnp.zeros_like(sums_in)
        sums_mid[...] = jnp.zeros_like(sums_mid)
        bias[...] = jnp.zeros_like(bias)
        carry_backward(inc, ends_in, start, (info[1] < info[2] - 1).astype(F32))

    keys_stage(g == last, start, h_in, keys, (dkf, dki, dkc), bias)
    keys_back_stage((dkf, dki, dkc), w, dn)
    dx[...] = dx_in[...]
    norm_back_stage(x, gain[0:1, :], dn, dx, sums_in, None)
    mlp_back_stage(dx, slope, mid, m, gain_prev[1:2, :], dn, dz, dpre, dout, sums_mid)
    adjoint_stage(dout, wo, take, kbuf, state, lam_o, prod_o)

    @pl.when(g == last)
    def _():
        fold(state, ends, fin, wo[0].shape[2], True)


def k_last(n_parts, n_after, *refs):
    info, inc, ends_in, h_in = refs[n_after : n_after + 4]
    refs = refs[n_after + 4 :]
    keys = refs[:8]
    x, dx_in, gain = refs[8:11]
    w = refs[11 : 11 + n_parts]
    dkf, dki, dkc, out, sums_in, bias = refs[11 + n_parts : 17 + n_parts]
    start, dn, dx, lanes = refs[17 + n_parts :]
    g = pl.program_id(0)
    last = pl.num_programs(0) - 1

    @pl.when(g == 0)
    def _():
        sums_in[...] = jnp.zeros_like(sums_in)
        bias[...] = jnp.zeros_like(bias)
        carry_backward(inc, ends_in, start, (info[1] < info[2] - 1).astype(F32))

    keys_stage(g == last, start, h_in, keys, (dkf, dki, dkc), bias)
    keys_back_stage((dkf, dki, dkc), w, dn)
    dx[...] = dx_in[...]
    norm_back_stage(x, gain[0:1, :], dn, dx, sums_in, None)
    gather_out(dx, out, lanes)


def k_grads(pairs, n_after, *refs):
    refs = refs[n_after:]
    out = refs[-1]
    for k, (left, right) in enumerate(pairs):
        out[k] = dot_tn(refs[left][...], refs[right][...]).astype(BF)


def place_of(owner, me, stages):
    if stages is None:
        return owner
    relative = owner ^ me
    place = None
    for low, count in stages:
        digit = (relative >> low) & ((1 << count) - 1)
        place = digit if place is None else (place << count) + digit
    return place


def turn_blocks(value, blocks, inverse):
    order = blocks.shape[-1]
    dot = dot_nt if inverse else dot_nn
    return jnp.concatenate(
        [
            dot(value[:, b * order : (b + 1) * order], blocks[0, 0, b].astype(BF))
            for b in range(blocks.shape[2])
        ],
        axis=1,
    )


def k_rotate(plan, n_recv, pairs, n_after, who, basis, *refs):
    refs = refs[n_after:]
    n_src = len(plan.sources)
    n_left, n_right = 1 + max(p[0] for p in pairs), len(pairs)
    blocks = refs[:n_src]
    recv = refs[n_src : n_src * (1 + n_recv)]
    refs = refs[n_src * (1 + n_recv) :]
    lefts, rights = refs[:n_left], refs[n_left : n_left + n_right]
    refs = refs[n_left + n_right :]
    n_out = sum(plan.firsts)
    outs, bufs = refs[:n_out], refs[n_out:]
    g = pl.program_id(0)
    share = plan.share
    width = basis.shape[2]
    count = width // share
    for chunk, runs in enumerate(plan.runs):
        at, pair = plan.source_of[chunk], pairs[plan.matrix_of[chunk]]

        @pl.when(g == chunk)
        def _(runs=runs, at=at, pair=pair):
            total = dot_tn(lefts[pair[0]][...], rights[pair[1]][...])
            for ref in recv[at * n_recv : (at + 1) * n_recv]:
                total = total + ref[0].astype(F32)
            turned = turn_blocks(total.astype(BF), blocks[at], False).astype(BF)
            done = dot_tn(basis[0, 0].astype(BF), turned).astype(BF)
            for b in range(count):
                for stream, src, dst, wide in runs:
                    row = place_of(who[b], who[count], plan.stages[stream]) * share
                    bufs[stream][pl.ds(pl.multiple_of(row, share), share), dst : dst + wide] = done[
                        b * share : (b + 1) * share, src : src + wide
                    ]

    @pl.when(g == pl.num_programs(0) - 1)
    def _():
        at = 0
        for stream, pieces in enumerate(plan.firsts):
            rows = width // pieces
            for r in range(pieces):
                outs[at][...] = bufs[stream][r * rows : (r + 1) * rows, :]
                at += 1


def sum_pieces(refs):
    total = refs[0][...].astype(F32)
    for ref in refs[1:]:
        total = total + ref[...].astype(F32)
    return total


def k_combine(n_in, n_out, n_after, n_small, *refs):
    refs = refs[n_after:]
    if n_small:
        at = sum(n_in)
        refs[-1][...] = refs[at][...] + refs[at + 1][...]
        refs = refs[:at] + refs[at + 2 : -1]
    i, o = 0, sum(n_in)
    for take, give in zip(n_in, n_out):
        total = sum_pieces(refs[i : i + take]).astype(BF)
        rows = total.shape[0] // give
        for r in range(give):
            refs[o + r][...] = total[r * rows : (r + 1) * rows, :]
        i += take
        o += give


def k_join(n_in, n_after, *refs):
    refs = refs[n_after:]
    outs = refs[sum(n_in) :]
    i = 0
    for out, take in zip(outs, n_in):
        rows = refs[i].shape[0]
        for r in range(take):
            out[r * rows : (r + 1) * rows, :] = refs[i + r][...]
        i += take


def k_adam(plan, spread_plan, splits, n_alias, fix, *refs):
    n_in = sum(plan.lasts)
    n_src = len(plan.sources)
    pieces = refs[:n_in]
    olds = refs[n_in : n_in + 2 * n_src]
    outs = refs[n_in + 2 * n_src + n_alias :]
    bufs = refs[len(refs) - n_src :]
    moves_o = outs[sum(2 + len(split) for split in splits) :][: len(spread_plan.stages)]
    sums, i = [], 0
    for take in plan.lasts:
        sums.append(sum_pieces(pieces[i : i + take]))
        i += take
    o = 0
    for at, split in enumerate(splits):
        grad_o, first_o = outs[o : o + 2]
        second_o = outs[o + 2 : o + 2 + len(split)]
        o += 2 + len(split)
        first, second = olds[2 * at : 2 * at + 2]
        for chunk in range(plan.begins[at], plan.begins[at + 1]):
            kind, base = plan.where(at, chunk)
            for stream, src, dst, wide in plan.runs[chunk]:
                grad_o[:, 0, kind, base + src : base + src + wide] = sums[stream][:, dst : dst + wide]
        grad = grad_o[...]
        one = BETA_ONE * first[...] + (1.0 - BETA_ONE) * grad
        two = BETA_TWO * second[...] + (1.0 - BETA_TWO) * grad * grad
        first_o[...] = one
        for ref, (lo, hi) in zip(second_o, split):
            ref[...] = two[:, :, lo:hi, :]
        bufs[at][...] = one * fix[0] / (jnp.sqrt(two * fix[1]) + ADAM_EPS)
        for chunk in range(plan.begins[at], plan.begins[at + 1]):
            kind, base = plan.where(at, chunk)
            for stream, src, dst, wide in spread_plan.runs[chunk]:
                moves_o[stream][:, dst : dst + wide] = bufs[at][
                    :, 0, kind, base + src : base + src + wide
                ].astype(BF)


def k_apply(plan, n_alias, who, basis, *refs):
    n_src = len(plan.sources)
    n_in = sum(plan.firsts)
    blocks = refs[:n_src]
    weights = refs[n_src : 2 * n_src]
    pieces = refs[2 * n_src : 2 * n_src + n_in]
    outs = refs[2 * n_src + n_in + n_alias :][:n_src]
    bufs = refs[2 * n_src + n_in + n_alias + n_src : -1]
    moves = refs[-1]
    g = pl.program_id(0)
    share = plan.share
    width = basis.shape[2]
    count = width // share

    @pl.when(g == 0)
    def _():
        at = 0
        for stream, n in enumerate(plan.firsts):
            rows = width // n
            for r in range(n):
                bufs[stream][r * rows : (r + 1) * rows, :] = pieces[at][...]
                at += 1

    for chunk, runs in enumerate(plan.runs):

        @pl.when(g == chunk)
        def _(runs=runs):
            for stream, src, dst, wide in runs:
                for b in range(count):
                    at = place_of(who[b], who[count], plan.stages[stream]) * share
                    moves[b * share : (b + 1) * share, src : src + wide] = bufs[stream][
                        pl.ds(pl.multiple_of(at, share), share), dst : dst + wide
                    ]

    for at in range(n_src):

        @pl.when((g >= plan.begins[at]) & (g < plan.begins[at + 1]))
        def _(at=at):
            wide = plan.blocks[at]
            back = dot_nn(basis[0, 0].astype(BF), moves[:, :wide]).astype(BF)
            step = turn_blocks(back, blocks[at], True)
            old = weights[at][0, 0]
            outs[at][0, 0] = old - MATRIX_RATE * (step + DECAY_RATE * old)


class Plan:
    def __init__(self, dp_count, width, sources, staged=True):
        bits = dp_count.bit_length() - 1
        x, y, z, rest = (0, 1), (1, 1), (2, 1), (3, bits - 3)
        orders = [[x, y, z, rest], [y, x, z, rest], [z, rest, x, y]]
        self.share = width // dp_count
        self.sources = sources
        self.blocks = [min(512, wide) for _, _, wide in sources]
        self.pers = [wide // block for (_, _, wide), block in zip(sources, self.blocks)]
        self.begins = [0]
        for (_, count, _), per in zip(sources, self.pers):
            self.begins.append(self.begins[-1] + count * per)
        self.source_of, self.matrix_of = [], []
        matrices = 0
        for at, (_, count, _) in enumerate(sources):
            for k in range(count):
                self.source_of += [at] * self.pers[at]
                self.matrix_of += [matrices + k] * self.pers[at]
            matrices += count
        named = []
        for at, block in enumerate(self.blocks):
            for chunk in range(self.begins[at], self.begins[at + 1]):
                named.append([0 if not staged else 2 if lane == 3 else chunk % 2 for lane in range(block // 128)])
        used = sorted({stream for row in named for stream in row})
        self.stages = [orders[stream] if staged else None for stream in used]
        self.cols = [0] * len(used)
        self.runs = []
        for row in named:
            runs = []
            for lane, stream in enumerate(row):
                at = used.index(stream)
                if runs and runs[-1][0] == at:
                    runs[-1][3] += 128
                else:
                    runs.append([at, lane * 128, self.cols[at], 128])
                self.cols[at] += 128
            self.runs.append(runs)
        self.firsts = [1 << stages[0][1] if staged else 1 for stages in self.stages]
        self.lasts = [1 << stages[-1][1] if staged else 1 for stages in self.stages]

    def where(self, at, chunk):
        local = chunk - self.begins[at]
        return local // self.pers[at], local % self.pers[at] * self.blocks[at]

    def local(self, at, g):
        return jnp.clip(g - self.begins[at], 0, self.begins[at + 1] - self.begins[at] - 1)

    def basis_at(self, g):
        index = None
        for at, (base, _, _) in enumerate(self.sources):
            here = base + self.local(at, g) // self.pers[at]
            index = here if index is None else jnp.where(g < self.begins[at], index, here)
        return index


def k_small(*refs):
    gains, biases = refs[-2:]
    for l in range(gains.shape[0]):
        sums_in, sums_mid, bias = refs[3 * l : 3 * l + 3]
        gains[l, 0:1, :] = jnp.sum(sums_in[...], axis=0, keepdims=True)
        gains[l, 1:2, :] = jnp.sum(sums_mid[...], axis=0, keepdims=True)
        for k in range(2):
            biases[l, k : k + 1, :] = jnp.sum(bias[k], axis=0, keepdims=True)


def adam_moments(grads, first, second, fix_one, fix_two):
    first = BETA_ONE * first + (1.0 - BETA_ONE) * grads
    second = BETA_TWO * second + (1.0 - BETA_TWO) * grads * grads
    moves = first / fix_one / (jnp.sqrt(second / fix_two) + ADAM_EPS)
    return (first, second, moves)


def params(parallel=False):
    return pltpu.CompilerParams(
        dimension_semantics=("arbitrary",), vmem_limit_bytes=VMEM_LIMIT
    )


def sds(*shape, dtype=F32):
    return jax.ShapeDtypeStruct(shape, dtype)


def per_device(
    inputs,
    cotangent,
    lengths,
    hidden_weights,
    mlp_weights,
    norm_gains,
    gate_bias,
    left_bases,
    hidden_blocks,
    mlp_blocks,
    hidden_first,
    hidden_second,
    mlp_first,
    mlp_second,
    gain_first,
    gain_second,
    bias_first,
    bias_second,
    step_count,
    row_owner,
):
    dp_count = lax.axis_size("dp")
    mp = lax.axis_size("mp")
    me = lax.axis_index("mp")
    tokens = inputs.shape[1]
    width = inputs.shape[2]
    part_h = hidden_weights.shape[3]
    part_f = mlp_weights.shape[3]
    hid = part_h * mp
    ff = part_f * mp
    layers = hidden_weights.shape[0]
    steps = tokens // SEG
    ts = min(TILE_STEPS, steps)
    tr = ts * SEG
    grid = steps // ts
    share = width // dp_count

    def from_peer(value, j):
        return lax.ppermute(value, "mp", [((m + j) % mp, m) for m in range(mp)])

    def to_next(value):
        return lax.ppermute(value, "mp", [(m, (m + 1) % mp) for m in range(mp)])

    def to_prev(value):
        return lax.ppermute(value, "mp", [((m + 1) % mp, m) for m in range(mp)])

    def cast(picks):
        in_specs, out_specs, shapes = [], [], []
        for weights, l in picks:
            _, count, _, wide = weights.shape
            per = 4 // count
            in_specs.append(
                pl.BlockSpec((1, 1, width, wide // per), lambda g, l=l, per=per: (l, g // per, 0, g % per))
            )
            out_specs.append(pl.BlockSpec((1, width, wide // per), lambda g, per=per: (g // per, 0, g % per)))
            shapes.append(sds(count, width, wide, dtype=BF))
        return pl.pallas_call(
            k_cast,
            grid=(4,),
            in_specs=in_specs,
            out_specs=out_specs,
            out_shape=shapes,
            compiler_params=params(),
            cost_estimate=pl.CostEstimate(flops=0, bytes_accessed=6 * len(picks) * 2**20, transcendentals=0),
            name="cast",
        )(*[weights for weights, _ in picks])

    def with_peers(own):
        return [own] + [from_peer(own, j) for j in range(1, mp)]

    own = cast([(hidden_weights, 0)])
    own += cast([(mlp_weights, 0)] + [(w, l) for l in range(1, layers) for w in (hidden_weights, mlp_weights)])
    hid_parts = [with_peers(own[2 * l]) for l in range(layers)]
    mlp_parts = [with_peers(own[2 * l + 1]) for l in range(layers)]
    bias_all = jnp.concatenate([gate_bias] + [from_peer(gate_bias, j) for j in range(1, mp)], axis=2)
    info = jnp.stack([lengths[0], me, jnp.int32(mp)]).astype(jnp.int32)

    def make_specs(order):
        def tile(cols):
            return pl.BlockSpec((tr, cols), lambda g: (order(g), 0))

        return tile

    def whole(*shape):
        return pl.BlockSpec(shape, lambda g: (0,) * len(shape), pipeline_mode=pl.Buffered(1))

    smem = pl.BlockSpec(memory_space=pltpu.SMEM)
    vmem = pl.BlockSpec(memory_space=pltpu.VMEM)
    hbm = pl.BlockSpec(memory_space=pl.ANY)
    fwd = make_specs(lambda g: g)
    rev = make_specs(lambda g: grid - 1 - g)
    seg_fwd = pl.BlockSpec((SEG, ts, width), lambda g: (0, g, 0))
    seg_rev = pl.BlockSpec((SEG, ts, width), lambda g: (0, grid - 1 - g, 0))
    before_rev = pl.BlockSpec(
        (16, hid), lambda g: (jnp.maximum((grid - 1 - g) * (tr // 16) - 1, 0), 0)
    )
    start_spec = pl.BlockSpec((SEG, hid), lambda g: (0, 0))
    gates_spec = pl.BlockSpec((3, width, part_h), lambda g: (0, 0, 0), pipeline_mode=pl.Buffered(1))
    wout_spec = pl.BlockSpec((1, width, part_h), lambda g: (3, 0, 0), pipeline_mode=pl.Buffered(1))
    mlp_spec = whole(2, width, part_f)
    gain_spec = whole(2, width)
    bias_spec = whole(2, hid)
    ends_spec = pl.BlockSpec((2, SEG, hid), lambda g: (0, 0, 0))
    fin_spec = pl.BlockSpec((2, hid), lambda g: (0, 0))
    sums_spec = pl.BlockSpec((SEG, width), lambda g: (0, 0))
    bsum_spec = pl.BlockSpec((2, SEG, hid), lambda g: (0, 0, 0))
    kbuf = pltpu.VMEM((2, 3, tr, min(HC, max(part_h, part_f))), F32)
    state = pltpu.VMEM((2, SEG, hid), F32)
    start = pltpu.VMEM((SEG, hid), F32)
    row_f32 = pltpu.VMEM((tr, width), F32)
    lanes = pltpu.VMEM((width // 128, tr, 128), F32)

    t_w = sds(tokens, width)
    t_wb = sds(tokens, width, dtype=BF)
    t_hb = sds(tokens, hid, dtype=BF)
    t_fb = sds(tokens, ff, dtype=BF)
    ends_s = sds(2, SEG, hid)
    start_s = sds(SEG, hid)
    fin_s = sds(2, hid)
    sums_s = sds(SEG, width)
    bsum_s = sds(2, SEG, hid)

    def cost(matmul_cols, elems):
        return pl.CostEstimate(
            flops=2 * tokens * width * matmul_cols,
            bytes_accessed=elems,
            transcendentals=0,
        )

    def chain(fin, send, shift, live):
        carry = send(fin)
        for _ in range(mp - 2):
            known = jnp.roll(carry[0:1] * live, shift, axis=1)
            carry = send(jnp.concatenate([fin[0:1] + fin[1:2] * known, fin[1:2]]))
        return carry

    def chain_forward(fin):
        return chain(fin, to_next, -part_h, (me > 0).astype(F32))

    def chain_backward(fin):
        return chain(fin, to_prev, part_h, (me < mp - 1).astype(F32))

    seg_in = inputs.reshape(SEG, steps, width)
    seg_cot = cotangent.reshape(SEG, steps, width)
    saved = []
    f1_out_specs = lambda t: [t(width)] + [t(hid)] * 7 + [ends_spec, fin_spec]
    f1_out_shapes = [t_wb] + [t_hb] * 7 + [ends_s, fin_s]
    outs = pl.pallas_call(
        functools.partial(k_first, mp),
        grid=(grid,),
        in_specs=[seg_fwd, gain_spec, bias_spec] + [gates_spec] * mp,
        out_specs=[fwd(width)] + f1_out_specs(fwd),
        out_shape=[t_w] + f1_out_shapes,
        scratch_shapes=[kbuf, state, lanes],
        compiler_params=params(),
        cost_estimate=cost(3 * hid, 24 * 2**20),
        name="gates_first",
    )(seg_in, norm_gains[0], bias_all[0], *hid_parts[0])
    x, gate = outs[0], outs[1:]
    xs = [x]
    for l in range(layers - 1):
        nin, take, loc, prod, cand, wf, wi, q, ends, fin = gate
        inc = chain_forward(fin)
        outs = pl.pallas_call(
            functools.partial(k_middle, mp),
            grid=(grid,),
            in_specs=[smem, fin_spec, ends_spec, fwd(width), fwd(hid), fwd(hid)]
            + [gain_spec, gain_spec, bias_spec]
            + [wout_spec] * mp
            + [mlp_spec] * mp
            + [gates_spec] * mp,
            out_specs=[fwd(hid), start_spec] + [fwd(width)] * 2 + [fwd(ff)] * 2 + [fwd(width)] + f1_out_specs(fwd),
            out_shape=[t_hb, start_s, t_w, t_wb, t_fb, t_fb, t_w] + f1_out_shapes,
            scratch_shapes=[kbuf, state],
            compiler_params=params(),
            cost_estimate=cost(4 * hid + 2 * ff, 60 * 2**20),
            name="block_forward",
        )(
            info, inc, ends, xs[l], loc, prod,
            norm_gains[l], norm_gains[l + 1], bias_all[l + 1],
            *hid_parts[l], *mlp_parts[l], *hid_parts[l + 1],
        )
        hlow, began, mid, nmid, act, slope, xn = outs[:7]
        saved.append((nin, take, hlow, began, cand, wf, wi, q, mid, nmid, act, slope))
        xs.append(xn)
        gate = outs[7:]
    top = layers - 1
    nin, take, loc, prod, cand, wf, wi, q, ends, fin = gate
    inc = chain_forward(fin)
    outs = pl.pallas_call(
        functools.partial(k_turn, mp),
        grid=(grid,),
        in_specs=[smem, fin_spec, ends_spec, rev(width), rev(hid), rev(hid), rev(hid)]
        + [gain_spec, seg_rev]
        + [wout_spec] * mp
        + [mlp_spec] * mp,
        out_specs=[rev(hid), start_spec, rev(width), rev(ff), seg_rev, rev(width), rev(ff), rev(width), rev(width)]
        + [rev(hid), rev(hid), ends_spec, fin_spec, sums_spec],
        out_shape=[t_hb, start_s, t_wb, t_fb, sds(SEG, steps, width), t_wb, t_fb, t_wb, t_w]
        + [t_hb, t_hb, ends_s, fin_s, sums_s],
        scratch_shapes=[kbuf, state, row_f32, pltpu.VMEM((tr, ff), BF), row_f32, lanes, lanes],
        compiler_params=params(),
        cost_estimate=cost(2 * hid + 4 * ff, 60 * 2**20),
        name="block_turn",
    )(
        info, inc, ends, xs[top], loc, prod, take, norm_gains[top], seg_cot,
        *hid_parts[top], *mlp_parts[top],
    )
    hlow, began, nmid, act, output, dz, dpre, dout, dx, lam, rprod, ends, fin, sums_mid = outs
    output = output.reshape(1, tokens, width)
    saved.append((nin, take, hlow, began, cand, wf, wi, q, None, nmid, act, None))

    def weight_grads(pairs, lefts, rights, part, wide, after):
        count = len(pairs)
        block = min(256, wide)
        per = wide // block
        in_specs = [whole(tokens, width) for _ in lefts]
        in_specs += [pl.BlockSpec((tokens, block), lambda g: (0, part * per + g)) for _ in rights]
        shifted = tuple((left, len(lefts) + right) for left, right in pairs)
        return pl.pallas_call(
            functools.partial(k_grads, shifted, len(after)),
            grid=(per,),
            in_specs=[hbm] * len(after) + in_specs,
            out_specs=pl.BlockSpec((count, width, block), lambda g: (0, 0, g)),
            out_shape=sds(count, width, wide, dtype=BF),
            compiler_params=params(),
            cost_estimate=cost(count * wide, tokens * wide * count * 2),
            name="weight_grads",
        )(*after, *lefts, *rights)

    def send_parts(pairs, lefts, rights, wide, after=()):
        others = []
        for j in range(1, mp):
            sent = weight_grads(pairs, lefts, rights, j, wide, after)
            others.append(lax.ppermute(sent, "mp", [(m, (m + j) % mp) for m in range(mp)]))
        return others

    dp_me = lax.axis_index("dp")
    who = jnp.concatenate([row_owner, dp_me[None].astype(jnp.int32)])
    count_value = step_count[0].astype(F32)
    fix_one = 1.0 - jnp.power(jnp.float32(BETA_ONE), count_value)
    fix_two = 1.0 - jnp.power(jnp.float32(BETA_TWO), count_value)
    fix = jnp.stack([1.0 / fix_one, 1.0 / fix_two])

    def exchange(value, stage):
        low, count = stage
        return [
            lax.ppermute(value, "dp", [(i, i ^ (r << low)) for i in range(dp_count)])
            for r in range(1, 1 << count)
        ]

    def source_spec(plan, at, shape, tail):
        return pl.BlockSpec(shape, lambda g: tail(plan.local(at, g) // plan.pers[at], plan.local(at, g) % plan.pers[at]))

    def rotate(plan, l, pairs, lefts, rights, recv, blocks, after):
        basis_spec = pl.BlockSpec((1, 1, width, width), lambda g: (l, plan.basis_at(g), 0, 0))
        specs, flat = [], []
        for at, one in enumerate(blocks):
            order = one.shape[-1]
            nb = plan.blocks[at] // order
            specs.append(source_spec(plan, at, (1, 1, nb, order, order), lambda k, c: (l, k, c, 0, 0)))
        for at, ones in enumerate(recv):
            for one in ones:
                specs.append(source_spec(plan, at, (1, width, plan.blocks[at]), lambda k, c: (k, 0, c)))
                flat.append(one)
        specs += [whole(tokens, width)] * len(lefts)
        for m in range(len(rights)):
            at = plan.source_of[plan.matrix_of.index(m)]
            first = plan.matrix_of.index(m)
            last = plan.pers[at] - 1
            specs.append(
                pl.BlockSpec(
                    (tokens, plan.blocks[at]), lambda g, first=first, last=last: (0, jnp.clip(g - first, 0, last))
                )
            )
        out_shapes = [
            sds(width // n, cols, dtype=BF) for n, cols in zip(plan.firsts, plan.cols) for _ in range(n)
        ]
        outs = pl.pallas_call(
            functools.partial(k_rotate, plan, mp - 1, pairs, len(after)),
            grid=(plan.begins[-1],),
            in_specs=[smem, basis_spec] + [hbm] * len(after) + specs,
            out_specs=[pl.BlockSpec(o.shape, lambda g: (0, 0)) for o in out_shapes],
            out_shape=out_shapes,
            scratch_shapes=[pltpu.VMEM((width, cols), BF) for cols in plan.cols],
            compiler_params=params(),
            cost_estimate=cost(6 * sum(plan.cols), 24 * 2**20),
            name="rotate",
        )(who, left_bases, *after, *blocks, *flat, *lefts, *rights)
        pieces, at = [], 0
        for n in plan.firsts:
            pieces.append(outs[at : at + n])
            at += n
        return pieces

    def scatter_stage(plan, pieces, at):
        held = []
        for stages, mine in zip(plan.stages, pieces):
            low, count = stages[at]
            got = [
                lax.ppermute(mine[r], "dp", [(i, i ^ (r << low)) for i in range(dp_count)])
                for r in range(1, 1 << count)
            ]
            held.append([mine[0]] + got)
        return held

    def combine(plan, held, at, after=(), small=()):
        flat = [v for one in held for v in one]
        n_in = [len(one) for one in held]
        n_out = [1 << stages[at + 1][1] for stages in plan.stages]
        shapes = [
            sds(one[0].shape[0] // n, one[0].shape[1], dtype=BF) for one, n in zip(held, n_out) for _ in range(n)
        ]
        halves = 2 if all(cols % 256 == 0 for cols in plan.cols) else 1

        def part_of(shape):
            return pl.BlockSpec((shape[0], shape[1] // halves), lambda g: (0, g))

        small_specs = [pl.BlockSpec(v.shape, lambda g: (0, 0)) for v in small]
        outs = pl.pallas_call(
            functools.partial(k_combine, n_in, n_out, len(after), len(small)),
            grid=(halves,),
            in_specs=[hbm] * len(after) + [part_of(v.shape) for v in flat] + small_specs,
            out_specs=[part_of(v.shape) for v in shapes] + small_specs[:1],
            out_shape=shapes + [sds(*v.shape) for v in small[:1]],
            compiler_params=params(),
            cost_estimate=pl.CostEstimate(flops=0, bytes_accessed=6 * 2**20, transcendentals=0),
            name="combine",
        )(*after, *flat, *small)
        if small:
            return [outs[sum(n_out[:i]) : sum(n_out[: i + 1])] for i in range(len(n_out))], outs[-1]
        pieces, i = [], 0
        for n in n_out:
            pieces.append(outs[i : i + n])
            i += n
        return pieces

    def adam(plan, spread_plan, l, held, olds, splits, before):
        flat = [v for one in held for v in one]
        out_specs, shapes, in_specs, bufs = [], [], [], []
        for (_, count, wide), split in zip(plan.sources, splits):
            for lo, hi in ((0, count),) * 2 + split:
                out_specs.append(pl.BlockSpec((share, 1, hi - lo, wide), lambda g: (0, l, 0, 0)))
                shapes.append(sds(share, layers, hi - lo, wide))
            in_specs += [pl.BlockSpec((share, 1, count, wide), lambda g: (0, l, 0, 0))] * 2
            bufs.append(pltpu.VMEM((share, 1, count, wide), F32))
        n_state = len(shapes)
        before = before or ()
        outs = pl.pallas_call(
            functools.partial(k_adam, plan, spread_plan, splits, len(before)),
            grid=(1,),
            in_specs=[smem] + [vmem] * len(flat) + in_specs + [hbm] * len(before),
            out_specs=out_specs + [vmem] * len(spread_plan.cols),
            out_shape=shapes + [sds(share, cols, dtype=BF) for cols in spread_plan.cols],
            scratch_shapes=bufs,
            input_output_aliases={1 + len(flat) + len(olds) + i: i for i in range(len(before))},
            compiler_params=pltpu.CompilerParams(vmem_limit_bytes=VMEM_LIMIT),
            cost_estimate=pl.CostEstimate(flops=0, bytes_accessed=8 * 2**20, transcendentals=0),
            name="adam",
        )(fix, *flat, *olds, *before)
        return tuple(outs[:n_state]), outs[n_state:]

    def gather_moves(plan, moves, after=()):
        held = []
        for stages, value in zip(plan.stages, moves):
            for stage in reversed(stages[2:]):
                value = jnp.concatenate([value] + exchange(value, stage), axis=0)
            held.append([value] + exchange(value, stages[1]))
        halves = 2 if all(cols % 256 == 0 for cols in plan.cols) else 1
        ins = [v for one in held for v in one]
        shapes = [sds(one[0].shape[0] * len(one), one[0].shape[1], dtype=BF) for one in held]

        def part_of(shape):
            return pl.BlockSpec((shape[0], shape[1] // halves), lambda g: (0, g))

        joined = pl.pallas_call(
            functools.partial(k_join, [len(one) for one in held], len(after)),
            grid=(halves,),
            in_specs=[hbm] * len(after) + [part_of(v.shape) for v in ins],
            out_specs=[part_of(v.shape) for v in shapes],
            out_shape=shapes,
            compiler_params=params(),
            cost_estimate=pl.CostEstimate(flops=0, bytes_accessed=4 * 2**20, transcendentals=0),
            name="join",
        )(*after, *ins)
        return [v for stages, value in zip(plan.stages, joined) for v in [value] + exchange(value, stages[0])]

    def apply_moves(plan, l, flat, blocks, weights, before):
        basis_spec = pl.BlockSpec((1, 1, width, width), lambda g: (l, plan.basis_at(g), 0, 0))
        block_specs, specs = [], []
        for at, one in enumerate(blocks):
            order = one.shape[-1]
            nb = plan.blocks[at] // order
            block_specs.append(source_spec(plan, at, (1, 1, nb, order, order), lambda k, c: (l, k, c, 0, 0)))
            specs.append(source_spec(plan, at, (1, 1, width, plan.blocks[at]), lambda k, c: (l, k, 0, c)))
        before = before or ()
        ins = 2 + 2 * len(blocks) + len(flat)
        return tuple(
            pl.pallas_call(
                functools.partial(k_apply, plan, len(before)),
                grid=(plan.begins[-1],),
                in_specs=[smem, basis_spec]
                + block_specs
                + specs
                + [whole(*v.shape) for v in flat]
                + [hbm] * len(before),
                out_specs=specs,
                out_shape=[sds(*w.shape) for w in weights],
                scratch_shapes=[pltpu.VMEM((width, cols), BF) for cols in plan.cols]
                + [pltpu.VMEM((width, max(plan.blocks)), BF)],
                input_output_aliases={ins + i: i for i in range(len(before))},
                compiler_params=params(),
                cost_estimate=cost(2 * sum(plan.cols), 24 * 2**20),
                name="apply_moves",
            )(who, left_bases, *blocks, *weights, *flat, *before)
        )

    plan = Plan(dp_count, width, ((4, 2, part_f), (0, 4, part_h)))
    plain = Plan(dp_count, width, plan.sources, staged=False)
    olds = (mlp_first, mlp_second, hidden_first, hidden_second)
    splits = (((0, 2),), ((0, 2), (2, 4)))

    all_blocks = (mlp_blocks, hidden_blocks)
    stages = len(plan.stages[0])
    mlp_pairs = ((0, 0), (1, 1))
    hid_pairs = ((0, 0), (0, 1), (0, 2), (1, 3))
    all_pairs = tuple(mlp_pairs) + tuple((left + 2, right + 2) for left, right in hid_pairs)

    def finish(l, held, before):
        state, new = before[:2] if before else (None, None)
        back = plan
        state, moves = adam(plan, back, l, held, olds, splits, state)
        flat = gather_moves(back, moves, new[:1] if new else ())
        return state, apply_moves(back, l, flat, all_blocks, (mlp_weights, hidden_weights), new), moves[0]

    done = None
    held = None
    small = []
    gates_after = ()
    for l in reversed(range(layers)):
        nin, take, hlow, began, cand, wf, wi, q, mid, nmid, act, slope = saved[l]
        keys = (lam, rprod, hlow, hlow, cand, wf, wi, q)
        key_specs = [rev(hid)] * 3 + [before_rev] + [rev(hid)] * 4
        inc = chain_backward(fin)
        mlp_recv = send_parts(mlp_pairs, (nmid, dz), (dpre, act), part_f, gates_after)
        if l > 0:
            below = saved[l - 1]
            outs = pl.pallas_call(
                functools.partial(k_return, mp),
                grid=(grid,),
                in_specs=[smem, fin_spec, ends_spec, start_spec]
                + key_specs
                + [rev(width)] * 3
                + [rev(ff), rev(hid), gain_spec, gain_spec]
                + [gates_spec] * mp
                + [mlp_spec] * mp
                + [wout_spec] * mp,
                out_specs=[rev(hid)] * 3
                + [rev(width), rev(ff), rev(width), rev(width), rev(hid), rev(hid)]
                + [ends_spec, fin_spec, sums_spec, sums_spec, bsum_spec],
                out_shape=[t_hb] * 3
                + [t_wb, t_fb, t_wb, t_w, t_hb, t_hb, ends_s, fin_s, sums_s, sums_s, bsum_s],
                scratch_shapes=[kbuf, state, start, row_f32],
                compiler_params=params(),
                cost_estimate=cost(4 * hid + 2 * ff, 60 * 2**20),
                name="block_return",
            )(
                info, inc, ends, began, *keys, xs[l], dx, below[8], below[11], below[1],
                norm_gains[l], norm_gains[l - 1],
                *hid_parts[l], *mlp_parts[l - 1], *hid_parts[l - 1],
            )
            dkf, dki, dkc, dz_next, dpre_next, dout_next, dx, lam, rprod, ends, fin, sums_in, sums_next, bsum = outs
        else:
            outs = pl.pallas_call(
                functools.partial(k_last, mp, len(gates_after)),
                grid=(grid,),
                in_specs=[hbm] * len(gates_after)
                + [smem, fin_spec, ends_spec, start_spec]
                + key_specs
                + [rev(width)] * 2
                + [gain_spec]
                + [gates_spec] * mp,
                out_specs=[rev(hid)] * 3 + [seg_rev, sums_spec, bsum_spec],
                out_shape=[t_hb] * 3 + [sds(SEG, steps, width), sums_s, bsum_s],
                scratch_shapes=[start, row_f32, row_f32, lanes],
                compiler_params=params(),
                cost_estimate=cost(3 * hid, 30 * 2**20),
                name="block_last",
            )(*gates_after, info, inc, ends, began, *keys, xs[l], dx, norm_gains[l], *hid_parts[l])
            dkf, dki, dkc, input_grad, sums_in, bsum = outs
            dz_next = dpre_next = dout_next = sums_next = None
        after = ()
        if held is not None:
            pieces = combine(plan, held, 0)
            after = (pieces[0][0],)
            held = scatter_stage(plan, pieces, 1)
        hid_recv = send_parts(hid_pairs, (nin, dout), (dkf, dki, dkc, hlow), part_h, after)
        after = ()
        if held is not None:
            pieces = combine(plan, held, 1)
            after = (pieces[0][0],)
            held = scatter_stage(plan, pieces, 2)
        pieces = rotate(
            plan, l, all_pairs, (nmid, dz, nin, dout), (dpre, act, dkf, dki, dkc, hlow),
            (mlp_recv, hid_recv), all_blocks, after,
        )
        previous, held = held, scatter_stage(plan, pieces, 0)
        gates_after = (pieces[0][0],)
        if previous is not None:
            previous = scatter_stage(plan, combine(plan, previous, 2, gates_after), 3)
            done = finish(l + 1, previous, done)
        small.append((sums_in, sums_mid, bsum))
        dz, dpre, dout, sums_mid = dz_next, dpre_next, dout_next, sums_next
    small_in = [v for one in reversed(small) for v in one]
    gains, biases = pl.pallas_call(
        k_small,
        in_specs=[vmem] * len(small_in),
        out_specs=[vmem] * 2,
        out_shape=[sds(layers, 2, width), sds(layers, 2, hid)],
        name="small_sums",
    )(*small_in)

    def flat_part(j):
        return jnp.concatenate(
            [gains.reshape(-1, 128), biases[:, :, j * part_h : (j + 1) * part_h].reshape(-1, 128)]
        )

    total = flat_part(0)
    for j in range(1, mp):
        total = total + lax.ppermute(flat_part(j), "mp", [(m, (m + j) % mp) for m in range(mp)])

    def other_half(value, bit):
        return lax.ppermute(value, "dp", [(i, i ^ (1 << bit)) for i in range(dp_count)])

    bits = dp_count.bit_length() - 1
    for at in range(stages - 1):
        pieces, total = combine(plan, held, at, (), (total, other_half(total, at)))
        held = scatter_stage(plan, pieces, at + 1)
    for bit in range(stages - 1, bits):
        total = total + other_half(total, bit)
    total = total.reshape(-1)
    gain_grad = total[: gains.size].reshape(gains.shape)
    bias_grad = total[gains.size :].reshape(layers, 2, part_h)
    done = finish(0, held, done)
    input_grad = input_grad.reshape(1, tokens, width)
    state, (mlp_new, hidden_new), _ = done
    mlp_grad, mlp_first_new, mlp_second_new = state[:3]
    hidden_grad, hidden_first_new, gate_second_new, hidden_second_new = state[3:]
    gain_first_new, gain_second_new, gain_moves = adam_moments(
        gain_grad, gain_first, gain_second, fix_one, fix_two
    )
    bias_first_new, bias_second_new, bias_moves = adam_moments(
        bias_grad, bias_first, bias_second, fix_one, fix_two
    )
    gain_new = norm_gains - GAIN_RATE * gain_moves
    bias_new = gate_bias - BIAS_RATE * bias_moves
    return (
        output,
        input_grad,
        hidden_grad,
        hidden_first_new,
        hidden_second_new,
        gate_second_new,
        hidden_new,
        mlp_grad,
        mlp_first_new,
        mlp_second_new,
        mlp_new,
        gain_grad,
        gain_first_new,
        gain_second_new,
        gain_new,
        bias_grad,
        bias_first_new,
        bias_second_new,
        bias_new,
    )


def solution(mesh):
    in_specs = (
        P("dp", "mp", None),
        P("dp", "mp", None),
        P("dp"),
        P(None, None, None, "mp"),
        P(None, None, None, "mp"),
        P(),
        P(None, None, "mp"),
        P(),
        P(None, None, "mp", None, None),
        P(None, None, "mp", None, None),
        P("dp", None, None, "mp"),
        P("dp", None, None, "mp"),
        P("dp", None, None, "mp"),
        P("dp", None, None, "mp"),
        P(),
        P(),
        P(None, None, "mp"),
        P(None, None, "mp"),
        P(),
        P(),
    )
    out_specs = (
        P("dp", "mp", None),
        P("dp", "mp", None),
        P("dp", None, None, "mp"),
        P("dp", None, None, "mp"),
        P("dp", None, None, "mp"),
        P("dp", None, None, "mp"),
        P(None, None, None, "mp"),
        P("dp", None, None, "mp"),
        P("dp", None, None, "mp"),
        P("dp", None, None, "mp"),
        P(None, None, None, "mp"),
        P(),
        P(),
        P(),
        P(),
        P(None, None, "mp"),
        P(None, None, "mp"),
        P(None, None, "mp"),
        P(None, None, "mp"),
    )
    return jax.shard_map(
        per_device, mesh=mesh, in_specs=in_specs, out_specs=out_specs, check_vma=False
    )
```

```python
import functools
import jax
import jax.numpy as jnp
from jax import lax
from jax.experimental import pallas as pl
from jax.experimental.pallas import tpu as pltpu
from jax.sharding import PartitionSpec as P

NORM_EPS = 1e-05
BETA_ONE = 0.9
BETA_TWO = 0.95
ADAM_EPS = 1e-08
MATRIX_RATE = 0.08
GAIN_RATE = 0.5
BIAS_RATE = 4.0
DECAY_RATE = 0.01
BF = jnp.bfloat16
F32 = jnp.float32
SEG = 8
TILE_STEPS = 64
HC = 256
VMEM_LIMIT = 60 * 1024 * 1024
LOG2E = 1.4426950408889634


def dot_nn(a, b):
    return lax.dot_general(a, b, (((1,), (0,)), ((), ())), preferred_element_type=F32)


def dot_nt(a, b):
    return lax.dot_general(a, b, (((1,), (1,)), ((), ())), preferred_element_type=F32)


def dot_tn(a, b):
    return lax.dot_general(a, b, (((0,), (0,)), ((), ())), preferred_element_type=F32)


def recip(x):
    r = pl.reciprocal(x, approx=True)
    return r * (2.0 - x * r)


def row_blocks(count, size):
    return [slice(at, at + size) for at in range(0, count, size)]


def row_scale(values):
    return lax.rsqrt(jnp.mean(values * values, axis=-1, keepdims=True) + NORM_EPS)


def norm_stage(x_ref, gain, out_ref):
    for r in row_blocks(x_ref.shape[0], 32):
        x = x_ref[r, :]
        out_ref[r, :] = (x * row_scale(x) * gain).astype(BF)


def column_chunks(parts, wide):
    step = min(HC, wide)
    return [(j, c0, j * wide + c0, step) for j in range(parts) for c0 in range(0, wide, step)]


def gate_stage(nin_ref, bias_ref, w_refs, kbuf, state, outs):
    take_ref, loc_ref, prod_ref, cand_ref, wf_ref, wi_ref, q_ref = outs
    for turn, (j, c0, at, wide) in enumerate(column_chunks(len(w_refs), w_refs[0].shape[2])):
        slot = turn % 2
        for k in range(3):
            kbuf[slot, k, :, :wide] = dot_nn(nin_ref[...], w_refs[j][k, :, c0 : c0 + wide])
        cols = slice(at, at + wide)
        bias_f, bias_i = bias_ref[0:1, cols], bias_ref[1:2, cols]
        loc, prod = state[0, :, cols], state[1, :, cols]
        for r in row_blocks(nin_ref.shape[0], 16):
            kf = kbuf[slot, 0, r, :wide] + bias_f
            ki = kbuf[slot, 1, r, :wide] + bias_i
            kc = kbuf[slot, 2, r, :wide]
            tf = jnp.exp(-jnp.abs(kf))
            ti = jnp.exp(-jnp.abs(ki))
            tc = jnp.exp(-jnp.abs(kc))
            gap = jnp.minimum(ki, 0.0) - jnp.minimum(kf, 0.0)
            e = jnp.exp(-jnp.abs(gap))
            ef = jnp.where(gap < 0, e, 1.0)
            ei = jnp.where(gap > 0, e, 1.0)
            nf, ni = ef + ef * tf, ei + ei * ti
            inv = recip(nf + ni)
            keep = ni * inv
            take = nf * inv
            sf = ef * jnp.where(kf >= 0, tf, 1.0)
            si = ei * jnp.where(ki >= 0, ti, 1.0)
            sc = tc * recip(1.0 + tc)
            up = kc >= 0
            cand = jnp.where(up, kc + 0.5, sc)
            slope = jnp.where(up, 1.0, sc - sc * sc)
            take_ref[r, cols] = take.astype(BF)
            cand_ref[r, cols] = cand.astype(BF)
            wf_ref[r, cols] = (keep * inv * sf).astype(BF)
            wi_ref[r, cols] = (take * inv * si).astype(BF)
            q_ref[r, cols] = (take * slope).astype(BF)
            drive = take * cand
            loc0 = keep[:8] * loc + drive[:8]
            prod0 = keep[:8] * prod
            loc = keep[8:] * loc0 + drive[8:]
            prod = keep[8:] * prod0
            loc_ref[r, cols] = jnp.concatenate([loc0, loc]).astype(BF)
            prod_ref[r, cols] = jnp.concatenate([prod0, prod]).astype(BF)
        state[0, :, cols] = loc
        state[1, :, cols] = prod


def fold(state, ends_ref, fin_ref, part, backward):
    hidden = state.shape[2]
    ends_ref[...] = state[...]
    order = list(reversed(range(SEG))) if backward else list(range(SEG))
    value = state[0, order[0] : order[0] + 1, :]
    prod = state[1, order[0] : order[0] + 1, :]
    for s in order[1:]:
        value = state[0, s : s + 1, :] + state[1, s : s + 1, :] * value
        prod = state[1, s : s + 1, :] * prod
    n = hidden // part
    for j in range(n):
        at = ((j - 1) % n if backward else (j + 1) % n) * part
        fin_ref[0:1, j * part : (j + 1) * part] = value[:, at : at + part]
        fin_ref[1:2, j * part : (j + 1) * part] = prod[:, at : at + part]


def carry_forward(inc_ref, ends_ref, start, live):
    start[0:1, :] = inc_ref[0:1, :] * live
    for s in range(SEG - 1):
        start[s + 1 : s + 2, :] = (
            ends_ref[0, s : s + 1, :] + ends_ref[1, s : s + 1, :] * start[s : s + 1, :]
        )


def carry_backward(inc_ref, ends_ref, start, live):
    start[SEG - 1 : SEG, :] = inc_ref[0:1, :] * live
    for s in reversed(range(1, SEG)):
        start[s - 1 : s, :] = (
            ends_ref[0, s : s + 1, :] + ends_ref[1, s : s + 1, :] * start[s : s + 1, :]
        )


def state_stage(start, loc_ref, prod_ref, hlow_ref):
    rows, hidden = loc_ref.shape
    for _, _, at, wide in column_chunks(1, hidden):
        cols = slice(at, at + wide)
        c = jnp.concatenate([start[:, cols], start[:, cols]])
        for r in row_blocks(rows, 16):
            hlow_ref[r, cols] = (loc_ref[r, cols].astype(F32) + prod_ref[r, cols].astype(F32) * c).astype(BF)


def mlp_stage(x_ref, hlow_ref, w_refs, m_refs, gain, kbuf, mid_ref, nmid_ref, act_ref, slope_ref):
    part = w_refs[0].shape[2]
    total = x_ref[...]
    for j, w in enumerate(w_refs):
        total = total + dot_nt(hlow_ref[:, j * part : (j + 1) * part], w[0])
    mid_ref[...] = total
    norm_stage(mid_ref, gain, nmid_ref)
    wide = m_refs[0].shape[2]
    total = mid_ref[...]
    for turn, (j, c0, at, step) in enumerate(column_chunks(len(m_refs), wide)):
        slot = turn % 2
        kbuf[slot, 0, :, :step] = dot_nn(nmid_ref[...], m_refs[j][0, :, c0 : c0 + step])
        cols = slice(at, at + step)
        acts = []
        for r in row_blocks(x_ref.shape[0], 16):
            pre = kbuf[slot, 0, r, :step]
            t = recip(1.0 + jnp.abs(pre) * (0.3275911 * 0.7071067811865476))
            bell = jnp.exp(pre * pre * -0.5)
            poly = (
                (((0.5307027145 * t - 0.7265760135) * t + 0.7107068705) * t - 0.142248368) * t
                + 0.127414796
            ) * t
            tail = poly * bell
            cdf = jnp.where(pre >= 0, 1.0 - tail, tail)
            acts.append((pre * cdf).astype(BF))
            slope_ref[r, cols] = (cdf + pre * (bell * 0.3989422804014327)).astype(BF)
        acts = jnp.concatenate(acts)
        act_ref[:, cols] = acts
        total = total + dot_nt(acts, m_refs[j][1, :, c0 : c0 + step])
    return total


def norm_back_stage(src_ref, gain, dn_ref, dx_ref, sums_ref, low_ref):
    sums = sums_ref[...]
    for r in row_blocks(src_ref.shape[0], 32):
        x = src_ref[r, :]
        scale = row_scale(x)
        unit = x * scale
        d = dn_ref[r, :]
        e = d * gain
        dx = dx_ref[r, :] + scale * (e - unit * jnp.mean(e * unit, axis=-1, keepdims=True))
        dx_ref[r, :] = dx
        if low_ref is not None:
            low_ref[r, :] = dx.astype(BF)
        g = d * unit
        sums = sums + ((g[:8] + g[8:16]) + (g[16:24] + g[24:]))
    sums_ref[...] = sums


def mlp_back_stage(dx_ref, slope_ref, mid_ref, m_refs, gain, dn_ref, dz_ref, dpre_ref, dout_ref, sums_ref):
    dz_ref[...] = dx_ref[...].astype(BF)
    wide = m_refs[0].shape[2]
    for j, c0, at, step in column_chunks(len(m_refs), wide):
        cols = slice(at, at + step)
        dact = dot_nn(dz_ref[...], m_refs[j][1, :, c0 : c0 + step])
        dpre_ref[:, cols] = (dact * slope_ref[:, cols].astype(F32)).astype(BF)
    total = None
    for j, m in enumerate(m_refs):
        term = dot_nt(dpre_ref[:, j * wide : (j + 1) * wide], m[0])
        total = term if total is None else total + term
    dn_ref[...] = total
    norm_back_stage(mid_ref, gain, dn_ref, dx_ref, sums_ref, dout_ref)


def adjoint_stage(dout_ref, w_refs, take_ref, kbuf, state, lam_ref, prod_ref):
    for turn, (j, c0, at, wide) in enumerate(column_chunks(len(w_refs), w_refs[0].shape[2])):
        slot = turn % 2
        kbuf[slot, 0, :, :wide] = dot_nn(dout_ref[...], w_refs[j][0, :, c0 : c0 + wide])
        cols = slice(at, at + wide)
        mu, prod = state[0, :, cols], state[1, :, cols]
        for r in reversed(row_blocks(dout_ref.shape[0], 16)):
            u = kbuf[slot, 0, r, :wide]
            keep = 1.0 - take_ref[r, cols].astype(F32)
            lam1 = u[8:] + mu
            lam0 = u[:8] + keep[8:] * lam1
            mu = keep[:8] * lam0
            prod0 = prod * keep[8:]
            lam_ref[r, cols] = jnp.concatenate([lam0, lam1]).astype(BF)
            prod_ref[r, cols] = jnp.concatenate([prod0, prod]).astype(BF)
            prod = prod0 * keep[:8]
        state[0, :, cols] = mu
        state[1, :, cols] = prod


def keys_stage(first, mu_in, h_in, ins, dk_refs, bias_ref):
    lam_ref, prod_ref, hlow_ref, hbefore_ref, cand_ref, wf_ref, wi_ref, q_ref = ins
    dkf_ref, dki_ref, dkc_ref = dk_refs
    rows, hidden = lam_ref.shape
    for _, _, at, wide in column_chunks(1, hidden):
        cols = slice(at, at + wide)
        c = jnp.concatenate([mu_in[:, cols], mu_in[:, cols]])
        before = jnp.where(first, h_in[:, cols], hbefore_ref[:, cols].astype(F32)[8:])
        sum_f, sum_i = bias_ref[0, :, cols], bias_ref[1, :, cols]
        for r in row_blocks(rows, 16):
            lam = lam_ref[r, cols].astype(F32) + prod_ref[r, cols].astype(F32) * c
            h = hlow_ref[r, cols].astype(F32)
            diff = lam * (cand_ref[r, cols].astype(F32) - jnp.concatenate([before, h[:8]]))
            before = h[8:]
            df = (-(diff * wf_ref[r, cols].astype(F32))).astype(BF)
            di = (diff * wi_ref[r, cols].astype(F32)).astype(BF)
            dkf_ref[r, cols] = df
            dki_ref[r, cols] = di
            dkc_ref[r, cols] = (lam * q_ref[r, cols].astype(F32)).astype(BF)
            df, di = df.astype(F32), di.astype(F32)
            sum_f = sum_f + (df[:8] + df[8:])
            sum_i = sum_i + (di[:8] + di[8:])
        bias_ref[0, :, cols] = sum_f
        bias_ref[1, :, cols] = sum_i


def keys_back_stage(dk_refs, w_refs, dn_ref):
    part = w_refs[0].shape[2]
    total = None
    for j, w in enumerate(w_refs):
        for k in range(3):
            term = dot_nt(dk_refs[k][:, j * part : (j + 1) * part], w[k])
            total = term if total is None else total + term
    dn_ref[...] = total


def spread(src_ref, dst, lanes):
    steps = src_ref.shape[1]
    for c in range(lanes.shape[0]):
        cols = slice(c * 128, c * 128 + 128)
        for s in range(SEG):
            lanes[c, pl.ds(s, steps, stride=SEG), :] = src_ref[s, :, cols].astype(F32)
        dst[:, cols] = lanes[c]


def gather_out(src, dst_ref, lanes):
    steps = dst_ref.shape[1]
    for c in range(lanes.shape[0]):
        cols = slice(c * 128, c * 128 + 128)
        lanes[c] = src[:, cols]
        for s in range(SEG):
            dst_ref[s, :, cols] = lanes[c, pl.ds(s, steps, stride=SEG), :]


def reset(state):
    state[0] = jnp.zeros_like(state[0])
    state[1] = jnp.ones_like(state[1])


def k_cast(*refs):
    half = len(refs) // 2
    for src, dst in zip(refs[:half], refs[half:]):
        dst[...] = src[0].astype(BF)


def k_first(n_parts, in_ref, gain_ref, bias_ref, *refs):
    w = refs[:n_parts]
    xp, nin = refs[n_parts : n_parts + 2]
    gates = refs[n_parts + 2 : n_parts + 9]
    ends, fin, kbuf, state, lanes = refs[n_parts + 9 :]
    g = pl.program_id(0)

    @pl.when(g == 0)
    def _():
        reset(state)

    spread(in_ref, xp, lanes)
    norm_stage(xp, gain_ref[0:1, :], nin)
    gate_stage(nin, bias_ref, w, kbuf, state, gates)

    @pl.when(g == pl.num_programs(0) - 1)
    def _():
        fold(state, ends, fin, w[0].shape[2], False)


def k_middle(n_parts, info, inc, ends_in, x, loc, prod, gain, gain_next, bias, *refs):
    wo = refs[:n_parts]
    m = refs[n_parts : 2 * n_parts]
    w = refs[2 * n_parts : 3 * n_parts]
    hlow, start, mid, nmid, act, slope, xn, nin = refs[3 * n_parts : 3 * n_parts + 8]
    gates = refs[3 * n_parts + 8 : 3 * n_parts + 15]
    ends, fin, kbuf, state = refs[3 * n_parts + 15 :]
    g = pl.program_id(0)

    @pl.when(g == 0)
    def _():
        reset(state)
        carry_forward(inc, ends_in, start, (info[1] > 0).astype(F32))

    state_stage(start, loc, prod, hlow)
    xn[...] = mlp_stage(x, hlow, wo, m, gain[1:2, :], kbuf, mid, nmid, act, slope)
    norm_stage(xn, gain_next[0:1, :], nin)
    gate_stage(nin, bias, w, kbuf, state, gates)

    @pl.when(g == pl.num_programs(0) - 1)
    def _():
        fold(state, ends, fin, w[0].shape[2], False)


def k_turn(n_parts, info, inc, ends_in, x, loc, prod, take, gain, cot, *refs):
    wo = refs[:n_parts]
    m = refs[n_parts : 2 * n_parts]
    (hlow, start, nmid, act, out, dz, dpre, dout, dx, lam, prod_o, ends, fin, sums) = refs[
        2 * n_parts : 2 * n_parts + 14
    ]
    kbuf, state, mid, slope, dn, lanes, out_lanes = refs[2 * n_parts + 14 :]
    g = pl.program_id(0)
    tile = pl.num_programs(0) - 1 - g
    rows = x.shape[0]
    steps_all = pl.num_programs(0) * (rows // SEG)

    @pl.when(g == 0)
    def _():
        reset(state)
        sums[...] = jnp.zeros_like(sums)
        carry_forward(inc, ends_in, start, (info[1] > 0).astype(F32))

    state_stage(start, loc, prod, hlow)
    top = mlp_stage(x, hlow, wo, m, gain[1:2, :], kbuf, mid, nmid, act, slope)
    at = lax.broadcasted_iota(jnp.int32, (rows, 1), 0)
    place = info[1] * (SEG * steps_all) + (at % SEG) * steps_all + tile * (rows // SEG) + at // SEG
    mask = (place < info[0]).astype(F32)
    gather_out(top * mask, out, out_lanes)

    @pl.when(g >= 0)
    def _():
        spread(cot, dx, lanes)
        dx[...] = dx[...] * mask
        mlp_back_stage(dx, slope, mid, m, gain[1:2, :], dn, dz, dpre, dout, sums)
        adjoint_stage(dout, wo, take, kbuf, state, lam, prod_o)

    @pl.when(g == pl.num_programs(0) - 1)
    def _():
        fold(state, ends, fin, wo[0].shape[2], True)


def k_return(n_parts, info, inc, ends_in, h_in, *refs):
    keys = refs[:8]
    x, dx_in, mid, slope, take, gain, gain_prev = refs[8:15]
    refs = refs[15:]
    w = refs[:n_parts]
    m = refs[n_parts : 2 * n_parts]
    wo = refs[2 * n_parts : 3 * n_parts]
    (dkf, dki, dkc, dz, dpre, dout, dx, lam_o, prod_o, ends, fin, sums_in, sums_mid, bias) = refs[
        3 * n_parts : 3 * n_parts + 14
    ]
    kbuf, state, start, dn = refs[3 * n_parts + 14 :]
    g = pl.program_id(0)
    last = pl.num_programs(0) - 1

    @pl.when(g == 0)
    def _():
        reset(state)
        sums_in[...] = jnp.zeros_like(sums_in)
        sums_mid[...] = jnp.zeros_like(sums_mid)
        bias[...] = jnp.zeros_like(bias)
        carry_backward(inc, ends_in, start, (info[1] < info[2] - 1).astype(F32))

    keys_stage(g == last, start, h_in, keys, (dkf, dki, dkc), bias)
    keys_back_stage((dkf, dki, dkc), w, dn)
    dx[...] = dx_in[...]
    norm_back_stage(x, gain[0:1, :], dn, dx, sums_in, None)
    mlp_back_stage(dx, slope, mid, m, gain_prev[1:2, :], dn, dz, dpre, dout, sums_mid)
    adjoint_stage(dout, wo, take, kbuf, state, lam_o, prod_o)

    @pl.when(g == last)
    def _():
        fold(state, ends, fin, wo[0].shape[2], True)


def k_last(n_parts, n_after, *refs):
    info, inc, ends_in, h_in = refs[n_after : n_after + 4]
    refs = refs[n_after + 4 :]
    keys = refs[:8]
    x, dx_in, gain = refs[8:11]
    w = refs[11 : 11 + n_parts]
    dkf, dki, dkc, out, sums_in, bias = refs[11 + n_parts : 17 + n_parts]
    start, dn, dx, lanes = refs[17 + n_parts :]
    g = pl.program_id(0)
    last = pl.num_programs(0) - 1

    @pl.when(g == 0)
    def _():
        sums_in[...] = jnp.zeros_like(sums_in)
        bias[...] = jnp.zeros_like(bias)
        carry_backward(inc, ends_in, start, (info[1] < info[2] - 1).astype(F32))

    keys_stage(g == last, start, h_in, keys, (dkf, dki, dkc), bias)
    keys_back_stage((dkf, dki, dkc), w, dn)
    dx[...] = dx_in[...]
    norm_back_stage(x, gain[0:1, :], dn, dx, sums_in, None)
    gather_out(dx, out, lanes)


def k_grads(pairs, n_after, *refs):
    refs = refs[n_after:]
    out = refs[-1]
    for k, (left, right) in enumerate(pairs):
        out[k] = dot_tn(refs[left][...], refs[right][...]).astype(BF)


def place_of(owner, me, stages):
    if stages is None:
        return owner
    relative = owner ^ me
    place = None
    for low, count in stages:
        digit = (relative >> low) & ((1 << count) - 1)
        place = digit if place is None else (place << count) + digit
    return place


def turn_blocks(value, blocks, inverse):
    order = blocks.shape[-1]
    dot = dot_nt if inverse else dot_nn
    return jnp.concatenate(
        [
            dot(value[:, b * order : (b + 1) * order], blocks[0, 0, b].astype(BF))
            for b in range(blocks.shape[2])
        ],
        axis=1,
    )


def k_rotate(plan, n_recv, pairs, n_after, who, basis, *refs):
    refs = refs[n_after:]
    n_src = len(plan.sources)
    n_left, n_right = 1 + max(p[0] for p in pairs), len(pairs)
    blocks = refs[:n_src]
    recv = refs[n_src : n_src * (1 + n_recv)]
    refs = refs[n_src * (1 + n_recv) :]
    lefts, rights = refs[:n_left], refs[n_left : n_left + n_right]
    refs = refs[n_left + n_right :]
    n_out = sum(plan.firsts)
    outs, bufs = refs[:n_out], refs[n_out:]
    g = pl.program_id(0)
    share = plan.share
    width = basis.shape[2]
    count = width // share
    for chunk, runs in enumerate(plan.runs):
        at, pair = plan.source_of[chunk], pairs[plan.matrix_of[chunk]]

        @pl.when(g == chunk)
        def _(runs=runs, at=at, pair=pair):
            total = dot_tn(lefts[pair[0]][...], rights[pair[1]][...])
            for ref in recv[at * n_recv : (at + 1) * n_recv]:
                total = total + ref[0].astype(F32)
            turned = turn_blocks(total.astype(BF), blocks[at], False).astype(BF)
            done = dot_tn(basis[0, 0].astype(BF), turned).astype(BF)
            for b in range(count):
                for stream, src, dst, wide in runs:
                    row = place_of(who[b], who[count], plan.stages[stream]) * share
                    bufs[stream][pl.ds(pl.multiple_of(row, share), share), dst : dst + wide] = done[
                        b * share : (b + 1) * share, src : src + wide
                    ]

    @pl.when(g == pl.num_programs(0) - 1)
    def _():
        at = 0
        for stream, pieces in enumerate(plan.firsts):
            rows = width // pieces
            for r in range(pieces):
                outs[at][...] = bufs[stream][r * rows : (r + 1) * rows, :]
                at += 1


def sum_pieces(refs):
    total = refs[0][...].astype(F32)
    for ref in refs[1:]:
        total = total + ref[...].astype(F32)
    return total


def k_combine(n_in, n_out, n_after, n_small, *refs):
    refs = refs[n_after:]
    if n_small:
        at = sum(n_in)
        refs[-1][...] = refs[at][...] + refs[at + 1][...]
        refs = refs[:at] + refs[at + 2 : -1]
    i, o = 0, sum(n_in)
    for take, give in zip(n_in, n_out):
        total = sum_pieces(refs[i : i + take]).astype(BF)
        rows = total.shape[0] // give
        for r in range(give):
            refs[o + r][...] = total[r * rows : (r + 1) * rows, :]
        i += take
        o += give


def k_join(n_in, n_after, *refs):
    refs = refs[n_after:]
    outs = refs[sum(n_in) :]
    i = 0
    for out, take in zip(outs, n_in):
        rows = refs[i].shape[0]
        for r in range(take):
            out[r * rows : (r + 1) * rows, :] = refs[i + r][...]
        i += take


def k_adam(plan, spread_plan, splits, n_alias, fix, *refs):
    n_in = sum(plan.lasts)
    n_src = len(plan.sources)
    pieces = refs[:n_in]
    olds = refs[n_in : n_in + 2 * n_src]
    outs = refs[n_in + 2 * n_src + n_alias :]
    bufs = refs[len(refs) - n_src :]
    moves_o = outs[sum(2 + len(split) for split in splits) :][: len(spread_plan.stages)]
    sums, i = [], 0
    for take in plan.lasts:
        sums.append(sum_pieces(pieces[i : i + take]))
        i += take
    o = 0
    for at, split in enumerate(splits):
        grad_o, first_o = outs[o : o + 2]
        second_o = outs[o + 2 : o + 2 + len(split)]
        o += 2 + len(split)
        first, second = olds[2 * at : 2 * at + 2]
        for chunk in range(plan.begins[at], plan.begins[at + 1]):
            kind, base = plan.where(at, chunk)
            for stream, src, dst, wide in plan.runs[chunk]:
                grad_o[:, 0, kind, base + src : base + src + wide] = sums[stream][:, dst : dst + wide]
        grad = grad_o[...]
        one = BETA_ONE * first[...] + (1.0 - BETA_ONE) * grad
        two = BETA_TWO * second[...] + (1.0 - BETA_TWO) * grad * grad
        first_o[...] = one
        for ref, (lo, hi) in zip(second_o, split):
            ref[...] = two[:, :, lo:hi, :]
        bufs[at][...] = one * fix[0] / (jnp.sqrt(two * fix[1]) + ADAM_EPS)
        for chunk in range(plan.begins[at], plan.begins[at + 1]):
            kind, base = plan.where(at, chunk)
            for stream, src, dst, wide in spread_plan.runs[chunk]:
                moves_o[stream][:, dst : dst + wide] = bufs[at][
                    :, 0, kind, base + src : base + src + wide
                ].astype(BF)


def k_apply(plan, n_alias, who, basis, *refs):
    n_src = len(plan.sources)
    n_in = sum(plan.firsts)
    blocks = refs[:n_src]
    weights = refs[n_src : 2 * n_src]
    pieces = refs[2 * n_src : 2 * n_src + n_in]
    outs = refs[2 * n_src + n_in + n_alias :][:n_src]
    bufs = refs[2 * n_src + n_in + n_alias + n_src : -1]
    moves = refs[-1]
    g = pl.program_id(0)
    share = plan.share
    width = basis.shape[2]
    count = width // share

    @pl.when(g == 0)
    def _():
        at = 0
        for stream, n in enumerate(plan.firsts):
            rows = width // n
            for r in range(n):
                bufs[stream][r * rows : (r + 1) * rows, :] = pieces[at][...]
                at += 1

    for chunk, runs in enumerate(plan.runs):

        @pl.when(g == chunk)
        def _(runs=runs):
            for stream, src, dst, wide in runs:
                for b in range(count):
                    at = place_of(who[b], who[count], plan.stages[stream]) * share
                    moves[b * share : (b + 1) * share, src : src + wide] = bufs[stream][
                        pl.ds(pl.multiple_of(at, share), share), dst : dst + wide
                    ]

    for at in range(n_src):

        @pl.when((g >= plan.begins[at]) & (g < plan.begins[at + 1]))
        def _(at=at):
            wide = plan.blocks[at]
            back = dot_nn(basis[0, 0].astype(BF), moves[:, :wide]).astype(BF)
            step = turn_blocks(back, blocks[at], True)
            old = weights[at][0, 0]
            outs[at][0, 0] = old - MATRIX_RATE * (step + DECAY_RATE * old)


class Plan:
    def __init__(self, dp_count, width, sources, staged=True):
        bits = dp_count.bit_length() - 1
        x, y, z, rest = (0, 1), (1, 1), (2, 1), (3, bits - 3)
        orders = [[x, y, z, rest], [y, x, z, rest], [z, rest, x, y]]
        self.share = width // dp_count
        self.sources = sources
        self.blocks = [min(512, wide) for _, _, wide in sources]
        self.pers = [wide // block for (_, _, wide), block in zip(sources, self.blocks)]
        self.begins = [0]
        for (_, count, _), per in zip(sources, self.pers):
            self.begins.append(self.begins[-1] + count * per)
        self.source_of, self.matrix_of = [], []
        matrices = 0
        for at, (_, count, _) in enumerate(sources):
            for k in range(count):
                self.source_of += [at] * self.pers[at]
                self.matrix_of += [matrices + k] * self.pers[at]
            matrices += count
        named = []
        for at, block in enumerate(self.blocks):
            for chunk in range(self.begins[at], self.begins[at + 1]):
                named.append([0 if not staged else 2 if lane == 3 else chunk % 2 for lane in range(block // 128)])
        used = sorted({stream for row in named for stream in row})
        self.stages = [orders[stream] if staged else None for stream in used]
        self.cols = [0] * len(used)
        self.runs = []
        for row in named:
            runs = []
            for lane, stream in enumerate(row):
                at = used.index(stream)
                if runs and runs[-1][0] == at:
                    runs[-1][3] += 128
                else:
                    runs.append([at, lane * 128, self.cols[at], 128])
                self.cols[at] += 128
            self.runs.append(runs)
        self.firsts = [1 << stages[0][1] if staged else 1 for stages in self.stages]
        self.lasts = [1 << stages[-1][1] if staged else 1 for stages in self.stages]

    def where(self, at, chunk):
        local = chunk - self.begins[at]
        return local // self.pers[at], local % self.pers[at] * self.blocks[at]

    def local(self, at, g):
        return jnp.clip(g - self.begins[at], 0, self.begins[at + 1] - self.begins[at] - 1)

    def basis_at(self, g):
        index = None
        for at, (base, _, _) in enumerate(self.sources):
            here = base + self.local(at, g) // self.pers[at]
            index = here if index is None else jnp.where(g < self.begins[at], index, here)
        return index


def k_small(*refs):
    gains, biases = refs[-2:]
    for l in range(gains.shape[0]):
        sums_in, sums_mid, bias = refs[3 * l : 3 * l + 3]
        gains[l, 0:1, :] = jnp.sum(sums_in[...], axis=0, keepdims=True)
        gains[l, 1:2, :] = jnp.sum(sums_mid[...], axis=0, keepdims=True)
        for k in range(2):
            biases[l, k : k + 1, :] = jnp.sum(bias[k], axis=0, keepdims=True)


def adam_moments(grads, first, second, fix_one, fix_two):
    first = BETA_ONE * first + (1.0 - BETA_ONE) * grads
    second = BETA_TWO * second + (1.0 - BETA_TWO) * grads * grads
    moves = first / fix_one / (jnp.sqrt(second / fix_two) + ADAM_EPS)
    return (first, second, moves)


def params(parallel=False):
    return pltpu.CompilerParams(
        dimension_semantics=("arbitrary",), vmem_limit_bytes=VMEM_LIMIT
    )


def sds(*shape, dtype=F32):
    return jax.ShapeDtypeStruct(shape, dtype)


def per_device(
    inputs,
    cotangent,
    lengths,
    hidden_weights,
    mlp_weights,
    norm_gains,
    gate_bias,
    left_bases,
    hidden_blocks,
    mlp_blocks,
    hidden_first,
    hidden_second,
    mlp_first,
    mlp_second,
    gain_first,
    gain_second,
    bias_first,
    bias_second,
    step_count,
    row_owner,
):
    dp_count = lax.axis_size("dp")
    mp = lax.axis_size("mp")
    me = lax.axis_index("mp")
    tokens = inputs.shape[1]
    width = inputs.shape[2]
    part_h = hidden_weights.shape[3]
    part_f = mlp_weights.shape[3]
    hid = part_h * mp
    ff = part_f * mp
    layers = hidden_weights.shape[0]
    steps = tokens // SEG
    ts = min(TILE_STEPS, steps)
    tr = ts * SEG
    grid = steps // ts
    share = width // dp_count

    def from_peer(value, j):
        return lax.ppermute(value, "mp", [((m + j) % mp, m) for m in range(mp)])

    def to_next(value):
        return lax.ppermute(value, "mp", [(m, (m + 1) % mp) for m in range(mp)])

    def to_prev(value):
        return lax.ppermute(value, "mp", [((m + 1) % mp, m) for m in range(mp)])

    def cast(picks):
        in_specs, out_specs, shapes = [], [], []
        for weights, l in picks:
            _, count, _, wide = weights.shape
            per = 4 // count
            in_specs.append(
                pl.BlockSpec((1, 1, width, wide // per), lambda g, l=l, per=per: (l, g // per, 0, g % per))
            )
            out_specs.append(pl.BlockSpec((1, width, wide // per), lambda g, per=per: (g // per, 0, g % per)))
            shapes.append(sds(count, width, wide, dtype=BF))
        return pl.pallas_call(
            k_cast,
            grid=(4,),
            in_specs=in_specs,
            out_specs=out_specs,
            out_shape=shapes,
            compiler_params=params(),
            cost_estimate=pl.CostEstimate(flops=0, bytes_accessed=6 * len(picks) * 2**20, transcendentals=0),
            name="cast",
        )(*[weights for weights, _ in picks])

    def with_peers(own):
        return [own] + [from_peer(own, j) for j in range(1, mp)]

    own = cast([(hidden_weights, 0)])
    own += cast([(mlp_weights, 0)] + [(w, l) for l in range(1, layers) for w in (hidden_weights, mlp_weights)])
    hid_parts = [with_peers(own[2 * l]) for l in range(layers)]
    mlp_parts = [with_peers(own[2 * l + 1]) for l in range(layers)]
    bias_all = jnp.concatenate([gate_bias] + [from_peer(gate_bias, j) for j in range(1, mp)], axis=2)
    info = jnp.stack([lengths[0], me, jnp.int32(mp)]).astype(jnp.int32)

    def make_specs(order):
        def tile(cols):
            return pl.BlockSpec((tr, cols), lambda g: (order(g), 0))

        return tile

    def whole(*shape):
        return pl.BlockSpec(shape, lambda g: (0,) * len(shape), pipeline_mode=pl.Buffered(1))

    smem = pl.BlockSpec(memory_space=pltpu.SMEM)
    vmem = pl.BlockSpec(memory_space=pltpu.VMEM)
    hbm = pl.BlockSpec(memory_space=pl.ANY)
    fwd = make_specs(lambda g: g)
    rev = make_specs(lambda g: grid - 1 - g)
    seg_fwd = pl.BlockSpec((SEG, ts, width), lambda g: (0, g, 0))
    seg_rev = pl.BlockSpec((SEG, ts, width), lambda g: (0, grid - 1 - g, 0))
    before_rev = pl.BlockSpec(
        (16, hid), lambda g: (jnp.maximum((grid - 1 - g) * (tr // 16) - 1, 0), 0)
    )
    start_spec = pl.BlockSpec((SEG, hid), lambda g: (0, 0))
    gates_spec = pl.BlockSpec((3, width, part_h), lambda g: (0, 0, 0), pipeline_mode=pl.Buffered(1))
    wout_spec = pl.BlockSpec((1, width, part_h), lambda g: (3, 0, 0), pipeline_mode=pl.Buffered(1))
    mlp_spec = whole(2, width, part_f)
    gain_spec = whole(2, width)
    bias_spec = whole(2, hid)
    ends_spec = pl.BlockSpec((2, SEG, hid), lambda g: (0, 0, 0))
    fin_spec = pl.BlockSpec((2, hid), lambda g: (0, 0))
    sums_spec = pl.BlockSpec((SEG, width), lambda g: (0, 0))
    bsum_spec = pl.BlockSpec((2, SEG, hid), lambda g: (0, 0, 0))
    kbuf = pltpu.VMEM((2, 3, tr, min(HC, max(part_h, part_f))), F32)
    state = pltpu.VMEM((2, SEG, hid), F32)
    start = pltpu.VMEM((SEG, hid), F32)
    row_f32 = pltpu.VMEM((tr, width), F32)
    lanes = pltpu.VMEM((width // 128, tr, 128), F32)

    t_w = sds(tokens, width)
    t_wb = sds(tokens, width, dtype=BF)
    t_hb = sds(tokens, hid, dtype=BF)
    t_fb = sds(tokens, ff, dtype=BF)
    ends_s = sds(2, SEG, hid)
    start_s = sds(SEG, hid)
    fin_s = sds(2, hid)
    sums_s = sds(SEG, width)
    bsum_s = sds(2, SEG, hid)

    def cost(matmul_cols, elems):
        return pl.CostEstimate(
            flops=2 * tokens * width * matmul_cols,
            bytes_accessed=elems,
            transcendentals=0,
        )

    def chain(fin, send, shift, live):
        carry = send(fin)
        for _ in range(mp - 2):
            known = jnp.roll(carry[0:1] * live, shift, axis=1)
            carry = send(jnp.concatenate([fin[0:1] + fin[1:2] * known, fin[1:2]]))
        return carry

    def chain_forward(fin):
        return chain(fin, to_next, -part_h, (me > 0).astype(F32))

    def chain_backward(fin):
        return chain(fin, to_prev, part_h, (me < mp - 1).astype(F32))

    seg_in = inputs.reshape(SEG, steps, width)
    seg_cot = cotangent.reshape(SEG, steps, width)
    saved = []
    f1_out_specs = lambda t: [t(width)] + [t(hid)] * 7 + [ends_spec, fin_spec]
    f1_out_shapes = [t_wb] + [t_hb] * 7 + [ends_s, fin_s]
    outs = pl.pallas_call(
        functools.partial(k_first, mp),
        grid=(grid,),
        in_specs=[seg_fwd, gain_spec, bias_spec] + [gates_spec] * mp,
        out_specs=[fwd(width)] + f1_out_specs(fwd),
        out_shape=[t_w] + f1_out_shapes,
        scratch_shapes=[kbuf, state, lanes],
        compiler_params=params(),
        cost_estimate=cost(3 * hid, 24 * 2**20),
        name="gates_first",
    )(seg_in, norm_gains[0], bias_all[0], *hid_parts[0])
    x, gate = outs[0], outs[1:]
    xs = [x]
    for l in range(layers - 1):
        nin, take, loc, prod, cand, wf, wi, q, ends, fin = gate
        inc = chain_forward(fin)
        outs = pl.pallas_call(
            functools.partial(k_middle, mp),
            grid=(grid,),
            in_specs=[smem, fin_spec, ends_spec, fwd(width), fwd(hid), fwd(hid)]
            + [gain_spec, gain_spec, bias_spec]
            + [wout_spec] * mp
            + [mlp_spec] * mp
            + [gates_spec] * mp,
            out_specs=[fwd(hid), start_spec] + [fwd(width)] * 2 + [fwd(ff)] * 2 + [fwd(width)] + f1_out_specs(fwd),
            out_shape=[t_hb, start_s, t_w, t_wb, t_fb, t_fb, t_w] + f1_out_shapes,
            scratch_shapes=[kbuf, state],
            compiler_params=params(),
            cost_estimate=cost(4 * hid + 2 * ff, 60 * 2**20),
            name="block_forward",
        )(
            info, inc, ends, xs[l], loc, prod,
            norm_gains[l], norm_gains[l + 1], bias_all[l + 1],
            *hid_parts[l], *mlp_parts[l], *hid_parts[l + 1],
        )
        hlow, began, mid, nmid, act, slope, xn = outs[:7]
        saved.append((nin, take, hlow, began, cand, wf, wi, q, mid, nmid, act, slope))
        xs.append(xn)
        gate = outs[7:]
    top = layers - 1
    nin, take, loc, prod, cand, wf, wi, q, ends, fin = gate
    inc = chain_forward(fin)
    outs = pl.pallas_call(
        functools.partial(k_turn, mp),
        grid=(grid,),
        in_specs=[smem, fin_spec, ends_spec, rev(width), rev(hid), rev(hid), rev(hid)]
        + [gain_spec, seg_rev]
        + [wout_spec] * mp
        + [mlp_spec] * mp,
        out_specs=[rev(hid), start_spec, rev(width), rev(ff), seg_rev, rev(width), rev(ff), rev(width), rev(width)]
        + [rev(hid), rev(hid), ends_spec, fin_spec, sums_spec],
        out_shape=[t_hb, start_s, t_wb, t_fb, sds(SEG, steps, width), t_wb, t_fb, t_wb, t_w]
        + [t_hb, t_hb, ends_s, fin_s, sums_s],
        scratch_shapes=[kbuf, state, row_f32, pltpu.VMEM((tr, ff), BF), row_f32, lanes, lanes],
        compiler_params=params(),
        cost_estimate=cost(2 * hid + 4 * ff, 60 * 2**20),
        name="block_turn",
    )(
        info, inc, ends, xs[top], loc, prod, take, norm_gains[top], seg_cot,
        *hid_parts[top], *mlp_parts[top],
    )
    hlow, began, nmid, act, output, dz, dpre, dout, dx, lam, rprod, ends, fin, sums_mid = outs
    output = output.reshape(1, tokens, width)
    saved.append((nin, take, hlow, began, cand, wf, wi, q, None, nmid, act, None))

    def weight_grads(pairs, lefts, rights, part, wide, after):
        count = len(pairs)
        block = min(256, wide)
        per = wide // block
        in_specs = [whole(tokens, width) for _ in lefts]
        in_specs += [pl.BlockSpec((tokens, block), lambda g: (0, part * per + g)) for _ in rights]
        shifted = tuple((left, len(lefts) + right) for left, right in pairs)
        return pl.pallas_call(
            functools.partial(k_grads, shifted, len(after)),
            grid=(per,),
            in_specs=[hbm] * len(after) + in_specs,
            out_specs=pl.BlockSpec((count, width, block), lambda g: (0, 0, g)),
            out_shape=sds(count, width, wide, dtype=BF),
            compiler_params=params(),
            cost_estimate=cost(count * wide, tokens * wide * count * 2),
            name="weight_grads",
        )(*after, *lefts, *rights)

    def send_parts(pairs, lefts, rights, wide, after=()):
        others = []
        for j in range(1, mp):
            sent = weight_grads(pairs, lefts, rights, j, wide, after)
            others.append(lax.ppermute(sent, "mp", [(m, (m + j) % mp) for m in range(mp)]))
        return others

    dp_me = lax.axis_index("dp")
    who = jnp.concatenate([row_owner, dp_me[None].astype(jnp.int32)])
    count_value = step_count[0].astype(F32)
    fix_one = 1.0 - jnp.power(jnp.float32(BETA_ONE), count_value)
    fix_two = 1.0 - jnp.power(jnp.float32(BETA_TWO), count_value)
    fix = jnp.stack([1.0 / fix_one, 1.0 / fix_two])

    def exchange(value, stage):
        low, count = stage
        return [
            lax.ppermute(value, "dp", [(i, i ^ (r << low)) for i in range(dp_count)])
            for r in range(1, 1 << count)
        ]

    def source_spec(plan, at, shape, tail):
        return pl.BlockSpec(shape, lambda g: tail(plan.local(at, g) // plan.pers[at], plan.local(at, g) % plan.pers[at]))

    def rotate(plan, l, pairs, lefts, rights, recv, blocks, after):
        basis_spec = pl.BlockSpec((1, 1, width, width), lambda g: (l, plan.basis_at(g), 0, 0))
        specs, flat = [], []
        for at, one in enumerate(blocks):
            order = one.shape[-1]
            nb = plan.blocks[at] // order
            specs.append(source_spec(plan, at, (1, 1, nb, order, order), lambda k, c: (l, k, c, 0, 0)))
        for at, ones in enumerate(recv):
            for one in ones:
                specs.append(source_spec(plan, at, (1, width, plan.blocks[at]), lambda k, c: (k, 0, c)))
                flat.append(one)
        specs += [whole(tokens, width)] * len(lefts)
        for m in range(len(rights)):
            at = plan.source_of[plan.matrix_of.index(m)]
            first = plan.matrix_of.index(m)
            last = plan.pers[at] - 1
            specs.append(
                pl.BlockSpec(
                    (tokens, plan.blocks[at]), lambda g, first=first, last=last: (0, jnp.clip(g - first, 0, last))
                )
            )
        out_shapes = [
            sds(width // n, cols, dtype=BF) for n, cols in zip(plan.firsts, plan.cols) for _ in range(n)
        ]
        outs = pl.pallas_call(
            functools.partial(k_rotate, plan, mp - 1, pairs, len(after)),
            grid=(plan.begins[-1],),
            in_specs=[smem, basis_spec] + [hbm] * len(after) + specs,
            out_specs=[pl.BlockSpec(o.shape, lambda g: (0, 0)) for o in out_shapes],
            out_shape=out_shapes,
            scratch_shapes=[pltpu.VMEM((width, cols), BF) for cols in plan.cols],
            compiler_params=params(),
            cost_estimate=cost(6 * sum(plan.cols), 24 * 2**20),
            name="rotate",
        )(who, left_bases, *after, *blocks, *flat, *lefts, *rights)
        pieces, at = [], 0
        for n in plan.firsts:
            pieces.append(outs[at : at + n])
            at += n
        return pieces

    def scatter_stage(plan, pieces, at):
        held = []
        for stages, mine in zip(plan.stages, pieces):
            low, count = stages[at]
            got = [
                lax.ppermute(mine[r], "dp", [(i, i ^ (r << low)) for i in range(dp_count)])
                for r in range(1, 1 << count)
            ]
            held.append([mine[0]] + got)
        return held

    def combine(plan, held, at, after=(), small=()):
        flat = [v for one in held for v in one]
        n_in = [len(one) for one in held]
        n_out = [1 << stages[at + 1][1] for stages in plan.stages]
        shapes = [
            sds(one[0].shape[0] // n, one[0].shape[1], dtype=BF) for one, n in zip(held, n_out) for _ in range(n)
        ]
        halves = 2 if all(cols % 256 == 0 for cols in plan.cols) else 1

        def part_of(shape):
            return pl.BlockSpec((shape[0], shape[1] // halves), lambda g: (0, g))

        small_specs = [pl.BlockSpec(v.shape, lambda g: (0, 0)) for v in small]
        outs = pl.pallas_call(
            functools.partial(k_combine, n_in, n_out, len(after), len(small)),
            grid=(halves,),
            in_specs=[hbm] * len(after) + [part_of(v.shape) for v in flat] + small_specs,
            out_specs=[part_of(v.shape) for v in shapes] + small_specs[:1],
            out_shape=shapes + [sds(*v.shape) for v in small[:1]],
            compiler_params=params(),
            cost_estimate=pl.CostEstimate(flops=0, bytes_accessed=6 * 2**20, transcendentals=0),
            name="combine",
        )(*after, *flat, *small)
        if small:
            return [outs[sum(n_out[:i]) : sum(n_out[: i + 1])] for i in range(len(n_out))], outs[-1]
        pieces, i = [], 0
        for n in n_out:
            pieces.append(outs[i : i + n])
            i += n
        return pieces

    def adam(plan, spread_plan, l, held, olds, splits, before):
        flat = [v for one in held for v in one]
        out_specs, shapes, in_specs, bufs = [], [], [], []
        for (_, count, wide), split in zip(plan.sources, splits):
            for lo, hi in ((0, count),) * 2 + split:
                out_specs.append(pl.BlockSpec((share, 1, hi - lo, wide), lambda g: (0, l, 0, 0)))
                shapes.append(sds(share, layers, hi - lo, wide))
            in_specs += [pl.BlockSpec((share, 1, count, wide), lambda g: (0, l, 0, 0))] * 2
            bufs.append(pltpu.VMEM((share, 1, count, wide), F32))
        n_state = len(shapes)
        before = before or ()
        outs = pl.pallas_call(
            functools.partial(k_adam, plan, spread_plan, splits, len(before)),
            grid=(1,),
            in_specs=[smem] + [vmem] * len(flat) + in_specs + [hbm] * len(before),
            out_specs=out_specs + [vmem] * len(spread_plan.cols),
            out_shape=shapes + [sds(share, cols, dtype=BF) for cols in spread_plan.cols],
            scratch_shapes=bufs,
            input_output_aliases={1 + len(flat) + len(olds) + i: i for i in range(len(before))},
            compiler_params=pltpu.CompilerParams(vmem_limit_bytes=VMEM_LIMIT),
            cost_estimate=pl.CostEstimate(flops=0, bytes_accessed=8 * 2**20, transcendentals=0),
            name="adam",
        )(fix, *flat, *olds, *before)
        return tuple(outs[:n_state]), outs[n_state:]

    def gather_moves(plan, moves, after=()):
        held = []
        for stages, value in zip(plan.stages, moves):
            for stage in reversed(stages[2:]):
                value = jnp.concatenate([value] + exchange(value, stage), axis=0)
            held.append([value] + exchange(value, stages[1]))
        halves = 2 if all(cols % 256 == 0 for cols in plan.cols) else 1
        ins = [v for one in held for v in one]
        shapes = [sds(one[0].shape[0] * len(one), one[0].shape[1], dtype=BF) for one in held]

        def part_of(shape):
            return pl.BlockSpec((shape[0], shape[1] // halves), lambda g: (0, g))

        joined = pl.pallas_call(
            functools.partial(k_join, [len(one) for one in held], len(after)),
            grid=(halves,),
            in_specs=[hbm] * len(after) + [part_of(v.shape) for v in ins],
            out_specs=[part_of(v.shape) for v in shapes],
            out_shape=shapes,
            compiler_params=params(),
            cost_estimate=pl.CostEstimate(flops=0, bytes_accessed=4 * 2**20, transcendentals=0),
            name="join",
        )(*after, *ins)
        return [v for stages, value in zip(plan.stages, joined) for v in [value] + exchange(value, stages[0])]

    def apply_moves(plan, l, flat, blocks, weights, before):
        basis_spec = pl.BlockSpec((1, 1, width, width), lambda g: (l, plan.basis_at(g), 0, 0))
        block_specs, specs = [], []
        for at, one in enumerate(blocks):
            order = one.shape[-1]
            nb = plan.blocks[at] // order
            block_specs.append(source_spec(plan, at, (1, 1, nb, order, order), lambda k, c: (l, k, c, 0, 0)))
            specs.append(source_spec(plan, at, (1, 1, width, plan.blocks[at]), lambda k, c: (l, k, 0, c)))
        before = before or ()
        ins = 2 + 2 * len(blocks) + len(flat)
        return tuple(
            pl.pallas_call(
                functools.partial(k_apply, plan, len(before)),
                grid=(plan.begins[-1],),
                in_specs=[smem, basis_spec]
                + block_specs
                + specs
                + [whole(*v.shape) for v in flat]
                + [hbm] * len(before),
                out_specs=specs,
                out_shape=[sds(*w.shape) for w in weights],
                scratch_shapes=[pltpu.VMEM((width, cols), BF) for cols in plan.cols]
                + [pltpu.VMEM((width, max(plan.blocks)), BF)],
                input_output_aliases={ins + i: i for i in range(len(before))},
                compiler_params=params(),
                cost_estimate=cost(2 * sum(plan.cols), 24 * 2**20),
                name="apply_moves",
            )(who, left_bases, *blocks, *weights, *flat, *before)
        )

    plan = Plan(dp_count, width, ((4, 2, part_f), (0, 4, part_h)))
    plain = Plan(dp_count, width, plan.sources, staged=False)
    olds = (mlp_first, mlp_second, hidden_first, hidden_second)
    splits = (((0, 2),), ((0, 2), (2, 4)))

    all_blocks = (mlp_blocks, hidden_blocks)
    stages = len(plan.stages[0])
    mlp_pairs = ((0, 0), (1, 1))
    hid_pairs = ((0, 0), (0, 1), (0, 2), (1, 3))
    all_pairs = tuple(mlp_pairs) + tuple((left + 2, right + 2) for left, right in hid_pairs)

    def finish(l, held, before):
        state, new = before[:2] if before else (None, None)
        back = plan
        state, moves = adam(plan, back, l, held, olds, splits, state)
        flat = gather_moves(back, moves, new[:1] if new else ())
        return state, apply_moves(back, l, flat, all_blocks, (mlp_weights, hidden_weights), new), moves[0]

    done = None
    held = None
    small = []
    gates_after = ()
    for l in reversed(range(layers)):
        nin, take, hlow, began, cand, wf, wi, q, mid, nmid, act, slope = saved[l]
        keys = (lam, rprod, hlow, hlow, cand, wf, wi, q)
        key_specs = [rev(hid)] * 3 + [before_rev] + [rev(hid)] * 4
        inc = chain_backward(fin)
        mlp_recv = send_parts(mlp_pairs, (nmid, dz), (dpre, act), part_f, gates_after)
        if l > 0:
            below = saved[l - 1]
            outs = pl.pallas_call(
                functools.partial(k_return, mp),
                grid=(grid,),
                in_specs=[smem, fin_spec, ends_spec, start_spec]
                + key_specs
                + [rev(width)] * 3
                + [rev(ff), rev(hid), gain_spec, gain_spec]
                + [gates_spec] * mp
                + [mlp_spec] * mp
                + [wout_spec] * mp,
                out_specs=[rev(hid)] * 3
                + [rev(width), rev(ff), rev(width), rev(width), rev(hid), rev(hid)]
                + [ends_spec, fin_spec, sums_spec, sums_spec, bsum_spec],
                out_shape=[t_hb] * 3
                + [t_wb, t_fb, t_wb, t_w, t_hb, t_hb, ends_s, fin_s, sums_s, sums_s, bsum_s],
                scratch_shapes=[kbuf, state, start, row_f32],
                compiler_params=params(),
                cost_estimate=cost(4 * hid + 2 * ff, 60 * 2**20),
                name="block_return",
            )(
                info, inc, ends, began, *keys, xs[l], dx, below[8], below[11], below[1],
                norm_gains[l], norm_gains[l - 1],
                *hid_parts[l], *mlp_parts[l - 1], *hid_parts[l - 1],
            )
            dkf, dki, dkc, dz_next, dpre_next, dout_next, dx, lam, rprod, ends, fin, sums_in, sums_next, bsum = outs
        else:
            outs = pl.pallas_call(
                functools.partial(k_last, mp, len(gates_after)),
                grid=(grid,),
                in_specs=[hbm] * len(gates_after)
                + [smem, fin_spec, ends_spec, start_spec]
                + key_specs
                + [rev(width)] * 2
                + [gain_spec]
                + [gates_spec] * mp,
                out_specs=[rev(hid)] * 3 + [seg_rev, sums_spec, bsum_spec],
                out_shape=[t_hb] * 3 + [sds(SEG, steps, width), sums_s, bsum_s],
                scratch_shapes=[start, row_f32, row_f32, lanes],
                compiler_params=params(),
                cost_estimate=cost(3 * hid, 30 * 2**20),
                name="block_last",
            )(*gates_after, info, inc, ends, began, *keys, xs[l], dx, norm_gains[l], *hid_parts[l])
            dkf, dki, dkc, input_grad, sums_in, bsum = outs
            dz_next = dpre_next = dout_next = sums_next = None
        after = ()
        if held is not None:
            pieces = combine(plan, held, 0)
            after = (pieces[0][0],)
            held = scatter_stage(plan, pieces, 1)
        hid_recv = send_parts(hid_pairs, (nin, dout), (dkf, dki, dkc, hlow), part_h, after)
        after = ()
        if held is not None:
            pieces = combine(plan, held, 1)
            after = (pieces[0][0],)
            held = scatter_stage(plan, pieces, 2)
        pieces = rotate(
            plan, l, all_pairs, (nmid, dz, nin, dout), (dpre, act, dkf, dki, dkc, hlow),
            (mlp_recv, hid_recv), all_blocks, after,
        )
        previous, held = held, scatter_stage(plan, pieces, 0)
        gates_after = (pieces[0][0],)
        if previous is not None:
            previous = scatter_stage(plan, combine(plan, previous, 2, gates_after), 3)
            done = finish(l + 1, previous, done)
        small.append((sums_in, sums_mid, bsum))
        dz, dpre, dout, sums_mid = dz_next, dpre_next, dout_next, sums_next
    small_in = [v for one in reversed(small) for v in one]
    gains, biases = pl.pallas_call(
        k_small,
        in_specs=[vmem] * len(small_in),
        out_specs=[vmem] * 2,
        out_shape=[sds(layers, 2, width), sds(layers, 2, hid)],
        name="small_sums",
    )(*small_in)

    def flat_part(j):
        return jnp.concatenate(
            [gains.reshape(-1, 128), biases[:, :, j * part_h : (j + 1) * part_h].reshape(-1, 128)]
        )

    total = flat_part(0)
    for j in range(1, mp):
        total = total + lax.ppermute(flat_part(j), "mp", [(m, (m + j) % mp) for m in range(mp)])

    def other_half(value, bit):
        return lax.ppermute(value, "dp", [(i, i ^ (1 << bit)) for i in range(dp_count)])

    bits = dp_count.bit_length() - 1
    for at in range(stages - 1):
        pieces, total = combine(plan, held, at, (), (total, other_half(total, at)))
        held = scatter_stage(plan, pieces, at + 1)
    for bit in range(stages - 1, bits):
        total = total + other_half(total, bit)
    total = total.reshape(-1)
    gain_grad = total[: gains.size].reshape(gains.shape)
    bias_grad = total[gains.size :].reshape(layers, 2, part_h)
    done = finish(0, held, done)
    input_grad = input_grad.reshape(1, tokens, width)
    state, (mlp_new, hidden_new), _ = done
    mlp_grad, mlp_first_new, mlp_second_new = state[:3]
    hidden_grad, hidden_first_new, gate_second_new, hidden_second_new = state[3:]
    gain_first_new, gain_second_new, gain_moves = adam_moments(
        gain_grad, gain_first, gain_second, fix_one, fix_two
    )
    bias_first_new, bias_second_new, bias_moves = adam_moments(
        bias_grad, bias_first, bias_second, fix_one, fix_two
    )
    gain_new = norm_gains - GAIN_RATE * gain_moves
    bias_new = gate_bias - BIAS_RATE * bias_moves
    return (
        output,
        input_grad,
        hidden_grad,
        hidden_first_new,
        hidden_second_new,
        gate_second_new,
        hidden_new,
        mlp_grad,
        mlp_first_new,
        mlp_second_new,
        mlp_new,
        gain_grad,
        gain_first_new,
        gain_second_new,
        gain_new,
        bias_grad,
        bias_first_new,
        bias_second_new,
        bias_new,
    )


def solution(mesh):
    in_specs = (
        P("dp", "mp", None),
        P("dp", "mp", None),
        P("dp"),
        P(None, None, None, "mp"),
        P(None, None, None, "mp"),
        P(),
        P(None, None, "mp"),
        P(),
        P(None, None, "mp", None, None),
        P(None, None, "mp", None, None),
        P("dp", None, None, "mp"),
        P("dp", None, None, "mp"),
        P("dp", None, None, "mp"),
        P("dp", None, None, "mp"),
        P(),
        P(),
        P(None, None, "mp"),
        P(None, None, "mp"),
        P(),
        P(),
    )
    out_specs = (
        P("dp", "mp", None),
        P("dp", "mp", None),
        P("dp", None, None, "mp"),
        P("dp", None, None, "mp"),
        P("dp", None, None, "mp"),
        P("dp", None, None, "mp"),
        P(None, None, None, "mp"),
        P("dp", None, None, "mp"),
        P("dp", None, None, "mp"),
        P("dp", None, None, "mp"),
        P(None, None, None, "mp"),
        P(),
        P(),
        P(),
        P(),
        P(None, None, "mp"),
        P(None, None, "mp"),
        P(None, None, "mp"),
        P(None, None, "mp"),
    )
    return jax.shard_map(
        per_device, mesh=mesh, in_specs=in_specs, out_specs=out_specs, check_vma=False
    )
```

```python
import functools
import jax
import jax.numpy as jnp
from jax import lax
from jax.experimental import pallas as pl
from jax.experimental.pallas import tpu as pltpu
from jax.sharding import PartitionSpec as P

NORM_EPS = 1e-05
BETA_ONE = 0.9
BETA_TWO = 0.95
ADAM_EPS = 1e-08
MATRIX_RATE = 0.08
GAIN_RATE = 0.5
BIAS_RATE = 4.0
DECAY_RATE = 0.01
BF = jnp.bfloat16
F32 = jnp.float32
SEG = 8
TILE_STEPS = 64
HC = 256
VMEM_LIMIT = 60 * 1024 * 1024
LOG2E = 1.4426950408889634


def dot_nn(a, b):
    return lax.dot_general(a, b, (((1,), (0,)), ((), ())), preferred_element_type=F32)


def dot_nt(a, b):
    return lax.dot_general(a, b, (((1,), (1,)), ((), ())), preferred_element_type=F32)


def dot_tn(a, b):
    return lax.dot_general(a, b, (((0,), (0,)), ((), ())), preferred_element_type=F32)


def recip(x):
    r = pl.reciprocal(x, approx=True)
    return r * (2.0 - x * r)


def row_blocks(count, size):
    return [slice(at, at + size) for at in range(0, count, size)]


def row_scale(values):
    return lax.rsqrt(jnp.mean(values * values, axis=-1, keepdims=True) + NORM_EPS)


def norm_stage(x_ref, gain, out_ref):
    for r in row_blocks(x_ref.shape[0], 32):
        x = x_ref[r, :]
        out_ref[r, :] = (x * row_scale(x) * gain).astype(BF)


def column_chunks(parts, wide):
    step = min(HC, wide)
    return [(j, c0, j * wide + c0, step) for j in range(parts) for c0 in range(0, wide, step)]


def gate_stage(nin_ref, bias_ref, w_refs, kbuf, state, outs):
    take_ref, loc_ref, prod_ref, cand_ref, wf_ref, wi_ref, q_ref = outs
    for turn, (j, c0, at, wide) in enumerate(column_chunks(len(w_refs), w_refs[0].shape[2])):
        slot = turn % 2
        for k in range(3):
            kbuf[slot, k, :, :wide] = dot_nn(nin_ref[...], w_refs[j][k, :, c0 : c0 + wide])
        cols = slice(at, at + wide)
        bias_f, bias_i = bias_ref[0:1, cols], bias_ref[1:2, cols]
        loc, prod = state[0, :, cols], state[1, :, cols]
        for r in row_blocks(nin_ref.shape[0], 16):
            kf = kbuf[slot, 0, r, :wide] + bias_f
            ki = kbuf[slot, 1, r, :wide] + bias_i
            kc = kbuf[slot, 2, r, :wide]
            tf = jnp.exp(-jnp.abs(kf))
            ti = jnp.exp(-jnp.abs(ki))
            tc = jnp.exp(-jnp.abs(kc))
            gap = jnp.minimum(ki, 0.0) - jnp.minimum(kf, 0.0)
            e = jnp.exp(-jnp.abs(gap))
            ef = jnp.where(gap < 0, e, 1.0)
            ei = jnp.where(gap > 0, e, 1.0)
            nf, ni = ef + ef * tf, ei + ei * ti
            inv = recip(nf + ni)
            keep = ni * inv
            take = nf * inv
            sf = ef * jnp.where(kf >= 0, tf, 1.0)
            si = ei * jnp.where(ki >= 0, ti, 1.0)
            sc = tc * recip(1.0 + tc)
            up = kc >= 0
            cand = jnp.where(up, kc + 0.5, sc)
            slope = jnp.where(up, 1.0, sc - sc * sc)
            take_ref[r, cols] = take.astype(BF)
            cand_ref[r, cols] = cand.astype(BF)
            wf_ref[r, cols] = (keep * inv * sf).astype(BF)
            wi_ref[r, cols] = (take * inv * si).astype(BF)
            q_ref[r, cols] = (take * slope).astype(BF)
            drive = take * cand
            loc0 = keep[:8] * loc + drive[:8]
            prod0 = keep[:8] * prod
            loc = keep[8:] * loc0 + drive[8:]
            prod = keep[8:] * prod0
            loc_ref[r, cols] = jnp.concatenate([loc0, loc]).astype(BF)
            prod_ref[r, cols] = jnp.concatenate([prod0, prod]).astype(BF)
        state[0, :, cols] = loc
        state[1, :, cols] = prod


def fold(state, ends_ref, fin_ref, part, backward):
    hidden = state.shape[2]
    ends_ref[...] = state[...]
    order = list(reversed(range(SEG))) if backward else list(range(SEG))
    value = state[0, order[0] : order[0] + 1, :]
    prod = state[1, order[0] : order[0] + 1, :]
    for s in order[1:]:
        value = state[0, s : s + 1, :] + state[1, s : s + 1, :] * value
        prod = state[1, s : s + 1, :] * prod
    n = hidden // part
    for j in range(n):
        at = ((j - 1) % n if backward else (j + 1) % n) * part
        fin_ref[0:1, j * part : (j + 1) * part] = value[:, at : at + part]
        fin_ref[1:2, j * part : (j + 1) * part] = prod[:, at : at + part]


def carry_forward(inc_ref, ends_ref, start, live):
    start[0:1, :] = inc_ref[0:1, :] * live
    for s in range(SEG - 1):
        start[s + 1 : s + 2, :] = (
            ends_ref[0, s : s + 1, :] + ends_ref[1, s : s + 1, :] * start[s : s + 1, :]
        )


def carry_backward(inc_ref, ends_ref, start, live):
    start[SEG - 1 : SEG, :] = inc_ref[0:1, :] * live
    for s in reversed(range(1, SEG)):
        start[s - 1 : s, :] = (
            ends_ref[0, s : s + 1, :] + ends_ref[1, s : s + 1, :] * start[s : s + 1, :]
        )


def state_stage(start, loc_ref, prod_ref, hlow_ref):
    rows, hidden = loc_ref.shape
    for _, _, at, wide in column_chunks(1, hidden):
        cols = slice(at, at + wide)
        c = jnp.concatenate([start[:, cols], start[:, cols]])
        for r in row_blocks(rows, 16):
            hlow_ref[r, cols] = (loc_ref[r, cols].astype(F32) + prod_ref[r, cols].astype(F32) * c).astype(BF)


def mlp_stage(x_ref, hlow_ref, w_refs, m_refs, gain, kbuf, mid_ref, nmid_ref, act_ref, slope_ref):
    part = w_refs[0].shape[2]
    total = x_ref[...]
    for j, w in enumerate(w_refs):
        total = total + dot_nt(hlow_ref[:, j * part : (j + 1) * part], w[0])
    mid_ref[...] = total
    norm_stage(mid_ref, gain, nmid_ref)
    wide = m_refs[0].shape[2]
    total = mid_ref[...]
    for turn, (j, c0, at, step) in enumerate(column_chunks(len(m_refs), wide)):
        slot = turn % 2
        kbuf[slot, 0, :, :step] = dot_nn(nmid_ref[...], m_refs[j][0, :, c0 : c0 + step])
        cols = slice(at, at + step)
        acts = []
        for r in row_blocks(x_ref.shape[0], 16):
            pre = kbuf[slot, 0, r, :step]
            t = recip(1.0 + jnp.abs(pre) * (0.3275911 * 0.7071067811865476))
            bell = jnp.exp(pre * pre * -0.5)
            poly = (
                (((0.5307027145 * t - 0.7265760135) * t + 0.7107068705) * t - 0.142248368) * t
                + 0.127414796
            ) * t
            tail = poly * bell
            cdf = jnp.where(pre >= 0, 1.0 - tail, tail)
            acts.append((pre * cdf).astype(BF))
            slope_ref[r, cols] = (cdf + pre * (bell * 0.3989422804014327)).astype(BF)
        acts = jnp.concatenate(acts)
        act_ref[:, cols] = acts
        total = total + dot_nt(acts, m_refs[j][1, :, c0 : c0 + step])
    return total


def norm_back_stage(src_ref, gain, dn_ref, dx_ref, sums_ref, low_ref):
    sums = sums_ref[...]
    for r in row_blocks(src_ref.shape[0], 32):
        x = src_ref[r, :]
        scale = row_scale(x)
        unit = x * scale
        d = dn_ref[r, :]
        e = d * gain
        dx = dx_ref[r, :] + scale * (e - unit * jnp.mean(e * unit, axis=-1, keepdims=True))
        dx_ref[r, :] = dx
        if low_ref is not None:
            low_ref[r, :] = dx.astype(BF)
        g = d * unit
        sums = sums + ((g[:8] + g[8:16]) + (g[16:24] + g[24:]))
    sums_ref[...] = sums


def mlp_back_stage(dx_ref, slope_ref, mid_ref, m_refs, gain, dn_ref, dz_ref, dpre_ref, dout_ref, sums_ref):
    dz_ref[...] = dx_ref[...].astype(BF)
    wide = m_refs[0].shape[2]
    for j, c0, at, step in column_chunks(len(m_refs), wide):
        cols = slice(at, at + step)
        dact = dot_nn(dz_ref[...], m_refs[j][1, :, c0 : c0 + step])
        dpre_ref[:, cols] = (dact * slope_ref[:, cols].astype(F32)).astype(BF)
    total = None
    for j, m in enumerate(m_refs):
        term = dot_nt(dpre_ref[:, j * wide : (j + 1) * wide], m[0])
        total = term if total is None else total + term
    dn_ref[...] = total
    norm_back_stage(mid_ref, gain, dn_ref, dx_ref, sums_ref, dout_ref)


def adjoint_stage(dout_ref, w_refs, take_ref, kbuf, state, lam_ref, prod_ref):
    for turn, (j, c0, at, wide) in enumerate(column_chunks(len(w_refs), w_refs[0].shape[2])):
        slot = turn % 2
        kbuf[slot, 0, :, :wide] = dot_nn(dout_ref[...], w_refs[j][0, :, c0 : c0 + wide])
        cols = slice(at, at + wide)
        mu, prod = state[0, :, cols], state[1, :, cols]
        for r in reversed(row_blocks(dout_ref.shape[0], 16)):
            u = kbuf[slot, 0, r, :wide]
            keep = 1.0 - take_ref[r, cols].astype(F32)
            lam1 = u[8:] + mu
            lam0 = u[:8] + keep[8:] * lam1
            mu = keep[:8] * lam0
            prod0 = prod * keep[8:]
            lam_ref[r, cols] = jnp.concatenate([lam0, lam1]).astype(BF)
            prod_ref[r, cols] = jnp.concatenate([prod0, prod]).astype(BF)
            prod = prod0 * keep[:8]
        state[0, :, cols] = mu
        state[1, :, cols] = prod


def keys_stage(first, mu_in, h_in, ins, dk_refs, bias_ref):
    lam_ref, prod_ref, hlow_ref, hbefore_ref, cand_ref, wf_ref, wi_ref, q_ref = ins
    dkf_ref, dki_ref, dkc_ref = dk_refs
    rows, hidden = lam_ref.shape
    for _, _, at, wide in column_chunks(1, hidden):
        cols = slice(at, at + wide)
        c = jnp.concatenate([mu_in[:, cols], mu_in[:, cols]])
        before = jnp.where(first, h_in[:, cols], hbefore_ref[:, cols].astype(F32)[8:])
        sum_f, sum_i = bias_ref[0, :, cols], bias_ref[1, :, cols]
        for r in row_blocks(rows, 16):
            lam = lam_ref[r, cols].astype(F32) + prod_ref[r, cols].astype(F32) * c
            h = hlow_ref[r, cols].astype(F32)
            diff = lam * (cand_ref[r, cols].astype(F32) - jnp.concatenate([before, h[:8]]))
            before = h[8:]
            df = (-(diff * wf_ref[r, cols].astype(F32))).astype(BF)
            di = (diff * wi_ref[r, cols].astype(F32)).astype(BF)
            dkf_ref[r, cols] = df
            dki_ref[r, cols] = di
            dkc_ref[r, cols] = (lam * q_ref[r, cols].astype(F32)).astype(BF)
            df, di = df.astype(F32), di.astype(F32)
            sum_f = sum_f + (df[:8] + df[8:])
            sum_i = sum_i + (di[:8] + di[8:])
        bias_ref[0, :, cols] = sum_f
        bias_ref[1, :, cols] = sum_i


def keys_back_stage(dk_refs, w_refs, dn_ref):
    part = w_refs[0].shape[2]
    total = None
    for j, w in enumerate(w_refs):
        for k in range(3):
            term = dot_nt(dk_refs[k][:, j * part : (j + 1) * part], w[k])
            total = term if total is None else total + term
    dn_ref[...] = total


def spread(src_ref, dst, lanes):
    steps = src_ref.shape[1]
    for c in range(lanes.shape[0]):
        cols = slice(c * 128, c * 128 + 128)
        for s in range(SEG):
            lanes[c, pl.ds(s, steps, stride=SEG), :] = src_ref[s, :, cols].astype(F32)
        dst[:, cols] = lanes[c]


def gather_out(src, dst_ref, lanes):
    steps = dst_ref.shape[1]
    for c in range(lanes.shape[0]):
        cols = slice(c * 128, c * 128 + 128)
        lanes[c] = src[:, cols]
        for s in range(SEG):
            dst_ref[s, :, cols] = lanes[c, pl.ds(s, steps, stride=SEG), :]


def reset(state):
    state[0] = jnp.zeros_like(state[0])
    state[1] = jnp.ones_like(state[1])


def k_cast(*refs):
    half = len(refs) // 2
    for src, dst in zip(refs[:half], refs[half:]):
        dst[...] = src[0].astype(BF)


def k_first(n_parts, in_ref, gain_ref, bias_ref, *refs):
    w = refs[:n_parts]
    xp, nin = refs[n_parts : n_parts + 2]
    gates = refs[n_parts + 2 : n_parts + 9]
    ends, fin, kbuf, state, lanes = refs[n_parts + 9 :]
    g = pl.program_id(0)

    @pl.when(g == 0)
    def _():
        reset(state)

    spread(in_ref, xp, lanes)
    norm_stage(xp, gain_ref[0:1, :], nin)
    gate_stage(nin, bias_ref, w, kbuf, state, gates)

    @pl.when(g == pl.num_programs(0) - 1)
    def _():
        fold(state, ends, fin, w[0].shape[2], False)


def k_middle(n_parts, info, inc, ends_in, x, loc, prod, gain, gain_next, bias, *refs):
    wo = refs[:n_parts]
    m = refs[n_parts : 2 * n_parts]
    w = refs[2 * n_parts : 3 * n_parts]
    hlow, start, mid, nmid, act, slope, xn, nin = refs[3 * n_parts : 3 * n_parts + 8]
    gates = refs[3 * n_parts + 8 : 3 * n_parts + 15]
    ends, fin, kbuf, state = refs[3 * n_parts + 15 :]
    g = pl.program_id(0)

    @pl.when(g == 0)
    def _():
        reset(state)
        carry_forward(inc, ends_in, start, (info[1] > 0).astype(F32))

    state_stage(start, loc, prod, hlow)
    xn[...] = mlp_stage(x, hlow, wo, m, gain[1:2, :], kbuf, mid, nmid, act, slope)
    norm_stage(xn, gain_next[0:1, :], nin)
    gate_stage(nin, bias, w, kbuf, state, gates)

    @pl.when(g == pl.num_programs(0) - 1)
    def _():
        fold(state, ends, fin, w[0].shape[2], False)


def k_turn(n_parts, info, inc, ends_in, x, loc, prod, take, gain, cot, *refs):
    wo = refs[:n_parts]
    m = refs[n_parts : 2 * n_parts]
    (hlow, start, nmid, act, out, dz, dpre, dout, dx, lam, prod_o, ends, fin, sums) = refs[
        2 * n_parts : 2 * n_parts + 14
    ]
    kbuf, state, mid, slope, dn, lanes, out_lanes = refs[2 * n_parts + 14 :]
    g = pl.program_id(0)
    tile = pl.num_programs(0) - 1 - g
    rows = x.shape[0]
    steps_all = pl.num_programs(0) * (rows // SEG)

    @pl.when(g == 0)
    def _():
        reset(state)
        sums[...] = jnp.zeros_like(sums)
        carry_forward(inc, ends_in, start, (info[1] > 0).astype(F32))

    state_stage(start, loc, prod, hlow)
    top = mlp_stage(x, hlow, wo, m, gain[1:2, :], kbuf, mid, nmid, act, slope)
    at = lax.broadcasted_iota(jnp.int32, (rows, 1), 0)
    place = info[1] * (SEG * steps_all) + (at % SEG) * steps_all + tile * (rows // SEG) + at // SEG
    mask = (place < info[0]).astype(F32)
    gather_out(top * mask, out, out_lanes)

    @pl.when(g >= 0)
    def _():
        spread(cot, dx, lanes)
        dx[...] = dx[...] * mask
        mlp_back_stage(dx, slope, mid, m, gain[1:2, :], dn, dz, dpre, dout, sums)
        adjoint_stage(dout, wo, take, kbuf, state, lam, prod_o)

    @pl.when(g == pl.num_programs(0) - 1)
    def _():
        fold(state, ends, fin, wo[0].shape[2], True)


def k_return(n_parts, info, inc, ends_in, h_in, *refs):
    keys = refs[:8]
    x, dx_in, mid, slope, take, gain, gain_prev = refs[8:15]
    refs = refs[15:]
    w = refs[:n_parts]
    m = refs[n_parts : 2 * n_parts]
    wo = refs[2 * n_parts : 3 * n_parts]
    (dkf, dki, dkc, dz, dpre, dout, dx, lam_o, prod_o, ends, fin, sums_in, sums_mid, bias) = refs[
        3 * n_parts : 3 * n_parts + 14
    ]
    kbuf, state, start, dn = refs[3 * n_parts + 14 :]
    g = pl.program_id(0)
    last = pl.num_programs(0) - 1

    @pl.when(g == 0)
    def _():
        reset(state)
        sums_in[...] = jnp.zeros_like(sums_in)
        sums_mid[...] = jnp.zeros_like(sums_mid)
        bias[...] = jnp.zeros_like(bias)
        carry_backward(inc, ends_in, start, (info[1] < info[2] - 1).astype(F32))

    keys_stage(g == last, start, h_in, keys, (dkf, dki, dkc), bias)
    keys_back_stage((dkf, dki, dkc), w, dn)
    dx[...] = dx_in[...]
    norm_back_stage(x, gain[0:1, :], dn, dx, sums_in, None)
    mlp_back_stage(dx, slope, mid, m, gain_prev[1:2, :], dn, dz, dpre, dout, sums_mid)
    adjoint_stage(dout, wo, take, kbuf, state, lam_o, prod_o)

    @pl.when(g == last)
    def _():
        fold(state, ends, fin, wo[0].shape[2], True)


def k_last(n_parts, n_after, *refs):
    info, inc, ends_in, h_in = refs[n_after : n_after + 4]
    refs = refs[n_after + 4 :]
    keys = refs[:8]
    x, dx_in, gain = refs[8:11]
    w = refs[11 : 11 + n_parts]
    dkf, dki, dkc, out, sums_in, bias = refs[11 + n_parts : 17 + n_parts]
    start, dn, dx, lanes = refs[17 + n_parts :]
    g = pl.program_id(0)
    last = pl.num_programs(0) - 1

    @pl.when(g == 0)
    def _():
        sums_in[...] = jnp.zeros_like(sums_in)
        bias[...] = jnp.zeros_like(bias)
        carry_backward(inc, ends_in, start, (info[1] < info[2] - 1).astype(F32))

    keys_stage(g == last, start, h_in, keys, (dkf, dki, dkc), bias)
    keys_back_stage((dkf, dki, dkc), w, dn)
    dx[...] = dx_in[...]
    norm_back_stage(x, gain[0:1, :], dn, dx, sums_in, None)
    gather_out(dx, out, lanes)


def k_grads(pairs, n_after, *refs):
    refs = refs[n_after:]
    out = refs[-1]
    for k, (left, right) in enumerate(pairs):
        out[k] = dot_tn(refs[left][...], refs[right][...]).astype(BF)


def place_of(owner, me, stages):
    if stages is None:
        return owner
    relative = owner ^ me
    place = None
    for low, count in stages:
        digit = (relative >> low) & ((1 << count) - 1)
        place = digit if place is None else (place << count) + digit
    return place


def turn_blocks(value, blocks, inverse):
    order = blocks.shape[-1]
    dot = dot_nt if inverse else dot_nn
    return jnp.concatenate(
        [
            dot(value[:, b * order : (b + 1) * order], blocks[0, 0, b].astype(BF))
            for b in range(blocks.shape[2])
        ],
        axis=1,
    )


def k_rotate(plan, n_recv, pairs, n_after, who, basis, *refs):
    refs = refs[n_after:]
    n_src = len(plan.sources)
    n_left, n_right = 1 + max(p[0] for p in pairs), len(pairs)
    blocks = refs[:n_src]
    recv = refs[n_src : n_src * (1 + n_recv)]
    refs = refs[n_src * (1 + n_recv) :]
    lefts, rights = refs[:n_left], refs[n_left : n_left + n_right]
    refs = refs[n_left + n_right :]
    n_out = sum(plan.firsts)
    outs, bufs = refs[:n_out], refs[n_out:]
    g = pl.program_id(0)
    share = plan.share
    width = basis.shape[2]
    count = width // share
    for chunk, runs in enumerate(plan.runs):
        at, pair = plan.source_of[chunk], pairs[plan.matrix_of[chunk]]

        @pl.when(g == chunk)
        def _(runs=runs, at=at, pair=pair):
            total = dot_tn(lefts[pair[0]][...], rights[pair[1]][...])
            for ref in recv[at * n_recv : (at + 1) * n_recv]:
                total = total + ref[0].astype(F32)
            turned = turn_blocks(total.astype(BF), blocks[at], False).astype(BF)
            done = dot_tn(basis[0, 0].astype(BF), turned).astype(BF)
            for b in range(count):
                for stream, src, dst, wide in runs:
                    row = place_of(who[b], who[count], plan.stages[stream]) * share
                    bufs[stream][pl.ds(pl.multiple_of(row, share), share), dst : dst + wide] = done[
                        b * share : (b + 1) * share, src : src + wide
                    ]

    @pl.when(g == pl.num_programs(0) - 1)
    def _():
        at = 0
        for stream, pieces in enumerate(plan.firsts):
            rows = width // pieces
            for r in range(pieces):
                outs[at][...] = bufs[stream][r * rows : (r + 1) * rows, :]
                at += 1


def sum_pieces(refs):
    total = refs[0][...].astype(F32)
    for ref in refs[1:]:
        total = total + ref[...].astype(F32)
    return total


def k_combine(n_in, n_out, n_after, n_small, *refs):
    refs = refs[n_after:]
    if n_small:
        at = sum(n_in)
        refs[-1][...] = refs[at][...] + refs[at + 1][...]
        refs = refs[:at] + refs[at + 2 : -1]
    i, o = 0, sum(n_in)
    for take, give in zip(n_in, n_out):
        total = sum_pieces(refs[i : i + take]).astype(BF)
        rows = total.shape[0] // give
        for r in range(give):
            refs[o + r][...] = total[r * rows : (r + 1) * rows, :]
        i += take
        o += give


def k_join(n_in, n_after, *refs):
    refs = refs[n_after:]
    outs = refs[sum(n_in) :]
    i = 0
    for out, take in zip(outs, n_in):
        rows = refs[i].shape[0]
        for r in range(take):
            out[r * rows : (r + 1) * rows, :] = refs[i + r][...]
        i += take


def k_adam(plan, spread_plan, splits, n_alias, fix, *refs):
    n_in = sum(plan.lasts)
    n_src = len(plan.sources)
    pieces = refs[:n_in]
    olds = refs[n_in : n_in + 2 * n_src]
    outs = refs[n_in + 2 * n_src + n_alias :]
    bufs = refs[len(refs) - n_src :]
    moves_o = outs[sum(2 + len(split) for split in splits) :][: len(spread_plan.stages)]
    sums, i = [], 0
    for take in plan.lasts:
        sums.append(sum_pieces(pieces[i : i + take]))
        i += take
    o = 0
    for at, split in enumerate(splits):
        grad_o, first_o = outs[o : o + 2]
        second_o = outs[o + 2 : o + 2 + len(split)]
        o += 2 + len(split)
        first, second = olds[2 * at : 2 * at + 2]
        for chunk in range(plan.begins[at], plan.begins[at + 1]):
            kind, base = plan.where(at, chunk)
            for stream, src, dst, wide in plan.runs[chunk]:
                grad_o[:, 0, kind, base + src : base + src + wide] = sums[stream][:, dst : dst + wide]
        grad = grad_o[...]
        one = BETA_ONE * first[...] + (1.0 - BETA_ONE) * grad
        two = BETA_TWO * second[...] + (1.0 - BETA_TWO) * grad * grad
        first_o[...] = one
        for ref, (lo, hi) in zip(second_o, split):
            ref[...] = two[:, :, lo:hi, :]
        bufs[at][...] = one * fix[0] / (jnp.sqrt(two * fix[1]) + ADAM_EPS)
        for chunk in range(plan.begins[at], plan.begins[at + 1]):
            kind, base = plan.where(at, chunk)
            for stream, src, dst, wide in spread_plan.runs[chunk]:
                moves_o[stream][:, dst : dst + wide] = bufs[at][
                    :, 0, kind, base + src : base + src + wide
                ].astype(BF)


def k_apply(plan, n_alias, who, basis, *refs):
    n_src = len(plan.sources)
    n_in = sum(plan.firsts)
    blocks = refs[:n_src]
    weights = refs[n_src : 2 * n_src]
    pieces = refs[2 * n_src : 2 * n_src + n_in]
    outs = refs[2 * n_src + n_in + n_alias :][:n_src]
    bufs = refs[2 * n_src + n_in + n_alias + n_src : -1]
    moves = refs[-1]
    g = pl.program_id(0)
    share = plan.share
    width = basis.shape[2]
    count = width // share

    @pl.when(g == 0)
    def _():
        at = 0
        for stream, n in enumerate(plan.firsts):
            rows = width // n
            for r in range(n):
                bufs[stream][r * rows : (r + 1) * rows, :] = pieces[at][...]
                at += 1

    for chunk, runs in enumerate(plan.runs):

        @pl.when(g == chunk)
        def _(runs=runs):
            for stream, src, dst, wide in runs:
                for b in range(count):
                    at = place_of(who[b], who[count], plan.stages[stream]) * share
                    moves[b * share : (b + 1) * share, src : src + wide] = bufs[stream][
                        pl.ds(pl.multiple_of(at, share), share), dst : dst + wide
                    ]

    for at in range(n_src):

        @pl.when((g >= plan.begins[at]) & (g < plan.begins[at + 1]))
        def _(at=at):
            wide = plan.blocks[at]
            back = dot_nn(basis[0, 0].astype(BF), moves[:, :wide]).astype(BF)
            step = turn_blocks(back, blocks[at], True)
            old = weights[at][0, 0]
            outs[at][0, 0] = old - MATRIX_RATE * (step + DECAY_RATE * old)


class Plan:
    def __init__(self, dp_count, width, sources, staged=True):
        bits = dp_count.bit_length() - 1
        x, y, z, rest = (0, 1), (1, 1), (2, 1), (3, bits - 3)
        orders = [[x, y, z, rest], [y, x, z, rest], [z, rest, x, y]]
        self.share = width // dp_count
        self.sources = sources
        self.blocks = [min(512, wide) for _, _, wide in sources]
        self.pers = [wide // block for (_, _, wide), block in zip(sources, self.blocks)]
        self.begins = [0]
        for (_, count, _), per in zip(sources, self.pers):
            self.begins.append(self.begins[-1] + count * per)
        self.source_of, self.matrix_of = [], []
        matrices = 0
        for at, (_, count, _) in enumerate(sources):
            for k in range(count):
                self.source_of += [at] * self.pers[at]
                self.matrix_of += [matrices + k] * self.pers[at]
            matrices += count
        named = []
        for at, block in enumerate(self.blocks):
            for chunk in range(self.begins[at], self.begins[at + 1]):
                named.append([0 if not staged else 2 if lane == 3 else chunk % 2 for lane in range(block // 128)])
        used = sorted({stream for row in named for stream in row})
        self.stages = [orders[stream] if staged else None for stream in used]
        self.cols = [0] * len(used)
        self.runs = []
        for row in named:
            runs = []
            for lane, stream in enumerate(row):
                at = used.index(stream)
                if runs and runs[-1][0] == at:
                    runs[-1][3] += 128
                else:
                    runs.append([at, lane * 128, self.cols[at], 128])
                self.cols[at] += 128
            self.runs.append(runs)
        self.firsts = [1 << stages[0][1] if staged else 1 for stages in self.stages]
        self.lasts = [1 << stages[-1][1] if staged else 1 for stages in self.stages]

    def where(self, at, chunk):
        local = chunk - self.begins[at]
        return local // self.pers[at], local % self.pers[at] * self.blocks[at]

    def local(self, at, g):
        return jnp.clip(g - self.begins[at], 0, self.begins[at + 1] - self.begins[at] - 1)

    def basis_at(self, g):
        index = None
        for at, (base, _, _) in enumerate(self.sources):
            here = base + self.local(at, g) // self.pers[at]
            index = here if index is None else jnp.where(g < self.begins[at], index, here)
        return index


def k_small(*refs):
    gains, biases = refs[-2:]
    for l in range(gains.shape[0]):
        sums_in, sums_mid, bias = refs[3 * l : 3 * l + 3]
        gains[l, 0:1, :] = jnp.sum(sums_in[...], axis=0, keepdims=True)
        gains[l, 1:2, :] = jnp.sum(sums_mid[...], axis=0, keepdims=True)
        for k in range(2):
            biases[l, k : k + 1, :] = jnp.sum(bias[k], axis=0, keepdims=True)


def adam_moments(grads, first, second, fix_one, fix_two):
    first = BETA_ONE * first + (1.0 - BETA_ONE) * grads
    second = BETA_TWO * second + (1.0 - BETA_TWO) * grads * grads
    moves = first / fix_one / (jnp.sqrt(second / fix_two) + ADAM_EPS)
    return (first, second, moves)


def params(parallel=False):
    return pltpu.CompilerParams(
        dimension_semantics=("arbitrary",), vmem_limit_bytes=VMEM_LIMIT
    )


def sds(*shape, dtype=F32):
    return jax.ShapeDtypeStruct(shape, dtype)


def per_device(
    inputs,
    cotangent,
    lengths,
    hidden_weights,
    mlp_weights,
    norm_gains,
    gate_bias,
    left_bases,
    hidden_blocks,
    mlp_blocks,
    hidden_first,
    hidden_second,
    mlp_first,
    mlp_second,
    gain_first,
    gain_second,
    bias_first,
    bias_second,
    step_count,
    row_owner,
):
    dp_count = lax.axis_size("dp")
    mp = lax.axis_size("mp")
    me = lax.axis_index("mp")
    tokens = inputs.shape[1]
    width = inputs.shape[2]
    part_h = hidden_weights.shape[3]
    part_f = mlp_weights.shape[3]
    hid = part_h * mp
    ff = part_f * mp
    layers = hidden_weights.shape[0]
    steps = tokens // SEG
    ts = min(TILE_STEPS, steps)
    tr = ts * SEG
    grid = steps // ts
    share = width // dp_count

    def from_peer(value, j):
        return lax.ppermute(value, "mp", [((m + j) % mp, m) for m in range(mp)])

    def to_next(value):
        return lax.ppermute(value, "mp", [(m, (m + 1) % mp) for m in range(mp)])

    def to_prev(value):
        return lax.ppermute(value, "mp", [((m + 1) % mp, m) for m in range(mp)])

    def cast(picks):
        in_specs, out_specs, shapes = [], [], []
        for weights, l in picks:
            _, count, _, wide = weights.shape
            per = 4 // count
            in_specs.append(
                pl.BlockSpec((1, 1, width, wide // per), lambda g, l=l, per=per: (l, g // per, 0, g % per))
            )
            out_specs.append(pl.BlockSpec((1, width, wide // per), lambda g, per=per: (g // per, 0, g % per)))
            shapes.append(sds(count, width, wide, dtype=BF))
        return pl.pallas_call(
            k_cast,
            grid=(4,),
            in_specs=in_specs,
            out_specs=out_specs,
            out_shape=shapes,
            compiler_params=params(),
            cost_estimate=pl.CostEstimate(flops=0, bytes_accessed=6 * len(picks) * 2**20, transcendentals=0),
            name="cast",
        )(*[weights for weights, _ in picks])

    def with_peers(own):
        return [own] + [from_peer(own, j) for j in range(1, mp)]

    own = cast([(hidden_weights, 0)])
    own += cast([(mlp_weights, 0)] + [(w, l) for l in range(1, layers) for w in (hidden_weights, mlp_weights)])
    hid_parts = [with_peers(own[2 * l]) for l in range(layers)]
    mlp_parts = [with_peers(own[2 * l + 1]) for l in range(layers)]
    bias_all = jnp.concatenate([gate_bias] + [from_peer(gate_bias, j) for j in range(1, mp)], axis=2)
    info = jnp.stack([lengths[0], me, jnp.int32(mp)]).astype(jnp.int32)

    def make_specs(order):
        def tile(cols):
            return pl.BlockSpec((tr, cols), lambda g: (order(g), 0))

        return tile

    def whole(*shape):
        return pl.BlockSpec(shape, lambda g: (0,) * len(shape), pipeline_mode=pl.Buffered(1))

    smem = pl.BlockSpec(memory_space=pltpu.SMEM)
    vmem = pl.BlockSpec(memory_space=pltpu.VMEM)
    hbm = pl.BlockSpec(memory_space=pl.ANY)
    fwd = make_specs(lambda g: g)
    rev = make_specs(lambda g: grid - 1 - g)
    seg_fwd = pl.BlockSpec((SEG, ts, width), lambda g: (0, g, 0))
    seg_rev = pl.BlockSpec((SEG, ts, width), lambda g: (0, grid - 1 - g, 0))
    before_rev = pl.BlockSpec(
        (16, hid), lambda g: (jnp.maximum((grid - 1 - g) * (tr // 16) - 1, 0), 0)
    )
    start_spec = pl.BlockSpec((SEG, hid), lambda g: (0, 0))
    gates_spec = pl.BlockSpec((3, width, part_h), lambda g: (0, 0, 0), pipeline_mode=pl.Buffered(1))
    wout_spec = pl.BlockSpec((1, width, part_h), lambda g: (3, 0, 0), pipeline_mode=pl.Buffered(1))
    mlp_spec = whole(2, width, part_f)
    gain_spec = whole(2, width)
    bias_spec = whole(2, hid)
    ends_spec = pl.BlockSpec((2, SEG, hid), lambda g: (0, 0, 0))
    fin_spec = pl.BlockSpec((2, hid), lambda g: (0, 0))
    sums_spec = pl.BlockSpec((SEG, width), lambda g: (0, 0))
    bsum_spec = pl.BlockSpec((2, SEG, hid), lambda g: (0, 0, 0))
    kbuf = pltpu.VMEM((2, 3, tr, min(HC, max(part_h, part_f))), F32)
    state = pltpu.VMEM((2, SEG, hid), F32)
    start = pltpu.VMEM((SEG, hid), F32)
    row_f32 = pltpu.VMEM((tr, width), F32)
    lanes = pltpu.VMEM((width // 128, tr, 128), F32)

    t_w = sds(tokens, width)
    t_wb = sds(tokens, width, dtype=BF)
    t_hb = sds(tokens, hid, dtype=BF)
    t_fb = sds(tokens, ff, dtype=BF)
    ends_s = sds(2, SEG, hid)
    start_s = sds(SEG, hid)
    fin_s = sds(2, hid)
    sums_s = sds(SEG, width)
    bsum_s = sds(2, SEG, hid)

    def cost(matmul_cols, elems):
        return pl.CostEstimate(
            flops=2 * tokens * width * matmul_cols,
            bytes_accessed=elems,
            transcendentals=0,
        )

    def chain(fin, send, shift, live):
        carry = send(fin)
        for _ in range(mp - 2):
            known = jnp.roll(carry[0:1] * live, shift, axis=1)
            carry = send(jnp.concatenate([fin[0:1] + fin[1:2] * known, fin[1:2]]))
        return carry

    def chain_forward(fin):
        return chain(fin, to_next, -part_h, (me > 0).astype(F32))

    def chain_backward(fin):
        return chain(fin, to_prev, part_h, (me < mp - 1).astype(F32))

    seg_in = inputs.reshape(SEG, steps, width)
    seg_cot = cotangent.reshape(SEG, steps, width)
    saved = []
    f1_out_specs = lambda t: [t(width)] + [t(hid)] * 7 + [ends_spec, fin_spec]
    f1_out_shapes = [t_wb] + [t_hb] * 7 + [ends_s, fin_s]
    outs = pl.pallas_call(
        functools.partial(k_first, mp),
        grid=(grid,),
        in_specs=[seg_fwd, gain_spec, bias_spec] + [gates_spec] * mp,
        out_specs=[fwd(width)] + f1_out_specs(fwd),
        out_shape=[t_w] + f1_out_shapes,
        scratch_shapes=[kbuf, state, lanes],
        compiler_params=params(),
        cost_estimate=cost(3 * hid, 24 * 2**20),
        name="gates_first",
    )(seg_in, norm_gains[0], bias_all[0], *hid_parts[0])
    x, gate = outs[0], outs[1:]
    xs = [x]
    for l in range(layers - 1):
        nin, take, loc, prod, cand, wf, wi, q, ends, fin = gate
        inc = chain_forward(fin)
        outs = pl.pallas_call(
            functools.partial(k_middle, mp),
            grid=(grid,),
            in_specs=[smem, fin_spec, ends_spec, fwd(width), fwd(hid), fwd(hid)]
            + [gain_spec, gain_spec, bias_spec]
            + [wout_spec] * mp
            + [mlp_spec] * mp
            + [gates_spec] * mp,
            out_specs=[fwd(hid), start_spec] + [fwd(width)] * 2 + [fwd(ff)] * 2 + [fwd(width)] + f1_out_specs(fwd),
            out_shape=[t_hb, start_s, t_w, t_wb, t_fb, t_fb, t_w] + f1_out_shapes,
            scratch_shapes=[kbuf, state],
            compiler_params=params(),
            cost_estimate=cost(4 * hid + 2 * ff, 60 * 2**20),
            name="block_forward",
        )(
            info, inc, ends, xs[l], loc, prod,
            norm_gains[l], norm_gains[l + 1], bias_all[l + 1],
            *hid_parts[l], *mlp_parts[l], *hid_parts[l + 1],
        )
        hlow, began, mid, nmid, act, slope, xn = outs[:7]
        saved.append((nin, take, hlow, began, cand, wf, wi, q, mid, nmid, act, slope))
        xs.append(xn)
        gate = outs[7:]
    top = layers - 1
    nin, take, loc, prod, cand, wf, wi, q, ends, fin = gate
    inc = chain_forward(fin)
    outs = pl.pallas_call(
        functools.partial(k_turn, mp),
        grid=(grid,),
        in_specs=[smem, fin_spec, ends_spec, rev(width), rev(hid), rev(hid), rev(hid)]
        + [gain_spec, seg_rev]
        + [wout_spec] * mp
        + [mlp_spec] * mp,
        out_specs=[rev(hid), start_spec, rev(width), rev(ff), seg_rev, rev(width), rev(ff), rev(width), rev(width)]
        + [rev(hid), rev(hid), ends_spec, fin_spec, sums_spec],
        out_shape=[t_hb, start_s, t_wb, t_fb, sds(SEG, steps, width), t_wb, t_fb, t_wb, t_w]
        + [t_hb, t_hb, ends_s, fin_s, sums_s],
        scratch_shapes=[kbuf, state, row_f32, pltpu.VMEM((tr, ff), BF), row_f32, lanes, lanes],
        compiler_params=params(),
        cost_estimate=cost(2 * hid + 4 * ff, 60 * 2**20),
        name="block_turn",
    )(
        info, inc, ends, xs[top], loc, prod, take, norm_gains[top], seg_cot,
        *hid_parts[top], *mlp_parts[top],
    )
    hlow, began, nmid, act, output, dz, dpre, dout, dx, lam, rprod, ends, fin, sums_mid = outs
    output = output.reshape(1, tokens, width)
    saved.append((nin, take, hlow, began, cand, wf, wi, q, None, nmid, act, None))

    def weight_grads(pairs, lefts, rights, part, wide, after):
        count = len(pairs)
        block = min(256, wide)
        per = wide // block
        in_specs = [whole(tokens, width) for _ in lefts]
        in_specs += [pl.BlockSpec((tokens, block), lambda g: (0, part * per + g)) for _ in rights]
        shifted = tuple((left, len(lefts) + right) for left, right in pairs)
        return pl.pallas_call(
            functools.partial(k_grads, shifted, len(after)),
            grid=(per,),
            in_specs=[hbm] * len(after) + in_specs,
            out_specs=pl.BlockSpec((count, width, block), lambda g: (0, 0, g)),
            out_shape=sds(count, width, wide, dtype=BF),
            compiler_params=params(),
            cost_estimate=cost(count * wide, tokens * wide * count * 2),
            name="weight_grads",
        )(*after, *lefts, *rights)

    def send_parts(pairs, lefts, rights, wide, after=()):
        others = []
        for j in range(1, mp):
            sent = weight_grads(pairs, lefts, rights, j, wide, after)
            others.append(lax.ppermute(sent, "mp", [(m, (m + j) % mp) for m in range(mp)]))
        return others

    dp_me = lax.axis_index("dp")
    who = jnp.concatenate([row_owner, dp_me[None].astype(jnp.int32)])
    count_value = step_count[0].astype(F32)
    fix_one = 1.0 - jnp.power(jnp.float32(BETA_ONE), count_value)
    fix_two = 1.0 - jnp.power(jnp.float32(BETA_TWO), count_value)
    fix = jnp.stack([1.0 / fix_one, 1.0 / fix_two])

    def exchange(value, stage):
        low, count = stage
        return [
            lax.ppermute(value, "dp", [(i, i ^ (r << low)) for i in range(dp_count)])
            for r in range(1, 1 << count)
        ]

    def source_spec(plan, at, shape, tail):
        return pl.BlockSpec(shape, lambda g: tail(plan.local(at, g) // plan.pers[at], plan.local(at, g) % plan.pers[at]))

    def rotate(plan, l, pairs, lefts, rights, recv, blocks, after):
        basis_spec = pl.BlockSpec((1, 1, width, width), lambda g: (l, plan.basis_at(g), 0, 0))
        specs, flat = [], []
        for at, one in enumerate(blocks):
            order = one.shape[-1]
            nb = plan.blocks[at] // order
            specs.append(source_spec(plan, at, (1, 1, nb, order, order), lambda k, c: (l, k, c, 0, 0)))
        for at, ones in enumerate(recv):
            for one in ones:
                specs.append(source_spec(plan, at, (1, width, plan.blocks[at]), lambda k, c: (k, 0, c)))
                flat.append(one)
        specs += [whole(tokens, width)] * len(lefts)
        for m in range(len(rights)):
            at = plan.source_of[plan.matrix_of.index(m)]
            first = plan.matrix_of.index(m)
            last = plan.pers[at] - 1
            specs.append(
                pl.BlockSpec(
                    (tokens, plan.blocks[at]), lambda g, first=first, last=last: (0, jnp.clip(g - first, 0, last))
                )
            )
        out_shapes = [
            sds(width // n, cols, dtype=BF) for n, cols in zip(plan.firsts, plan.cols) for _ in range(n)
        ]
        outs = pl.pallas_call(
            functools.partial(k_rotate, plan, mp - 1, pairs, len(after)),
            grid=(plan.begins[-1],),
            in_specs=[smem, basis_spec] + [hbm] * len(after) + specs,
            out_specs=[pl.BlockSpec(o.shape, lambda g: (0, 0)) for o in out_shapes],
            out_shape=out_shapes,
            scratch_shapes=[pltpu.VMEM((width, cols), BF) for cols in plan.cols],
            compiler_params=params(),
            cost_estimate=cost(6 * sum(plan.cols), 24 * 2**20),
            name="rotate",
        )(who, left_bases, *after, *blocks, *flat, *lefts, *rights)
        pieces, at = [], 0
        for n in plan.firsts:
            pieces.append(outs[at : at + n])
            at += n
        return pieces

    def scatter_stage(plan, pieces, at):
        held = []
        for stages, mine in zip(plan.stages, pieces):
            low, count = stages[at]
            got = [
                lax.ppermute(mine[r], "dp", [(i, i ^ (r << low)) for i in range(dp_count)])
                for r in range(1, 1 << count)
            ]
            held.append([mine[0]] + got)
        return held

    def combine(plan, held, at, after=(), small=()):
        flat = [v for one in held for v in one]
        n_in = [len(one) for one in held]
        n_out = [1 << stages[at + 1][1] for stages in plan.stages]
        shapes = [
            sds(one[0].shape[0] // n, one[0].shape[1], dtype=BF) for one, n in zip(held, n_out) for _ in range(n)
        ]
        halves = 2 if all(cols % 256 == 0 for cols in plan.cols) else 1

        def part_of(shape):
            return pl.BlockSpec((shape[0], shape[1] // halves), lambda g: (0, g))

        small_specs = [pl.BlockSpec(v.shape, lambda g: (0, 0)) for v in small]
        outs = pl.pallas_call(
            functools.partial(k_combine, n_in, n_out, len(after), len(small)),
            grid=(halves,),
            in_specs=[hbm] * len(after) + [part_of(v.shape) for v in flat] + small_specs,
            out_specs=[part_of(v.shape) for v in shapes] + small_specs[:1],
            out_shape=shapes + [sds(*v.shape) for v in small[:1]],
            compiler_params=params(),
            cost_estimate=pl.CostEstimate(flops=0, bytes_accessed=6 * 2**20, transcendentals=0),
            name="combine",
        )(*after, *flat, *small)
        if small:
            return [outs[sum(n_out[:i]) : sum(n_out[: i + 1])] for i in range(len(n_out))], outs[-1]
        pieces, i = [], 0
        for n in n_out:
            pieces.append(outs[i : i + n])
            i += n
        return pieces

    def adam(plan, spread_plan, l, held, olds, splits, before):
        flat = [v for one in held for v in one]
        out_specs, shapes, in_specs, bufs = [], [], [], []
        for (_, count, wide), split in zip(plan.sources, splits):
            for lo, hi in ((0, count),) * 2 + split:
                out_specs.append(pl.BlockSpec((share, 1, hi - lo, wide), lambda g: (0, l, 0, 0)))
                shapes.append(sds(share, layers, hi - lo, wide))
            in_specs += [pl.BlockSpec((share, 1, count, wide), lambda g: (0, l, 0, 0))] * 2
            bufs.append(pltpu.VMEM((share, 1, count, wide), F32))
        n_state = len(shapes)
        before = before or ()
        outs = pl.pallas_call(
            functools.partial(k_adam, plan, spread_plan, splits, len(before)),
            grid=(1,),
            in_specs=[smem] + [vmem] * len(flat) + in_specs + [hbm] * len(before),
            out_specs=out_specs + [vmem] * len(spread_plan.cols),
            out_shape=shapes + [sds(share, cols, dtype=BF) for cols in spread_plan.cols],
            scratch_shapes=bufs,
            input_output_aliases={1 + len(flat) + len(olds) + i: i for i in range(len(before))},
            compiler_params=pltpu.CompilerParams(vmem_limit_bytes=VMEM_LIMIT),
            cost_estimate=pl.CostEstimate(flops=0, bytes_accessed=8 * 2**20, transcendentals=0),
            name="adam",
        )(fix, *flat, *olds, *before)
        return tuple(outs[:n_state]), outs[n_state:]

    def gather_moves(plan, moves, after=()):
        held = []
        for stages, value in zip(plan.stages, moves):
            for stage in reversed(stages[2:]):
                value = jnp.concatenate([value] + exchange(value, stage), axis=0)
            held.append([value] + exchange(value, stages[1]))
        halves = 2 if all(cols % 256 == 0 for cols in plan.cols) else 1
        ins = [v for one in held for v in one]
        shapes = [sds(one[0].shape[0] * len(one), one[0].shape[1], dtype=BF) for one in held]

        def part_of(shape):
            return pl.BlockSpec((shape[0], shape[1] // halves), lambda g: (0, g))

        joined = pl.pallas_call(
            functools.partial(k_join, [len(one) for one in held], len(after)),
            grid=(halves,),
            in_specs=[hbm] * len(after) + [part_of(v.shape) for v in ins],
            out_specs=[part_of(v.shape) for v in shapes],
            out_shape=shapes,
            compiler_params=params(),
            cost_estimate=pl.CostEstimate(flops=0, bytes_accessed=4 * 2**20, transcendentals=0),
            name="join",
        )(*after, *ins)
        return [v for stages, value in zip(plan.stages, joined) for v in [value] + exchange(value, stages[0])]

    def apply_moves(plan, l, flat, blocks, weights, before):
        basis_spec = pl.BlockSpec((1, 1, width, width), lambda g: (l, plan.basis_at(g), 0, 0))
        block_specs, specs = [], []
        for at, one in enumerate(blocks):
            order = one.shape[-1]
            nb = plan.blocks[at] // order
            block_specs.append(source_spec(plan, at, (1, 1, nb, order, order), lambda k, c: (l, k, c, 0, 0)))
            specs.append(source_spec(plan, at, (1, 1, width, plan.blocks[at]), lambda k, c: (l, k, 0, c)))
        before = before or ()
        ins = 2 + 2 * len(blocks) + len(flat)
        return tuple(
            pl.pallas_call(
                functools.partial(k_apply, plan, len(before)),
                grid=(plan.begins[-1],),
                in_specs=[smem, basis_spec]
                + block_specs
                + specs
                + [whole(*v.shape) for v in flat]
                + [hbm] * len(before),
                out_specs=specs,
                out_shape=[sds(*w.shape) for w in weights],
                scratch_shapes=[pltpu.VMEM((width, cols), BF) for cols in plan.cols]
                + [pltpu.VMEM((width, max(plan.blocks)), BF)],
                input_output_aliases={ins + i: i for i in range(len(before))},
                compiler_params=params(),
                cost_estimate=cost(2 * sum(plan.cols), 24 * 2**20),
                name="apply_moves",
            )(who, left_bases, *blocks, *weights, *flat, *before)
        )

    plan = Plan(dp_count, width, ((4, 2, part_f), (0, 4, part_h)))
    plain = Plan(dp_count, width, plan.sources, staged=False)
    olds = (mlp_first, mlp_second, hidden_first, hidden_second)
    splits = (((0, 2),), ((0, 2), (2, 4)))

    all_blocks = (mlp_blocks, hidden_blocks)
    stages = len(plan.stages[0])
    mlp_pairs = ((0, 0), (1, 1))
    hid_pairs = ((0, 0), (0, 1), (0, 2), (1, 3))
    all_pairs = tuple(mlp_pairs) + tuple((left + 2, right + 2) for left, right in hid_pairs)

    def finish(l, held, before):
        state, new = before[:2] if before else (None, None)
        back = plan
        state, moves = adam(plan, back, l, held, olds, splits, state)
        flat = gather_moves(back, moves, new[:1] if new else ())
        return state, apply_moves(back, l, flat, all_blocks, (mlp_weights, hidden_weights), new), moves[0]

    done = None
    held = None
    small = []
    gates_after = ()
    for l in reversed(range(layers)):
        nin, take, hlow, began, cand, wf, wi, q, mid, nmid, act, slope = saved[l]
        keys = (lam, rprod, hlow, hlow, cand, wf, wi, q)
        key_specs = [rev(hid)] * 3 + [before_rev] + [rev(hid)] * 4
        inc = chain_backward(fin)
        mlp_recv = send_parts(mlp_pairs, (nmid, dz), (dpre, act), part_f, gates_after)
        if l > 0:
            below = saved[l - 1]
            outs = pl.pallas_call(
                functools.partial(k_return, mp),
                grid=(grid,),
                in_specs=[smem, fin_spec, ends_spec, start_spec]
                + key_specs
                + [rev(width)] * 3
                + [rev(ff), rev(hid), gain_spec, gain_spec]
                + [gates_spec] * mp
                + [mlp_spec] * mp
                + [wout_spec] * mp,
                out_specs=[rev(hid)] * 3
                + [rev(width), rev(ff), rev(width), rev(width), rev(hid), rev(hid)]
                + [ends_spec, fin_spec, sums_spec, sums_spec, bsum_spec],
                out_shape=[t_hb] * 3
                + [t_wb, t_fb, t_wb, t_w, t_hb, t_hb, ends_s, fin_s, sums_s, sums_s, bsum_s],
                scratch_shapes=[kbuf, state, start, row_f32],
                compiler_params=params(),
                cost_estimate=cost(4 * hid + 2 * ff, 60 * 2**20),
                name="block_return",
            )(
                info, inc, ends, began, *keys, xs[l], dx, below[8], below[11], below[1],
                norm_gains[l], norm_gains[l - 1],
                *hid_parts[l], *mlp_parts[l - 1], *hid_parts[l - 1],
            )
            dkf, dki, dkc, dz_next, dpre_next, dout_next, dx, lam, rprod, ends, fin, sums_in, sums_next, bsum = outs
        else:
            outs = pl.pallas_call(
                functools.partial(k_last, mp, len(gates_after)),
                grid=(grid,),
                in_specs=[hbm] * len(gates_after)
                + [smem, fin_spec, ends_spec, start_spec]
                + key_specs
                + [rev(width)] * 2
                + [gain_spec]
                + [gates_spec] * mp,
                out_specs=[rev(hid)] * 3 + [seg_rev, sums_spec, bsum_spec],
                out_shape=[t_hb] * 3 + [sds(SEG, steps, width), sums_s, bsum_s],
                scratch_shapes=[start, row_f32, row_f32, lanes],
                compiler_params=params(),
                cost_estimate=cost(3 * hid, 30 * 2**20),
                name="block_last",
            )(*gates_after, info, inc, ends, began, *keys, xs[l], dx, norm_gains[l], *hid_parts[l])
            dkf, dki, dkc, input_grad, sums_in, bsum = outs
            dz_next = dpre_next = dout_next = sums_next = None
        after = ()
        if held is not None:
            pieces = combine(plan, held, 0)
            after = (pieces[0][0],)
            held = scatter_stage(plan, pieces, 1)
        hid_recv = send_parts(hid_pairs, (nin, dout), (dkf, dki, dkc, hlow), part_h, after)
        early = after
        pieces = rotate(
            plan, l, all_pairs, (nmid, dz, nin, dout), (dpre, act, dkf, dki, dkc, hlow),
            (mlp_recv, hid_recv), all_blocks, early,
        )
        previous, held = held, scatter_stage(plan, pieces, 0)
        gates_after = (pieces[0][0],)
        if previous is not None:
            previous = scatter_stage(plan, combine(plan, previous, 1, gates_after), 2)
            previous = scatter_stage(plan, combine(plan, previous, 2), 3)
            done = finish(l + 1, previous, done)
        small.append((sums_in, sums_mid, bsum))
        dz, dpre, dout, sums_mid = dz_next, dpre_next, dout_next, sums_next
    small_in = [v for one in reversed(small) for v in one]
    gains, biases = pl.pallas_call(
        k_small,
        in_specs=[vmem] * len(small_in),
        out_specs=[vmem] * 2,
        out_shape=[sds(layers, 2, width), sds(layers, 2, hid)],
        name="small_sums",
    )(*small_in)

    def flat_part(j):
        return jnp.concatenate(
            [gains.reshape(-1, 128), biases[:, :, j * part_h : (j + 1) * part_h].reshape(-1, 128)]
        )

    total = flat_part(0)
    for j in range(1, mp):
        total = total + lax.ppermute(flat_part(j), "mp", [(m, (m + j) % mp) for m in range(mp)])

    def other_half(value, bit):
        return lax.ppermute(value, "dp", [(i, i ^ (1 << bit)) for i in range(dp_count)])

    bits = dp_count.bit_length() - 1
    for at in range(stages - 1):
        pieces, total = combine(plan, held, at, (), (total, other_half(total, at)))
        held = scatter_stage(plan, pieces, at + 1)
    for bit in range(stages - 1, bits):
        total = total + other_half(total, bit)
    total = total.reshape(-1)
    gain_grad = total[: gains.size].reshape(gains.shape)
    bias_grad = total[gains.size :].reshape(layers, 2, part_h)
    done = finish(0, held, done)
    input_grad = input_grad.reshape(1, tokens, width)
    state, (mlp_new, hidden_new), _ = done
    mlp_grad, mlp_first_new, mlp_second_new = state[:3]
    hidden_grad, hidden_first_new, gate_second_new, hidden_second_new = state[3:]
    gain_first_new, gain_second_new, gain_moves = adam_moments(
        gain_grad, gain_first, gain_second, fix_one, fix_two
    )
    bias_first_new, bias_second_new, bias_moves = adam_moments(
        bias_grad, bias_first, bias_second, fix_one, fix_two
    )
    gain_new = norm_gains - GAIN_RATE * gain_moves
    bias_new = gate_bias - BIAS_RATE * bias_moves
    return (
        output,
        input_grad,
        hidden_grad,
        hidden_first_new,
        hidden_second_new,
        gate_second_new,
        hidden_new,
        mlp_grad,
        mlp_first_new,
        mlp_second_new,
        mlp_new,
        gain_grad,
        gain_first_new,
        gain_second_new,
        gain_new,
        bias_grad,
        bias_first_new,
        bias_second_new,
        bias_new,
    )


def solution(mesh):
    in_specs = (
        P("dp", "mp", None),
        P("dp", "mp", None),
        P("dp"),
        P(None, None, None, "mp"),
        P(None, None, None, "mp"),
        P(),
        P(None, None, "mp"),
        P(),
        P(None, None, "mp", None, None),
        P(None, None, "mp", None, None),
        P("dp", None, None, "mp"),
        P("dp", None, None, "mp"),
        P("dp", None, None, "mp"),
        P("dp", None, None, "mp"),
        P(),
        P(),
        P(None, None, "mp"),
        P(None, None, "mp"),
        P(),
        P(),
    )
    out_specs = (
        P("dp", "mp", None),
        P("dp", "mp", None),
        P("dp", None, None, "mp"),
        P("dp", None, None, "mp"),
        P("dp", None, None, "mp"),
        P("dp", None, None, "mp"),
        P(None, None, None, "mp"),
        P("dp", None, None, "mp"),
        P("dp", None, None, "mp"),
        P("dp", None, None, "mp"),
        P(None, None, None, "mp"),
        P(),
        P(),
        P(),
        P(),
        P(None, None, "mp"),
        P(None, None, "mp"),
        P(None, None, "mp"),
        P(None, None, "mp"),
    )
    return jax.shard_map(
        per_device, mesh=mesh, in_specs=in_specs, out_specs=out_specs, check_vma=False
    )
```
